32 devices in a mesh: parts: 1, ep: 16 (over z, y, x), fan: 2 (over core).
Axes of the slice: x: 2, y: 2, z: 4, core: 2. Of those that a mesh axis runs over, the one named last changes fastest.
Arguments:
- queries: bfloat16 [1024, 2, 8192], P(('parts', 'ep', 'fan')), may hold values from -300 to 300
- new_kv: bfloat16 [1024, 2, 1024], P(('parts', 'ep', 'fan')), may hold values from -6 to 6
- prompt_kv: bfloat16 [64, 1024, 1024], P(('parts', 'ep', 'fan')), may hold values from -6 to 6
- prompt_lens: int32 [64], P(('parts', 'ep')), may hold values from 1 to 1024, 40960 in all
- sample_prompt: int32 [1024], P(('parts', 'ep', 'fan')), may hold values from 0 to 3, as said below
- hidden: bfloat16 [1024, 4096], P(('parts', 'ep', 'fan')), may hold values from -6 to 6
- norm_gain: bfloat16 [4096], replicated, may hold values from 0.099609375 to 1.8984375
- route_ids: int32 [1024, 8], P(('parts', 'ep', 'fan')), may hold values from 0 to 15, all different within a row; in each aligned block of 32 rows (0 to 31, 32 to 63, ...) at most 32 rows name the same one
- route_logits: float32 [1024, 8], P(('parts', 'ep', 'fan')), may hold values from -8 to 8
- w_gate: bfloat16 [16, 4096, 1536], P('ep', None, 'fan'), may hold values from -0.09375 to 0.09375
- w_up: bfloat16 [16, 4096, 1536], P('ep', None, 'fan'), may hold values from -0.09375 to 0.09375
- w_down: bfloat16 [16, 1536, 4096], P('ep', 'fan'), may hold values from -0.15625 to 0.15625
Outputs:
- context: bfloat16 [1024, 2, 8192], P(('parts', 'ep', 'fan'))
- expert_out: bfloat16 [1024, 4096], P(('parts', 'ep', 'fan'))
The draws below stay inside these ranges and needn't reach their ends.
Inputs may be any that keep to these rules, and one draw needn't show every extreme that they name: `sample_prompt`: each sample names one of the 4 prompts held by the devices of its chip, numbered by device then position; each of them has exactly 16 samples on that chip. `prompt_lens`: some prompt has exactly 1024. `route_ids`: each token names 8 different experts; among the tokens of one device no expert is named more than 32 times.
All inputs are finite; a program needn't handle non-finite values. No bound on the sum of `prompt_lens` on one device may be relied on, other than what follows from the above.
Results may differ from the reference program's by a relative error of at most 0.0071.
Values may be sent and summed in bfloat16 or wider, within the bound.
No kernel may reach another device: no remote copies, remote signals or barrier semaphores. Data moves between devices by JAX's collectives and lax.ppermute only.
A program may use at most 256 MiB of HBM per device.

```python
import math
import jax
import jax.numpy as jnp
import numpy as np
from jax import lax

D = 4096
HEADS = 64
KVH = 4
HD = 128
FF = 1536
TOP = 8
SAMP = 16
STEPS = 2
PR_DEV = 2
LEN = 1024
ROWS = 32
CAP = 32
CHIP_ROWS = 64
EXPERTS = 16
PROMPTS = 64
SAMPLES = 1024
N_FAN = 2


def draw_queries(key, part):
    key = jax.random.fold_in(key, 11)
    normal_key = jax.random.fold_in(key, 0)
    values = jax.random.normal(normal_key, (SAMPLES, STEPS, HEADS * HD), jnp.float32)
    values = jnp.clip(values * 2.5, -15.0, 15.0)
    return values.astype(jnp.bfloat16)


def draw_sample_prompt(key, part):
    key = jax.random.fold_in(key, 23)
    chip_keys = jax.random.split(key, SAMPLES // CHIP_ROWS)
    orders = jax.vmap(lambda single: jax.random.permutation(single, CHIP_ROWS))(chip_keys)
    return (orders // SAMP).reshape(SAMPLES).astype(jnp.int32)


def block_levels(rng, shape, pieces, least, largest):
    factor_of, own = 1.0, jax.random.fold_in(rng, 6)
    for axis_at, parts in pieces:
        heights = jnp.exp(jax.random.uniform(jax.random.fold_in(own, axis_at), (parts,), jnp.float32, least / len(pieces), largest / len(pieces)))
        factor_of = factor_of * jnp.repeat(heights, shape[axis_at] // parts).reshape([-1 if axis == axis_at else 1 for axis in range(len(shape))])
    return factor_of


def split_up(amount, total, bound, slope):
    portions = [(1 << 20) // math.isqrt(rank ** slope) + 1 for rank in range(2, amount + 1)]
    rest, holding = total - bound - (amount - 1), [1] * (amount - 1)
    while rest > 0:
        free = [i for i in range(amount - 1) if holding[i] < bound]
        mass, left = sum([portions[i] for i in free]), rest
        for i in free:
            extra = min(bound - holding[i], max(1, left * portions[i] // mass), rest)
            holding[i] = holding[i] + extra
            rest = rest - extra
    return np.array([bound] + holding)


def uneven_parts(stream_key, amount, total, reach, lean):
    if amount == 2:
        one = jax.random.randint(stream_key, (), max(1, total - reach), min(reach, total - 1) + 1)
        return jnp.stack([one, total - one])
    tallies = jnp.asarray(split_up(amount, total, reach, lean), jnp.int32)
    couples = (amount - 1) // 2
    giver, taker = tallies[1:1 + 2 * couples:2], tallies[2:2 + 2 * couples:2]
    room = jnp.minimum(giver - 1, reach - taker)
    moved = jax.random.randint(jax.random.fold_in(stream_key, 1), (couples,), 0, 1 << 20) % (room + 1)
    tallies = tallies.at[1:1 + 2 * couples:2].set(giver - moved).at[2:2 + 2 * couples:2].set(taker + moved)
    return tallies[jax.random.permutation(jax.random.fold_in(stream_key, 2), amount)]


def assign_block(own_key, own, number, rows, number_of, top, most, slope):
    order = jax.random.permutation(own_key, number_of)
    crowded, common = shares(number_of, rows * top, most, slope, True), shares(number_of, rows * top, most, slope, False)
    places = jnp.arange(number_of)

    def named(sizes, rotation):
        used = int((sizes > 0).sum())
        fixed = max(1, used // 4)
        shifted = fixed + (places - fixed + rotation * (used - fixed)) % max(1, number_of - fixed)
        return jnp.zeros((number_of,), jnp.int32).at[order[jnp.where(places < fixed, places, shifted)]].set(jnp.asarray(sizes, jnp.int32))

    sizes = jnp.where(number % 4 == 0, named(crowded, number // 4), named(common, number - number // 4 - 1))
    mixed = jax.random.permutation(jax.random.fold_in(own, 3), number_of)
    donor, receiver = mixed[0:number_of // 2 * 2:2], mixed[1:number_of // 2 * 2:2]
    margin = jnp.minimum(sizes[donor] - 1, most - sizes[receiver]) // 2
    margin = jnp.where((donor == order[0]) | (receiver == order[0]) | (sizes[receiver] == 0), 0, jnp.maximum(margin, 0))
    shifted = jax.random.randint(jax.random.fold_in(own, 4), (number_of // 2,), 0, 1 << 20) % (margin + 1)
    sizes = sizes.at[donor].add(-shifted).at[receiver].add(shifted)
    items = jnp.searchsorted(jnp.cumsum(sizes), jnp.arange(rows * top), side="right").astype(jnp.int32)
    grid = items.reshape(top, rows).T
    grid = grid[jax.random.permutation(jax.random.fold_in(own, 1), rows)]
    rotation = jax.random.randint(jax.random.fold_in(own, 2), (rows, 1), 0, top)
    return jnp.take_along_axis(grid, (jnp.arange(top)[None, :] + rotation) % top, axis=1)


def shares(number_of, total, reach, slope, full):
    loads = [(1 << 20) // math.isqrt(grade ** slope) + 1 for grade in range(1, number_of + 1)]
    largest = reach if full else min(reach, max(-(-total // number_of), total * loads[0] // sum(loads)))
    least = 1 if total - largest >= number_of - 1 else 0
    holding, spare = [largest] + [least] * (number_of - 1), total - largest - least * (number_of - 1)
    while spare > 0:
        candidates = [i for i in range(1, number_of) if holding[i] < largest] or [i for i in range(1, number_of) if holding[i] < reach]
        pool, budget = sum([loads[i] for i in candidates]), spare
        for i in candidates:
            extra = min(reach - holding[i], max(1, budget * loads[i] // pool), spare)
            holding[i] = holding[i] + extra
            spare = spare - extra
    return np.array(holding)


def centred(key, dims, deviation, bound, cuts=(), kind=jnp.bfloat16):
    factor_of = block_levels(key, dims, cuts, -0.22, 0.18) if cuts else 1.0
    entries = jax.random.normal(key, dims, jnp.float32) * deviation * factor_of
    return jnp.minimum(jnp.maximum(entries, -bound), bound).astype(kind)


def setup_inputs(seed: int = 0, part: int = 0) -> dict:
    splits = jax.random.split(jax.random.key(seed), 13)
    part_keys = jax.random.split(jax.random.fold_in(splits[12], part), 13)
    queries = draw_queries(jax.random.fold_in(jax.random.fold_in(splits[12], part), 71), part)
    new_kv = centred(part_keys[1], (SAMPLES, STEPS, 2 * KVH * HD), 1.0, 6.0, ((0, 32),))
    prompt_kv = centred(part_keys[2], (PROMPTS, LEN, 2 * KVH * HD), 1.0, 6.0, ((0, 32),))
    prompt_lens = uneven_parts(part_keys[3], PROMPTS, PROMPTS * LEN * 5 // 8, LEN, 1).astype(jnp.int32)
    sample_prompt = draw_sample_prompt(jax.random.fold_in(jax.random.fold_in(splits[12], part), 71), part)
    hidden = centred(part_keys[5], (SAMPLES, D), 1.0, 6.0, ((0, 32),))
    norm_gain = jnp.clip(1.0 + 0.18 * jax.random.normal(splits[6], (D,), jnp.float32), 0.099609375, 1.8984375).astype(jnp.bfloat16)
    route_ids_keys = jax.random.split(jax.random.fold_in(part_keys[7], 1), SAMPLES // ROWS)
    route_ids_turns = jax.random.permutation(jax.random.fold_in(part_keys[7], 3), SAMPLES // ROWS)
    route_ids = jax.vmap(lambda own, number: assign_block(jax.random.fold_in(part_keys[7], 2), own, number, ROWS, EXPERTS, TOP, CAP, 2))(route_ids_keys, route_ids_turns).reshape((SAMPLES, TOP))
    route_logits = centred(part_keys[8], (SAMPLES, TOP), 1.5, 8.0, ((0, 32),), jnp.float32)
    w_gate = centred(splits[9], (EXPERTS, D, FF), D ** -0.5, 0.09375, ((0, 16), (2, 2)))
    w_up = centred(splits[10], (EXPERTS, D, FF), D ** -0.5, 0.09375, ((0, 16), (2, 2)))
    w_down = centred(splits[11], (EXPERTS, FF, D), FF ** -0.5, 0.15625, ((0, 16), (1, 2)))
    return dict(queries=queries, new_kv=new_kv, prompt_kv=prompt_kv, prompt_lens=prompt_lens, sample_prompt=sample_prompt, hidden=hidden, norm_gain=norm_gain, route_ids=route_ids, route_logits=route_logits, w_gate=w_gate, w_up=w_up, w_down=w_down)


def attend_row(query, own_rows, cache, length):
    width = KVH * HD
    groups = HEADS // KVH
    key_rows = cache[:, :width].reshape(-1, KVH, HD).astype(jnp.float32)
    value_rows = cache[:, width:].reshape(-1, KVH, HD).astype(jnp.float32)
    own_keys = own_rows[:, :width].reshape(STEPS, KVH, HD).astype(jnp.float32)
    own_values = own_rows[:, width:].reshape(STEPS, KVH, HD).astype(jnp.float32)
    query_heads = query.reshape(STEPS, KVH, groups, HD).astype(jnp.float32)
    scaling = HD ** (-0.5)
    cache_scores = jnp.einsum('skgd,lkd->kgsl', query_heads, key_rows, precision=lax.Precision.HIGHEST) * scaling
    own_scores = jnp.einsum('skgd,jkd->kgsj', query_heads, own_keys, precision=lax.Precision.HIGHEST) * scaling
    valid = jnp.arange(cache.shape[0], dtype=jnp.int32) < length
    cache_scores = jnp.where(valid, cache_scores, -1e+30)
    causal = jnp.arange(STEPS)[None, :] <= jnp.arange(STEPS)[:, None]
    own_scores = jnp.where(causal, own_scores, -1e+30)
    highest = jnp.maximum(lax.optimization_barrier(jnp.max(cache_scores, axis=-1)), lax.optimization_barrier(jnp.max(own_scores, axis=-1)))
    cache_exp = jnp.exp(cache_scores - highest[..., None])
    own_exp = jnp.exp(own_scores - highest[..., None])
    denominator = lax.optimization_barrier(jnp.sum(cache_exp, axis=-1)) + lax.optimization_barrier(jnp.sum(own_exp, axis=-1))
    cache_weights = (cache_exp / denominator[..., None]).astype(jnp.bfloat16).astype(jnp.float32)
    own_weights = (own_exp / denominator[..., None]).astype(jnp.bfloat16).astype(jnp.float32)
    mixed = jnp.einsum('kgsl,lkd->skgd', cache_weights, value_rows, precision=lax.Precision.HIGHEST)
    mixed = mixed + jnp.einsum('kgsj,jkd->skgd', own_weights, own_values, precision=lax.Precision.HIGHEST)
    return mixed.reshape(STEPS, HEADS * HD).astype(jnp.bfloat16)

def reference(queries, new_kv, prompt_kv, prompt_lens, sample_prompt, hidden, norm_gain, route_ids, route_logits, w_gate, w_up, w_down):
    chip_prompts = N_FAN * PR_DEV
    chip_number = jnp.arange(SAMPLES, dtype=jnp.int32) // CHIP_ROWS
    owner_prompt = (chip_number * chip_prompts + sample_prompt).astype(jnp.int32)

    def one_sample(packed):
        query, own_rows, prompt_number = packed
        cache = lax.dynamic_index_in_dim(prompt_kv, prompt_number, 0, keepdims=False)
        length = lax.dynamic_index_in_dim(prompt_lens, prompt_number, 0, keepdims=False)
        return attend_row(query, own_rows, cache, length)
    context = lax.map(one_sample, (queries, new_kv, owner_prompt))
    hidden32 = hidden.astype(jnp.float32)
    meansq = lax.optimization_barrier(jnp.mean(hidden32 * hidden32, axis=-1, keepdims=True))
    normed = (hidden32 * lax.rsqrt(meansq + 1e-06) * norm_gain.astype(jnp.float32)).astype(jnp.bfloat16)
    normed32 = normed.astype(jnp.float32)
    route_weights = jax.nn.softmax(route_logits, axis=-1)
    span = FF // N_FAN

    def expert_step(running, packed):
        gate_w, up_w, down_w, number = packed
        column = lax.optimization_barrier(jnp.sum(jnp.where(route_ids == number, route_weights, 0.0), axis=1))
        summed = jnp.zeros((SAMPLES, D), jnp.float32)
        for portion in range(N_FAN):
            offset = portion * span
            gate_out = jnp.dot(normed32, gate_w[:, offset:offset + span].astype(jnp.float32), precision=lax.Precision.HIGHEST)
            up_out = jnp.dot(normed32, up_w[:, offset:offset + span].astype(jnp.float32), precision=lax.Precision.HIGHEST)
            units = (jax.nn.silu(gate_out) * up_out).astype(jnp.bfloat16)
            partial_out = jnp.dot(units.astype(jnp.float32), down_w[offset:offset + span].astype(jnp.float32), precision=lax.Precision.HIGHEST).astype(jnp.bfloat16)
            summed = summed + partial_out.astype(jnp.float32)
        return (running + column[:, None] * summed, None)
    start = jnp.zeros((SAMPLES, D), jnp.float32)
    numbers = jnp.arange(EXPERTS, dtype=jnp.int32)
    combined, unused = lax.scan(expert_step, start, (w_gate, w_up, w_down, numbers))
    return (context, combined.astype(jnp.bfloat16))
```

```python
import jax
import jax.numpy as jnp
from jax import lax
from jax.sharding import PartitionSpec as P

HEADS = 64
KVH = 4
HD = 128
STEPS = 2


def attend_block(query_block, own_block, cache, length, matches):
    width = KVH * HD
    groups = HEADS // KVH
    count = query_block.shape[0]
    key_rows = cache[:, :width].reshape(-1, KVH, HD)
    value_rows = cache[:, width:].reshape(-1, KVH, HD)
    own_keys = own_block[:, :, :width].reshape(count, STEPS, KVH, HD)
    own_values = own_block[:, :, width:].reshape(count, STEPS, KVH, HD)
    query_heads = query_block.reshape(count, STEPS, KVH, groups, HD)
    scaling = HD ** (-0.5)
    cache_scores = (
        jnp.einsum("rskgd,lkd->rkgsl", query_heads, key_rows, preferred_element_type=jnp.float32)
        * scaling
    )
    own_scores = (
        jnp.einsum("rskgd,rjkd->rkgsj", query_heads, own_keys, preferred_element_type=jnp.float32)
        * scaling
    )
    valid = jnp.arange(cache.shape[0], dtype=jnp.int32) < length
    usable = matches[:, None, None, None, None] & valid[None, None, None, None, :]
    cache_scores = jnp.where(usable, cache_scores, -1e30)
    causal = jnp.arange(STEPS)[None, :] <= jnp.arange(STEPS)[:, None]
    own_scores = jnp.where(causal, own_scores, -1e30)
    highest = jnp.maximum(jnp.max(cache_scores, axis=-1), jnp.max(own_scores, axis=-1))
    cache_exp = jnp.exp(cache_scores - highest[..., None])
    own_exp = jnp.exp(own_scores - highest[..., None])
    denominator = jnp.sum(cache_exp, axis=-1) + jnp.sum(own_exp, axis=-1)
    cache_weights = (cache_exp / denominator[..., None]).astype(jnp.bfloat16)
    own_weights = (own_exp / denominator[..., None]).astype(jnp.bfloat16)
    mixed = jnp.einsum(
        "rkgsl,lkd->rskgd", cache_weights, value_rows, preferred_element_type=jnp.float32
    )
    mixed = mixed + jnp.einsum(
        "rkgsj,rjkd->rskgd", own_weights, own_values, preferred_element_type=jnp.float32
    )
    return mixed.reshape(count, STEPS, HEADS * HD).astype(jnp.bfloat16)


def attend_all(query_block, own_block, prompt_index, caches, lengths):
    result = jnp.zeros(query_block.shape, jnp.bfloat16)
    for number in range(caches.shape[0]):
        matches = prompt_index == number
        part_out = attend_block(query_block, own_block, caches[number], lengths[number], matches)
        result = jnp.where(matches[:, None, None], part_out, result)
    return result


def on_device(
    queries,
    new_kv,
    prompt_kv,
    prompt_lens,
    sample_prompt,
    hidden,
    norm_gain,
    route_ids,
    route_logits,
    w_gate,
    w_up,
    w_down,
):
    all_caches = lax.all_gather(prompt_kv, "fan", axis=0, tiled=True)
    context = attend_all(queries, new_kv, sample_prompt, all_caches, prompt_lens)
    experts = lax.axis_size("ep")
    hidden32 = hidden.astype(jnp.float32)
    meansq = jnp.mean(hidden32 * hidden32, axis=-1, keepdims=True)
    normed = (hidden32 * lax.rsqrt(meansq + 1e-06) * norm_gain.astype(jnp.float32)).astype(
        jnp.bfloat16
    )
    route_weights = jax.nn.softmax(route_logits, axis=-1)
    matched = route_ids[:, :, None] == jnp.arange(experts, dtype=jnp.int32)
    combine = jnp.sum(jnp.where(matched, route_weights[:, :, None], 0.0), axis=1)
    tokens = lax.all_gather(normed, ("ep", "fan"), axis=0, tiled=True)
    all_combine = lax.all_gather(combine, ("ep", "fan"), axis=0, tiled=True)
    column = lax.dynamic_slice_in_dim(all_combine, lax.axis_index("ep"), 1, axis=1)
    gate_out = jnp.dot(tokens, w_gate[0], preferred_element_type=jnp.float32)
    up_out = jnp.dot(tokens, w_up[0], preferred_element_type=jnp.float32)
    units = (jax.nn.silu(gate_out) * up_out).astype(jnp.bfloat16)
    partial_out = jnp.dot(units, w_down[0], preferred_element_type=jnp.float32)
    weighted = (partial_out * column).astype(jnp.bfloat16)
    expert_out = lax.psum_scatter(weighted, ("ep", "fan"), scatter_dimension=0, tiled=True)
    return (context, expert_out.astype(jnp.bfloat16))


def solution(mesh):
    placed = (
        P(("parts", "ep", "fan"), None, None),
        P(("parts", "ep", "fan"), None, None),
        P(("parts", "ep", "fan"), None, None),
        P(("parts", "ep")),
        P(("parts", "ep", "fan")),
        P(("parts", "ep", "fan"), None),
        P(),
        P(("parts", "ep", "fan"), None),
        P(("parts", "ep", "fan"), None),
        P("ep", None, "fan"),
        P("ep", None, "fan"),
        P("ep", "fan", None),
    )
    return jax.shard_map(
        on_device,
        mesh=mesh,
        in_specs=placed,
        out_specs=(P(("parts", "ep", "fan"), None, None), P(("parts", "ep", "fan"), None)),
        check_vma=False,
    )
```

```python
import functools

import jax
import jax.numpy as jnp
from jax import lax
from jax.experimental import pallas as pl
from jax.experimental.pallas import tpu as pltpu
from jax.sharding import PartitionSpec as P

KVH = 4
HD = 128
STEPS = 2
SAMP = 16
TOP = 8
GROUP = SAMP * STEPS
LANES = 128
LOG2E = 1.4426950408889634
MIB = 1 << 20


def dot(a, b, contract=((1,), (0,))):
    return lax.dot_general(a, b, (contract, ((), ())), preferred_element_type=jnp.float32)


def cost(flops, moved):
    return pl.CostEstimate(flops=int(flops), bytes_accessed=int(moved), transcendentals=0)


def norm_kernel(hidden_ref, gain_ref, ids_ref, logits_ref, out_ref):
    rows, width = hidden_ref.shape
    hidden = hidden_ref[...].astype(jnp.float32)
    meansq = jnp.mean(hidden * hidden, axis=-1, keepdims=True)
    gain = gain_ref[...].astype(jnp.float32)
    out_ref[:, :width] = (hidden * lax.rsqrt(meansq + 1e-06) * gain).astype(jnp.bfloat16)
    logits = logits_ref[...]
    raised = jnp.exp(logits - jnp.max(logits, axis=0, keepdims=True))
    weights = raised / jnp.sum(raised, axis=0, keepdims=True)
    ids = ids_ref[...]
    number = lax.broadcasted_iota(jnp.int32, (LANES, rows), 0)
    total = jnp.zeros((LANES, rows), jnp.float32)
    for choice in range(TOP):
        picked = (number % 16) == ids[choice : choice + 1, :]
        total = total + jnp.where(picked, weights[choice : choice + 1, :], 0.0)
    high = total.astype(jnp.bfloat16).astype(jnp.float32)
    middle = (total - high).astype(jnp.bfloat16).astype(jnp.float32)
    low = total - high - middle
    piece = number // 16
    parts = jnp.where(
        piece == 0, high, jnp.where(piece == 1, middle, jnp.where(piece == 2, low, 0.0))
    ).astype(jnp.bfloat16)
    first = lax.broadcasted_iota(jnp.int32, (LANES, LANES), 0)
    second = lax.broadcasted_iota(jnp.int32, (LANES, LANES), 1)
    identity = jnp.where(first == second, 1.0, 0.0).astype(jnp.bfloat16)
    out_ref[:, width:] = dot(parts, identity, ((0,), (0,))).astype(jnp.bfloat16)


def norm_message(hidden, gain, ids, logits):
    rows, width = hidden.shape
    return pl.pallas_call(
        norm_kernel,
        out_shape=jax.ShapeDtypeStruct((rows, width + LANES), jnp.bfloat16),
        cost_estimate=cost(1e6, rows * width * 4),
        name="norm_message",
    )(hidden, gain.reshape(1, width), ids.T, logits.T)


def rank_rows(match, rows):
    first = lax.broadcasted_iota(jnp.int32, (rows, rows), 0)
    second = lax.broadcasted_iota(jnp.int32, (rows, rows), 1)
    below = jnp.where(second < first, 1.0, 0.0).astype(jnp.bfloat16)
    return dot(below, match)


def attend_kernel(
    local, lens_ref, q_mine, q_other, k_mine, k_other, v_mine, v_other, n_mine, n_other,
    key_ref, value_ref, out_ref
):
    number = lax.axis_index("fan") * 2 + local
    length = lens_ref[number]
    prompts = jnp.concatenate([n_mine[...], n_other[...]], axis=0).astype(jnp.float32)
    chosen = prompts == number.astype(jnp.float32)
    match = jnp.where(chosen, 1.0, 0.0).astype(jnp.bfloat16)
    rank = rank_rows(match, LANES)
    lane = lax.broadcasted_iota(jnp.int32, (LANES, LANES), 1)
    select = jnp.where(chosen & (rank == lane.astype(jnp.float32)), 1.0, 0.0).astype(jnp.bfloat16)

    def pick(mine, other):
        both = jnp.concatenate([mine[...], other[...]], axis=0)
        return dot(select, both, ((0,), (0,))).astype(jnp.bfloat16)

    queries = pick(q_mine, q_other)[:GROUP]
    own_keys = pick(k_mine, k_other)
    own_values = pick(v_mine, v_other)
    keys, values = key_ref[0], value_ref[0]
    span = keys.shape[0]
    factor = HD**-0.5 * LOG2E
    usable = lax.broadcasted_iota(jnp.int32, (1, span), 1) < length
    row = lax.broadcasted_iota(jnp.int32, (LANES, LANES), 0) % GROUP
    causal = (row // STEPS == lane // STEPS) & (lane <= row)
    heads = queries.shape[1] // HD
    together = LANES // GROUP
    for base in range(0, heads, together):
        block = jnp.concatenate(
            [queries[:, (base + i) * HD : (base + i + 1) * HD] for i in range(together)], axis=0
        )
        scores = jnp.where(usable, dot(block, keys, ((1,), (1,))), -1e30)
        own = jnp.where(causal, dot(block, own_keys, ((1,), (1,))), -1e30)
        highest = jnp.maximum(
            jnp.max(scores, axis=-1, keepdims=True), jnp.max(own, axis=-1, keepdims=True)
        )
        raised = jnp.exp2((scores - highest) * factor)
        own_raised = jnp.exp2((own - highest) * factor)
        total = jnp.sum(raised, axis=-1, keepdims=True) + jnp.sum(
            own_raised, axis=-1, keepdims=True
        )
        mixed = dot(raised.astype(jnp.bfloat16), values)
        mixed = mixed + dot(own_raised.astype(jnp.bfloat16), own_values)
        mixed = (mixed / total).astype(jnp.bfloat16)
        for i in range(together):
            out_ref[:, (base + i) * HD : (base + i + 1) * HD] = mixed[i * GROUP : (i + 1) * GROUP]


def attend(local, lens, mine, other, cache):
    rows = mine.shape[0]
    span = cache.shape[1]
    q_width = mine.shape[1] - 2 * KVH * HD - LANES
    head = q_width // KVH
    first = q_width // HD

    def column(at):
        return pl.BlockSpec((rows, HD), at)

    q_spec = pl.BlockSpec((rows, head), lambda k: (0, k))
    k_spec = column(lambda k: (0, first + k))
    v_spec = column(lambda k: (0, first + KVH + k))
    n_spec = column(lambda k: (0, first + 2 * KVH))
    return pl.pallas_call(
        functools.partial(attend_kernel, local),
        grid=(KVH,),
        out_shape=jax.ShapeDtypeStruct((GROUP, q_width), jnp.bfloat16),
        in_specs=[pl.BlockSpec(memory_space=pltpu.SMEM)]
        + [q_spec, q_spec, k_spec, k_spec, v_spec, v_spec, n_spec, n_spec]
        + [
            pl.BlockSpec((1, span, HD), lambda k: (local, 0, k)),
            pl.BlockSpec((1, span, HD), lambda k: (local, 0, KVH + k)),
        ],
        out_specs=pl.BlockSpec((GROUP, head), lambda k: (0, k)),
        compiler_params=pltpu.CompilerParams(vmem_limit_bytes=32 * MIB),
        cost_estimate=cost(5e9, 5 * MIB),
        name="attend",
    )(lens, mine, other, mine, other, mine, other, mine, other, cache, cache)


def place_kernel(n_mine, mine_0, mine_1, other_0, other_1, out_ref):
    rows = out_ref.shape[0]
    fan = lax.axis_index("fan")
    prompts = n_mine[...].astype(jnp.float32)
    lane = lax.broadcasted_iota(jnp.int32, (rows, LANES), 1).astype(jnp.float32)
    every = jnp.ones((rows, rows), jnp.bfloat16)
    place = jnp.zeros((rows, LANES), jnp.float32)
    for side in range(2):
        for local in range(2):
            number = (fan if side == 0 else 1 - fan) * 2 + local
            chosen = prompts == number.astype(jnp.float32)
            match = jnp.where(chosen, 1.0, 0.0).astype(jnp.bfloat16)
            rank = rank_rows(match, rows)
            if side == 1:
                rank = rank + (GROUP - dot(every, match))
            here = chosen & (rank + (side * 2 + local) * GROUP == lane)
            place = jnp.where(here, 1.0, place)
    stacked = jnp.concatenate([mine_0[...], mine_1[...], other_0[...], other_1[...]], axis=0)
    out_ref[...] = dot(place.astype(jnp.bfloat16), stacked).astype(jnp.bfloat16)


def place_context(message, mine, other):
    rows = message.shape[0]
    q_width = mine[0].shape[1]
    width = q_width // 4
    marks = message.shape[1] // LANES - 1
    block = pl.BlockSpec((GROUP, width), lambda k: (0, k))
    return pl.pallas_call(
        place_kernel,
        grid=(q_width // width,),
        out_shape=jax.ShapeDtypeStruct((rows, q_width), jnp.bfloat16),
        in_specs=[pl.BlockSpec((rows, LANES), lambda k: (0, marks)), block, block, block, block],
        out_specs=pl.BlockSpec((rows, width), lambda k: (0, k)),
        cost_estimate=cost(1e8, 3 * MIB),
        name="place_context",
    )(message, *mine, *other)


def expert_kernel(pieces, *refs):
    xs, (gate, up, down) = refs[:pieces], refs[pieces : pieces + 3]
    keep, send, other = refs[pieces + 3 : pieces + 6]
    x, w_gate, w_up, w_down, units, x_sem, g_sem, u_sem, d_sem = refs[pieces + 6 :]
    width, hidden = gate.shape
    piece_rows = xs[0].shape[0]
    step = 256
    deep = 1024
    copies = []
    for i in range(pieces):
        copies.append(
            pltpu.make_async_copy(
                xs[i], x.at[pl.ds(i * piece_rows, piece_rows)], x_sem.at[i]
            )
        )
    gates, ups, downs = [], [], []
    for i in range(hidden // step):
        at = pl.ds(i * step, step)
        gates.append(pltpu.make_async_copy(gate.at[:, at], w_gate.at[:, at], g_sem.at[i]))
        ups.append(pltpu.make_async_copy(up.at[:, at], w_up.at[:, at], u_sem.at[i]))
    for i in range(width // deep):
        at = pl.ds(i * deep, deep)
        downs.append(pltpu.make_async_copy(down.at[:, at], w_down.at[:, at], d_sem.at[i]))
    for copy in copies:
        copy.start()
    for i in range(hidden // step):
        gates[i].start()
        ups[i].start()
    for copy in downs:
        copy.start()
    for copy in copies:
        copy.wait()
    for i in range(hidden // step):
        at = slice(i * step, (i + 1) * step)
        gates[i].wait()
        opened = dot(x[:, :width], w_gate[:, at])
        ups[i].wait()
        raised = dot(x[:, :width], w_up[:, at])
        units[:, at] = (opened * jax.nn.sigmoid(opened) * raised).astype(jnp.bfloat16)
    marks = x[:, width:].astype(jnp.float32)
    lane = lax.broadcasted_iota(jnp.int32, marks.shape, 1)
    mine = (lane % 16 == lax.axis_index("ep")) & (lane < 48)
    weight = jnp.sum(jnp.where(mine, marks, 0.0), axis=1, keepdims=True)
    half = pieces // 2 * piece_rows
    near = half // 2
    for i in range(width // deep):
        downs[i].wait()
        at = slice(i * deep, (i + 1) * deep)
        result = (dot(units[...], w_down[:, at]) * weight).astype(jnp.bfloat16)
        keep[:, at] = result[:near]
        send[:, at] = result[near:half]
        other[:, at] = result[half:]


def expert_chunk(pieces, gate, up, down):
    count = len(pieces)
    piece_rows, message = pieces[0].shape
    width, hidden = gate.shape
    rows = count * piece_rows
    anywhere = pl.BlockSpec(memory_space=pl.ANY)
    whole = pl.BlockSpec(memory_space=pltpu.VMEM)
    return pl.pallas_call(
        functools.partial(expert_kernel, count),
        out_shape=(
            jax.ShapeDtypeStruct((rows // 4, width), jnp.bfloat16),
            jax.ShapeDtypeStruct((rows // 4, width), jnp.bfloat16),
            jax.ShapeDtypeStruct((rows // 2, width), jnp.bfloat16),
        ),
        in_specs=[anywhere] * (count + 3),
        out_specs=(whole, whole, whole),
        scratch_shapes=[
            pltpu.VMEM((rows, message), jnp.bfloat16),
            pltpu.VMEM((width, hidden), jnp.bfloat16),
            pltpu.VMEM((width, hidden), jnp.bfloat16),
            pltpu.VMEM((hidden, width), jnp.bfloat16),
            pltpu.VMEM((rows, hidden), jnp.bfloat16),
            pltpu.SemaphoreType.DMA((count,)),
            pltpu.SemaphoreType.DMA((hidden // 256,)),
            pltpu.SemaphoreType.DMA((hidden // 256,)),
            pltpu.SemaphoreType.DMA((width // 1024,)),
        ],
        compiler_params=pltpu.CompilerParams(vmem_limit_bytes=40 * MIB),
        cost_estimate=cost(6 * rows * width * hidden, 6 * width * hidden),
        name="expert_chunk",
    )(*pieces, gate, up, down)


def on_device(
    queries,
    new_kv,
    prompt_kv,
    prompt_lens,
    sample_prompt,
    hidden,
    norm_gain,
    route_ids,
    route_logits,
    w_gate,
    w_up,
    w_down,
):
    chips = lax.axis_size("ep")
    layers = chips // 4
    count, _, q_width = queries.shape
    rows = count * STEPS

    def swap(value, by_fan):
        pairs = [
            ((e * 2 + f), ((e ^ by_fan[f]) * 2 + f)) for e in range(chips) for f in range(2)
        ]
        return lax.ppermute(value, ("ep", "fan"), pairs)

    def near(value):
        return swap(value, (1, 2))

    def cross(value):
        return swap(value, (2, 1))

    def far(value, layer):
        return swap(value, (4 * layer, 4 * layer))

    def beside(value):
        return lax.ppermute(value, "fan", [(0, 1), (1, 0)])

    token = norm_message(hidden, norm_gain, route_ids, route_logits)
    arrived = [token] + [far(token, layer) for layer in range(1, layers)]

    marks = jnp.broadcast_to(sample_prompt.astype(jnp.bfloat16)[:, None, None], (count, STEPS, LANES))
    mine = jnp.concatenate([queries, new_kv, marks], axis=2).reshape(rows, -1)
    other = beside(mine)
    context_mine = [attend(local, prompt_lens, mine, other, prompt_kv) for local in range(2)]
    context_other = [beside(value) for value in context_mine]
    context = place_context(mine, context_mine, context_other).reshape(count, STEPS, q_width)

    parts = []
    for layer in range(layers):
        own = arrived[layer]
        first = near(own)
        pieces = [own, first, cross(own), cross(first)]
        pieces = pieces + [beside(piece) for piece in pieces]
        keep, send, away = expert_chunk(pieces, w_gate[0], w_up[0], w_down[0])
        back = beside(away).astype(jnp.float32)
        half = send.shape[0]
        single = half // 2
        there = (send.astype(jnp.float32) + back[half:]).astype(jnp.bfloat16)
        turned = cross(there).astype(jnp.float32)
        held = keep.astype(jnp.float32) + back[:half] + turned
        last = near(held[single:].astype(jnp.bfloat16)).astype(jnp.float32)
        reached = held[:single] + last
        if layer:
            reached = far(reached.astype(jnp.bfloat16), layer).astype(jnp.float32)
        parts.append(reached)
    expert_out = functools.reduce(jnp.add, parts).astype(jnp.bfloat16)
    return (context, expert_out)


def solution(mesh):
    placed = (
        P(("parts", "ep", "fan"), None, None),
        P(("parts", "ep", "fan"), None, None),
        P(("parts", "ep", "fan"), None, None),
        P(("parts", "ep")),
        P(("parts", "ep", "fan")),
        P(("parts", "ep", "fan"), None),
        P(),
        P(("parts", "ep", "fan"), None),
        P(("parts", "ep", "fan"), None),
        P("ep", None, "fan"),
        P("ep", None, "fan"),
        P("ep", "fan", None),
    )
    return jax.shard_map(
        on_device,
        mesh=mesh,
        in_specs=placed,
        out_specs=(P(("parts", "ep", "fan"), None, None), P(("parts", "ep", "fan"), None)),
        check_vma=False,
    )
```

```python
import functools

import jax
import jax.numpy as jnp
from jax import lax
from jax.experimental import pallas as pl
from jax.experimental.pallas import tpu as pltpu
from jax.sharding import PartitionSpec as P

KVH = 4
HD = 128
STEPS = 2
SAMP = 16
TOP = 8
GROUP = SAMP * STEPS
LANES = 128
BAND = 64
LOG2E = 1.4426950408889634
MIB = 1 << 20


def dot(a, b, contract=((1,), (0,))):
    return lax.dot_general(a, b, (contract, ((), ())), preferred_element_type=jnp.float32)


def cost(flops, moved):
    return pl.CostEstimate(flops=int(flops), bytes_accessed=int(moved), transcendentals=0)


def norm_kernel(hidden_ref, gain_ref, ids_ref, logits_ref, out_ref):
    rows, width = hidden_ref.shape
    hidden = hidden_ref[...].astype(jnp.float32)
    meansq = jnp.mean(hidden * hidden, axis=-1, keepdims=True)
    gain = gain_ref[...].astype(jnp.float32)
    out_ref[:, :width] = (hidden * lax.rsqrt(meansq + 1e-06) * gain).astype(jnp.bfloat16)
    logits = logits_ref[...]
    raised = jnp.exp(logits - jnp.max(logits, axis=0, keepdims=True))
    weights = raised / jnp.sum(raised, axis=0, keepdims=True)
    ids = ids_ref[...]
    number = lax.broadcasted_iota(jnp.int32, (LANES, rows), 0)
    total = jnp.zeros((LANES, rows), jnp.float32)
    for choice in range(TOP):
        picked = (number % 16) == ids[choice : choice + 1, :]
        total = total + jnp.where(picked, weights[choice : choice + 1, :], 0.0)
    high = total.astype(jnp.bfloat16).astype(jnp.float32)
    middle = (total - high).astype(jnp.bfloat16).astype(jnp.float32)
    low = total - high - middle
    piece = number // 16
    parts = jnp.where(
        piece == 0, high, jnp.where(piece == 1, middle, jnp.where(piece == 2, low, 0.0))
    ).astype(jnp.bfloat16)
    first = lax.broadcasted_iota(jnp.int32, (LANES, LANES), 0)
    second = lax.broadcasted_iota(jnp.int32, (LANES, LANES), 1)
    identity = jnp.where(first == second, 1.0, 0.0).astype(jnp.bfloat16)
    out_ref[:, width:] = dot(parts, identity, ((0,), (0,))).astype(jnp.bfloat16)


def norm_message(hidden, gain, ids, logits):
    rows, width = hidden.shape
    return pl.pallas_call(
        norm_kernel,
        out_shape=jax.ShapeDtypeStruct((rows, width + LANES), jnp.bfloat16),
        cost_estimate=cost(1e6, rows * width * 4),
        name="norm_message",
    )(hidden, gain.reshape(1, width), ids.T, logits.T)


def rank_rows(match, rows):
    first = lax.broadcasted_iota(jnp.int32, (rows, rows), 0)
    second = lax.broadcasted_iota(jnp.int32, (rows, rows), 1)
    below = jnp.where(second < first, 1.0, 0.0).astype(jnp.bfloat16)
    return dot(below, match)


def attend_kernel(
    local, lens_ref, q_mine, q_other, k_mine, k_other, v_mine, v_other, n_mine, n_other,
    key_ref, value_ref, *refs
):
    out_ref, q_ref, score_ref, weight_ref, total_ref = refs[-5:]
    number = lax.axis_index("fan") * 2 + local
    length = lens_ref[number]
    prompts = jnp.concatenate([n_mine[...], n_other[...]], axis=0).astype(jnp.float32)
    chosen = prompts == number.astype(jnp.float32)
    match = jnp.where(chosen, 1.0, 0.0).astype(jnp.bfloat16)
    rank = rank_rows(match, LANES)
    lane = lax.broadcasted_iota(jnp.int32, (LANES, LANES), 1)
    select = jnp.where(chosen & (rank == lane.astype(jnp.float32)), 1.0, 0.0).astype(jnp.bfloat16)

    def pick(mine, other):
        both = jnp.concatenate([mine[...], other[...]], axis=0)
        return dot(select, both, ((0,), (0,))).astype(jnp.bfloat16)

    queries = pick(q_mine, q_other)[:GROUP]
    span = key_ref.shape[1]
    factor = HD**-0.5 * LOG2E
    heads = queries.shape[1] // HD
    for head in range(heads):
        q_ref[head * GROUP : (head + 1) * GROUP] = queries[:, head * HD : (head + 1) * HD]
    score_ref[:, :span] = dot(q_ref[...], key_ref[0], ((1,), (1,)))
    score_ref[:, span:] = dot(q_ref[...], pick(k_mine, k_other), ((1,), (1,)))
    usable = lax.broadcasted_iota(jnp.int32, (1, span), 1) < length
    row = lax.broadcasted_iota(jnp.int32, (LANES, LANES), 0) % GROUP
    causal = (row // STEPS == lane // STEPS) & (lane <= row)
    for base in range(0, heads * GROUP, BAND):
        at = slice(base, base + BAND)
        scores = jnp.where(usable, score_ref[at, :span], -1e30)
        own = jnp.where(causal[:BAND], score_ref[at, span:], -1e30)
        highest = jnp.maximum(
            jnp.max(scores, axis=-1, keepdims=True), jnp.max(own, axis=-1, keepdims=True)
        )
        raised = jnp.exp2((scores - highest) * factor)
        own_raised = jnp.exp2((own - highest) * factor)
        total = jnp.sum(raised, axis=-1, keepdims=True) + jnp.sum(
            own_raised, axis=-1, keepdims=True
        )
        weight_ref[at, :span] = raised.astype(jnp.bfloat16)
        weight_ref[at, span:] = own_raised.astype(jnp.bfloat16)
        total_ref[at] = jnp.broadcast_to(1.0 / total, (BAND, HD))
    mixed = dot(weight_ref[:, :span], value_ref[0])
    mixed = mixed + dot(weight_ref[:, span:], pick(v_mine, v_other))
    mixed = (mixed * total_ref[...]).astype(jnp.bfloat16)
    for head in range(heads):
        out_ref[:, head * HD : (head + 1) * HD] = mixed[head * GROUP : (head + 1) * GROUP]


def attend(local, lens, queries, own, cache, after):
    rows, q_width = queries[0].shape
    span = cache.shape[1]
    head = q_width // KVH
    band = head // HD * GROUP

    def column(at):
        return pl.BlockSpec((rows, HD), at)

    q_spec = pl.BlockSpec((rows, head), lambda k: (0, k))
    k_spec = column(lambda k: (0, k))
    v_spec = column(lambda k: (0, KVH + k))
    n_spec = column(lambda k: (0, 2 * KVH))
    return pl.pallas_call(
        functools.partial(attend_kernel, local),
        grid=(KVH,),
        out_shape=jax.ShapeDtypeStruct((GROUP, q_width), jnp.bfloat16),
        in_specs=[pl.BlockSpec(memory_space=pltpu.SMEM)]
        + [q_spec, q_spec, k_spec, k_spec, v_spec, v_spec, n_spec, n_spec]
        + [
            pl.BlockSpec((1, span, HD), lambda k: (local, 0, k)),
            pl.BlockSpec((1, span, HD), lambda k: (local, 0, KVH + k)),
        ]
        + [pl.BlockSpec(memory_space=pl.ANY)] * len(after),
        out_specs=pl.BlockSpec((GROUP, head), lambda k: (0, k)),
        scratch_shapes=[
            pltpu.VMEM((band, HD), jnp.bfloat16),
            pltpu.VMEM((band, span + LANES), jnp.float32),
            pltpu.VMEM((band, span + LANES), jnp.bfloat16),
            pltpu.VMEM((band, HD), jnp.float32),
        ],
        compiler_params=pltpu.CompilerParams(vmem_limit_bytes=24 * MIB),
        cost_estimate=cost(5e9, 5 * MIB),
        name="attend",
    )(lens, *queries, *own, *own, *own, cache, cache, *after)


def place_kernel(n_mine, mine_0, mine_1, other_0, other_1, out_ref):
    rows = out_ref.shape[0]
    fan = lax.axis_index("fan")
    prompts = n_mine[...].astype(jnp.float32)
    lane = lax.broadcasted_iota(jnp.int32, (rows, LANES), 1).astype(jnp.float32)
    every = jnp.ones((rows, rows), jnp.bfloat16)
    place = jnp.zeros((rows, LANES), jnp.float32)
    for side in range(2):
        for local in range(2):
            number = (fan if side == 0 else 1 - fan) * 2 + local
            chosen = prompts == number.astype(jnp.float32)
            match = jnp.where(chosen, 1.0, 0.0).astype(jnp.bfloat16)
            rank = rank_rows(match, rows)
            if side == 1:
                rank = rank + (GROUP - dot(every, match))
            here = chosen & (rank + (side * 2 + local) * GROUP == lane)
            place = jnp.where(here, 1.0, place)
    stacked = jnp.concatenate([mine_0[...], mine_1[...], other_0[...], other_1[...]], axis=0)
    out_ref[...] = dot(place.astype(jnp.bfloat16), stacked).astype(jnp.bfloat16)


def place_context(message, mine, other):
    rows = message.shape[0]
    q_width = mine[0].shape[1]
    width = q_width // 4
    marks = message.shape[1] // LANES - 1
    block = pl.BlockSpec((GROUP, width), lambda k: (0, k))
    return pl.pallas_call(
        place_kernel,
        grid=(q_width // width,),
        out_shape=jax.ShapeDtypeStruct((rows, q_width), jnp.bfloat16),
        in_specs=[pl.BlockSpec((rows, LANES), lambda k: (0, marks)), block, block, block, block],
        out_specs=pl.BlockSpec((rows, width), lambda k: (0, k)),
        cost_estimate=cost(1e8, 3 * MIB),
        name="place_context",
    )(message, *mine, *other)


def expert_kernel(pieces, *refs):
    xs, (gate, up, down) = refs[:pieces], refs[pieces : pieces + 3]
    keep, send, other = refs[-12:-9]
    x, w_gate, w_up, w_down, units, x_sem, g_sem, u_sem, d_sem = refs[-9:]
    width, hidden = gate.shape
    piece_rows = xs[0].shape[0]
    step = 256
    deep = 1024
    copies = []
    for i in range(pieces):
        copies.append(
            pltpu.make_async_copy(
                xs[i], x.at[pl.ds(i * piece_rows, piece_rows)], x_sem.at[i]
            )
        )
    gates, ups, downs = [], [], []
    for i in range(hidden // step):
        at = pl.ds(i * step, step)
        gates.append(pltpu.make_async_copy(gate.at[:, at], w_gate.at[:, at], g_sem.at[i]))
        ups.append(pltpu.make_async_copy(up.at[:, at], w_up.at[:, at], u_sem.at[i]))
    for i in range(width // deep):
        at = pl.ds(i * deep, deep)
        downs.append(pltpu.make_async_copy(down.at[:, at], w_down.at[:, at], d_sem.at[i]))
    for copy in copies:
        copy.start()
    for i in range(hidden // step):
        gates[i].start()
        ups[i].start()
    for copy in downs:
        copy.start()
    for copy in copies:
        copy.wait()
    for i in range(hidden // step):
        at = slice(i * step, (i + 1) * step)
        gates[i].wait()
        opened = dot(x[:, :width], w_gate[:, at])
        ups[i].wait()
        raised = dot(x[:, :width], w_up[:, at])
        units[:, at] = (opened * jax.nn.sigmoid(opened) * raised).astype(jnp.bfloat16)
    marks = x[:, width:].astype(jnp.float32)
    lane = lax.broadcasted_iota(jnp.int32, marks.shape, 1)
    mine = (lane % 16 == lax.axis_index("ep")) & (lane < 48)
    weight = jnp.sum(jnp.where(mine, marks, 0.0), axis=1, keepdims=True)
    half = pieces // 2 * piece_rows
    near = half // 2
    for i in range(width // deep):
        downs[i].wait()
        at = slice(i * deep, (i + 1) * deep)
        result = (dot(units[...], w_down[:, at]) * weight).astype(jnp.bfloat16)
        keep[:, at] = result[:near]
        send[:, at] = result[near:half]
        other[:, at] = result[half:]


def expert_chunk(pieces, gate, up, down, after):
    count = len(pieces)
    piece_rows, message = pieces[0].shape
    width, hidden = gate.shape
    rows = count * piece_rows
    anywhere = pl.BlockSpec(memory_space=pl.ANY)
    stored = pl.BlockSpec(memory_space=pltpu.HBM)
    whole = pl.BlockSpec(memory_space=pltpu.VMEM)
    return pl.pallas_call(
        functools.partial(expert_kernel, count),
        out_shape=(
            jax.ShapeDtypeStruct((rows // 4, width), jnp.bfloat16),
            jax.ShapeDtypeStruct((rows // 4, width), jnp.bfloat16),
            jax.ShapeDtypeStruct((rows // 2, width), jnp.bfloat16),
        ),
        in_specs=[stored] * (count + 3) + [anywhere] * len(after),
        out_specs=(whole, whole, whole),
        scratch_shapes=[
            pltpu.VMEM((rows, message), jnp.bfloat16),
            pltpu.VMEM((width, hidden), jnp.bfloat16),
            pltpu.VMEM((width, hidden), jnp.bfloat16),
            pltpu.VMEM((hidden, width), jnp.bfloat16),
            pltpu.VMEM((rows, hidden), jnp.bfloat16),
            pltpu.SemaphoreType.DMA((count,)),
            pltpu.SemaphoreType.DMA((hidden // 256,)),
            pltpu.SemaphoreType.DMA((hidden // 256,)),
            pltpu.SemaphoreType.DMA((width // 1024,)),
        ],
        compiler_params=pltpu.CompilerParams(vmem_limit_bytes=40 * MIB),
        cost_estimate=cost(6 * rows * width * hidden, 6 * width * hidden),
        name="expert_chunk",
    )(*pieces, gate, up, down, *after)


def on_device(
    queries,
    new_kv,
    prompt_kv,
    prompt_lens,
    sample_prompt,
    hidden,
    norm_gain,
    route_ids,
    route_logits,
    w_gate,
    w_up,
    w_down,
):
    chips = lax.axis_size("ep")
    count, _, q_width = queries.shape
    rows = count * STEPS

    def swap(value, by_fan):
        pairs = [
            ((e * 2 + f), ((e ^ by_fan[f]) * 2 + f)) for e in range(chips) for f in range(2)
        ]
        return lax.ppermute(value, ("ep", "fan"), pairs)

    def near(value):
        return swap(value, (1, 2))

    def cross(value):
        return swap(value, (2, 1))

    def far(value, layer):
        return swap(value, (4 * layer, 4 * layer))

    def beside(value):
        return lax.ppermute(value, "fan", [(0, 1), (1, 0)])

    token = norm_message(hidden, norm_gain, route_ids, route_logits)
    opposite = far(token, 2)
    arrived = {0: token, 1: far(token, 1), 2: opposite, 3: far(opposite, 1)}
    pieces = {}
    for layer in (0, 1, 3, 2):
        own = arrived[layer]
        first = near(own)
        four = [own, first, cross(own), cross(first)]
        pieces[layer] = four + [beside(piece) for piece in four]

    marks = jnp.broadcast_to(sample_prompt.astype(jnp.bfloat16)[:, None, None], (count, STEPS, LANES))
    q_mine = queries.reshape(rows, q_width)
    own_mine = jnp.concatenate([new_kv, marks], axis=2).reshape(rows, -1)
    q_both = (q_mine, beside(q_mine))
    own_both = (own_mine, beside(own_mine))

    def expert(layer, *after):
        return expert_chunk(pieces[layer], w_gate[0], w_up[0], w_down[0], after)

    def add_cores(result):
        keep, send, away = result
        back = beside(away)
        half = send.shape[0]
        there = (send.astype(jnp.float32) + back[half:].astype(jnp.float32)).astype(jnp.bfloat16)
        return keep, back, there

    def add_cross(keep, back, there):
        half = keep.shape[0]
        single = half // 2
        turned = cross(there).astype(jnp.float32)
        held = keep.astype(jnp.float32) + back[:half].astype(jnp.float32) + turned
        return held[:single], held[single:].astype(jnp.bfloat16)

    def add_near(held, passed):
        return held + near(passed).astype(jnp.float32)

    def add_far(total, layer):
        return far(total.astype(jnp.bfloat16), layer).astype(jnp.float32)

    context_0 = attend(0, prompt_lens, q_both, own_both, prompt_kv, ())
    result_1 = expert(1, context_0, *pieces[0][1:4], *pieces[3][1:3])
    result_3 = expert(3, result_1[0], *pieces[2][1:4])
    cores_1 = add_cores(result_1)
    result_2 = expert(2, result_3[0], cores_1[2])
    cores_3 = add_cores(result_3)
    cross_1 = add_cross(*cores_1)
    result_0 = expert(0, result_2[0], cores_3[2], cross_1[1])
    cores_2 = add_cores(result_2)
    cross_3 = add_cross(*cores_3)
    near_1 = add_near(*cross_1)
    far_1 = add_far(near_1, 1)
    context_1 = attend(
        1, prompt_lens, q_both, own_both, prompt_kv, (result_0[0], cores_2[2], cross_3[1])
    )
    cores_0 = add_cores(result_0)
    cross_2 = add_cross(*cores_2)
    near_3 = add_near(*cross_3)
    far_3 = add_far(near_3, 1)
    cross_0 = add_cross(*cores_0)
    near_2 = add_near(*cross_2)
    far_2 = add_far(near_2 + far_3, 2)
    near_0 = add_near(*cross_0)
    expert_out = (near_0 + far_1 + far_2).astype(jnp.bfloat16)

    context_mine = [context_0, context_1]
    context_other = [beside(value) for value in context_mine]
    context = place_context(own_mine, context_mine, context_other).reshape(count, STEPS, q_width)
    return (context, expert_out)


def solution(mesh):
    placed = (
        P(("parts", "ep", "fan"), None, None),
        P(("parts", "ep", "fan"), None, None),
        P(("parts", "ep", "fan"), None, None),
        P(("parts", "ep")),
        P(("parts", "ep", "fan")),
        P(("parts", "ep", "fan"), None),
        P(),
        P(("parts", "ep", "fan"), None),
        P(("parts", "ep", "fan"), None),
        P("ep", None, "fan"),
        P("ep", None, "fan"),
        P("ep", "fan", None),
    )
    return jax.shard_map(
        on_device,
        mesh=mesh,
        in_specs=placed,
        out_specs=(P(("parts", "ep", "fan"), None, None), P(("parts", "ep", "fan"), None)),
        check_vma=False,
    )
```

```python
import functools

import jax
import jax.numpy as jnp
from jax import lax
from jax.experimental import pallas as pl
from jax.experimental.pallas import tpu as pltpu
from jax.sharding import PartitionSpec as P

KVH = 4
HD = 128
STEPS = 2
SAMP = 16
TOP = 8
GROUP = SAMP * STEPS
LANES = 128
BAND = 64
UNITS_STEP = 256
DOWN_STEP = 1024
LOG2E = 1.4426950408889634
MIB = 1 << 20


def dot(a, b, contract=((1,), (0,))):
    return lax.dot_general(a, b, (contract, ((), ())), preferred_element_type=jnp.float32)


def cost(flops, moved):
    return pl.CostEstimate(flops=int(flops), bytes_accessed=int(moved), transcendentals=0)


def norm_kernel(hidden_ref, gain_ref, ids_ref, logits_ref, out_ref):
    rows, width = hidden_ref.shape
    hidden = hidden_ref[...].astype(jnp.float32)
    meansq = jnp.mean(hidden * hidden, axis=-1, keepdims=True)
    gain = gain_ref[...].astype(jnp.float32)
    out_ref[:, :width] = (hidden * lax.rsqrt(meansq + 1e-06) * gain).astype(jnp.bfloat16)
    logits = logits_ref[...]
    raised = jnp.exp(logits - jnp.max(logits, axis=0, keepdims=True))
    weights = raised / jnp.sum(raised, axis=0, keepdims=True)
    ids = ids_ref[...]
    number = lax.broadcasted_iota(jnp.int32, (LANES, rows), 0)
    total = jnp.zeros((LANES, rows), jnp.float32)
    for choice in range(TOP):
        picked = (number % 16) == ids[choice : choice + 1, :]
        total = total + jnp.where(picked, weights[choice : choice + 1, :], 0.0)
    high = total.astype(jnp.bfloat16).astype(jnp.float32)
    middle = (total - high).astype(jnp.bfloat16).astype(jnp.float32)
    low = total - high - middle
    piece = number // 16
    parts = jnp.where(
        piece == 0, high, jnp.where(piece == 1, middle, jnp.where(piece == 2, low, 0.0))
    ).astype(jnp.bfloat16)
    first = lax.broadcasted_iota(jnp.int32, (LANES, LANES), 0)
    second = lax.broadcasted_iota(jnp.int32, (LANES, LANES), 1)
    identity = jnp.where(first == second, 1.0, 0.0).astype(jnp.bfloat16)
    out_ref[:, width:] = dot(parts, identity, ((0,), (0,))).astype(jnp.bfloat16)


def norm_message(hidden, gain, ids, logits):
    rows, width = hidden.shape
    return pl.pallas_call(
        norm_kernel,
        out_shape=jax.ShapeDtypeStruct((rows, width + LANES), jnp.bfloat16),
        cost_estimate=cost(1e6, rows * width * 4),
        name="norm_message",
    )(hidden, gain.reshape(1, width), ids.T, logits.T)


def rank_rows(match, rows):
    first = lax.broadcasted_iota(jnp.int32, (rows, rows), 0)
    second = lax.broadcasted_iota(jnp.int32, (rows, rows), 1)
    below = jnp.where(second < first, 1.0, 0.0).astype(jnp.bfloat16)
    return dot(below, match)


def attend_kernel(
    local, lens_ref, q_mine, q_other, k_mine, k_other, v_mine, v_other, n_mine, n_other,
    key_ref, value_ref, *refs
):
    out_ref, q_ref, score_ref, weight_ref, total_ref, select_ref = refs[-6:]
    number = lax.axis_index("fan") * 2 + local
    length = lens_ref[number]
    lane = lax.broadcasted_iota(jnp.int32, (LANES, LANES), 1)

    @pl.when(pl.program_id(0) == 0)
    def _():
        prompts = jnp.concatenate([n_mine[...], n_other[...]], axis=0).astype(jnp.float32)
        chosen = prompts == number.astype(jnp.float32)
        match = jnp.where(chosen, 1.0, 0.0).astype(jnp.bfloat16)
        rank = rank_rows(match, LANES)
        here = chosen & (rank == lane.astype(jnp.float32))
        select_ref[...] = jnp.where(here, 1.0, 0.0).astype(jnp.bfloat16)

    select = select_ref[...]

    def pick(mine, other):
        both = jnp.concatenate([mine[...], other[...]], axis=0)
        return dot(select, both, ((0,), (0,))).astype(jnp.bfloat16)

    queries = pick(q_mine, q_other)[:GROUP]
    span = key_ref.shape[1]
    factor = HD**-0.5 * LOG2E
    heads = queries.shape[1] // HD
    for head in range(heads):
        q_ref[head * GROUP : (head + 1) * GROUP] = queries[:, head * HD : (head + 1) * HD]
    score_ref[:, :span] = dot(q_ref[...], key_ref[0], ((1,), (1,)))
    score_ref[:, span:] = dot(q_ref[...], pick(k_mine, k_other), ((1,), (1,)))
    usable = lax.broadcasted_iota(jnp.int32, (1, span), 1) < length
    row = lax.broadcasted_iota(jnp.int32, (LANES, LANES), 0) % GROUP
    causal = (row // STEPS == lane // STEPS) & (lane <= row)
    for base in range(0, heads * GROUP, BAND):
        at = slice(base, base + BAND)
        scores = jnp.where(usable, score_ref[at, :span], -1e30)
        own = jnp.where(causal[:BAND], score_ref[at, span:], -1e30)
        highest = jnp.maximum(
            jnp.max(scores, axis=-1, keepdims=True), jnp.max(own, axis=-1, keepdims=True)
        )
        raised = jnp.exp2((scores - highest) * factor)
        own_raised = jnp.exp2((own - highest) * factor)
        total = jnp.sum(raised, axis=-1, keepdims=True) + jnp.sum(
            own_raised, axis=-1, keepdims=True
        )
        weight_ref[at, :span] = raised.astype(jnp.bfloat16)
        weight_ref[at, span:] = own_raised.astype(jnp.bfloat16)
        total_ref[at] = jnp.broadcast_to(1.0 / total, (BAND, HD))
    mixed = dot(weight_ref[:, :span], value_ref[0])
    mixed = mixed + dot(weight_ref[:, span:], pick(v_mine, v_other))
    mixed = (mixed * total_ref[...]).astype(jnp.bfloat16)
    for head in range(heads):
        out_ref[:, head * HD : (head + 1) * HD] = mixed[head * GROUP : (head + 1) * GROUP]


def attend(local, lens, queries, own, cache, after):
    rows, q_width = queries[0].shape
    span = cache.shape[1]
    head = q_width // KVH
    band = head // HD * GROUP

    def column(at):
        return pl.BlockSpec((rows, HD), at)

    q_spec = pl.BlockSpec((rows, head), lambda k: (0, k))
    k_spec = column(lambda k: (0, k))
    v_spec = column(lambda k: (0, KVH + k))
    n_spec = column(lambda k: (0, 2 * KVH))
    return pl.pallas_call(
        functools.partial(attend_kernel, local),
        grid=(KVH,),
        out_shape=jax.ShapeDtypeStruct((GROUP, q_width), jnp.bfloat16),
        in_specs=[pl.BlockSpec(memory_space=pltpu.SMEM)]
        + [q_spec, q_spec, k_spec, k_spec, v_spec, v_spec, n_spec, n_spec]
        + [
            pl.BlockSpec((1, span, HD), lambda k: (local, 0, k)),
            pl.BlockSpec((1, span, HD), lambda k: (local, 0, KVH + k)),
        ]
        + [pl.BlockSpec(memory_space=pl.ANY)] * len(after),
        out_specs=pl.BlockSpec((GROUP, head), lambda k: (0, k)),
        scratch_shapes=[
            pltpu.VMEM((band, HD), jnp.bfloat16),
            pltpu.VMEM((band, span + LANES), jnp.float32),
            pltpu.VMEM((band, span + LANES), jnp.bfloat16),
            pltpu.VMEM((band, HD), jnp.float32),
            pltpu.VMEM((LANES, LANES), jnp.bfloat16),
        ],
        compiler_params=pltpu.CompilerParams(vmem_limit_bytes=24 * MIB),
        cost_estimate=cost(5e9, 5 * MIB),
        name="attend",
    )(lens, *queries, *own, *own, *own, cache, cache, *after)


def place_kernel(n_mine, mine_0, mine_1, other_0, other_1, out_ref, place_ref):
    rows = out_ref.shape[0]

    @pl.when(pl.program_id(0) == 0)
    def _():
        fan = lax.axis_index("fan")
        prompts = n_mine[...].astype(jnp.float32)
        lane = lax.broadcasted_iota(jnp.int32, (rows, LANES), 1).astype(jnp.float32)
        every = jnp.ones((rows, rows), jnp.bfloat16)
        place = jnp.zeros((rows, LANES), jnp.float32)
        for side in range(2):
            for local in range(2):
                number = (fan if side == 0 else 1 - fan) * 2 + local
                chosen = prompts == number.astype(jnp.float32)
                match = jnp.where(chosen, 1.0, 0.0).astype(jnp.bfloat16)
                rank = rank_rows(match, rows)
                if side == 1:
                    rank = rank + (GROUP - dot(every, match))
                here = chosen & (rank + (side * 2 + local) * GROUP == lane)
                place = jnp.where(here, 1.0, place)
        place_ref[...] = place.astype(jnp.bfloat16)

    stacked = jnp.concatenate([mine_0[...], mine_1[...], other_0[...], other_1[...]], axis=0)
    out_ref[...] = dot(place_ref[...], stacked).astype(jnp.bfloat16)


def place_context(message, mine, other):
    rows = message.shape[0]
    q_width = mine[0].shape[1]
    width = q_width // 4
    marks = message.shape[1] // LANES - 1
    block = pl.BlockSpec((GROUP, width), lambda k: (0, k))
    return pl.pallas_call(
        place_kernel,
        grid=(q_width // width,),
        out_shape=jax.ShapeDtypeStruct((rows, q_width), jnp.bfloat16),
        in_specs=[pl.BlockSpec((rows, LANES), lambda k: (0, marks)), block, block, block, block],
        out_specs=pl.BlockSpec((rows, width), lambda k: (0, k)),
        scratch_shapes=[pltpu.VMEM((rows, LANES), jnp.bfloat16)],
        cost_estimate=cost(1e8, 3 * MIB),
        name="place_context",
    )(message, *mine, *other)


def units_kernel(pieces, *refs):
    xs, (gate, up) = refs[:pieces], refs[pieces : pieces + 2]
    units, scale, x, w_gate, w_up, x_sem, g_sem, u_sem = refs[-8:]
    width, hidden = gate.shape
    piece_rows = xs[0].shape[0]
    copies = []
    for i in range(pieces):
        at = pl.ds(i * piece_rows, piece_rows)
        copies.append(pltpu.make_async_copy(xs[i], x.at[at], x_sem.at[i]))
    gates, ups = [], []
    for i in range(hidden // UNITS_STEP):
        at = pl.ds(i * UNITS_STEP, UNITS_STEP)
        gates.append(pltpu.make_async_copy(gate.at[:, at], w_gate.at[:, at], g_sem.at[i]))
        ups.append(pltpu.make_async_copy(up.at[:, at], w_up.at[:, at], u_sem.at[i]))
    for copy in copies:
        copy.start()
    for i in range(hidden // UNITS_STEP):
        gates[i].start()
        ups[i].start()
    for copy in copies:
        copy.wait()
    marks = x[:, width:].astype(jnp.float32)
    lane = lax.broadcasted_iota(jnp.int32, marks.shape, 1)
    mine = (lane % 16 == lax.axis_index("ep")) & (lane < 48)
    weight = jnp.sum(jnp.where(mine, marks, 0.0), axis=1, keepdims=True)
    scale[...] = jnp.broadcast_to(weight, scale.shape)
    for i in range(hidden // UNITS_STEP):
        at = slice(i * UNITS_STEP, (i + 1) * UNITS_STEP)
        gates[i].wait()
        opened = dot(x[:, :width], w_gate[:, at])
        ups[i].wait()
        raised = dot(x[:, :width], w_up[:, at])
        units[:, at] = (opened * jax.nn.sigmoid(opened) * raised).astype(jnp.bfloat16)


def expert_units(pieces, gate, up, after):
    count = len(pieces)
    piece_rows, message = pieces[0].shape
    width, hidden = gate.shape
    rows = count * piece_rows
    anywhere = pl.BlockSpec(memory_space=pl.ANY)
    whole = pl.BlockSpec(memory_space=pltpu.VMEM)
    steps = hidden // UNITS_STEP
    return pl.pallas_call(
        functools.partial(units_kernel, count),
        out_shape=(
            jax.ShapeDtypeStruct((rows, hidden), jnp.bfloat16),
            jax.ShapeDtypeStruct((rows, LANES), jnp.float32),
        ),
        in_specs=[anywhere] * (count + 2 + len(after)),
        out_specs=(whole, whole),
        scratch_shapes=[
            pltpu.VMEM((rows, message), jnp.bfloat16),
            pltpu.VMEM((width, hidden), jnp.bfloat16),
            pltpu.VMEM((width, hidden), jnp.bfloat16),
            pltpu.SemaphoreType.DMA((count,)),
            pltpu.SemaphoreType.DMA((steps,)),
            pltpu.SemaphoreType.DMA((steps,)),
        ],
        compiler_params=pltpu.CompilerParams(vmem_limit_bytes=32 * MIB),
        cost_estimate=cost(4 * rows * width * hidden, 4 * width * hidden),
        name="expert_units",
    )(*pieces, gate, up, *after)


def results_kernel(splits, units, scale, down, *refs):
    count = len(splits)
    outs = refs[-count - 2 : -2]
    w_down, sem = refs[-2:]
    width = down.shape[1]
    downs = []
    for i in range(width // DOWN_STEP):
        at = pl.ds(i * DOWN_STEP, DOWN_STEP)
        downs.append(pltpu.make_async_copy(down.at[:, at], w_down.at[:, at], sem.at[i]))
        downs[i].start()
    weight = scale[:, :1]
    for i in range(width // DOWN_STEP):
        downs[i].wait()
        at = slice(i * DOWN_STEP, (i + 1) * DOWN_STEP)
        result = (dot(units[...], w_down[:, at]) * weight).astype(jnp.bfloat16)
        for out, parts in zip(outs, splits):
            filled = 0
            for first, amount in parts:
                out[filled : filled + amount, at] = result[first : first + amount]
                filled += amount


def expert_results(units, scale, down, splits, after):
    rows, hidden = units.shape
    width = down.shape[1]
    anywhere = pl.BlockSpec(memory_space=pl.ANY)
    whole = pl.BlockSpec(memory_space=pltpu.VMEM)
    return pl.pallas_call(
        functools.partial(results_kernel, splits),
        out_shape=[
            jax.ShapeDtypeStruct((sum(amount for _, amount in parts), width), jnp.bfloat16)
            for parts in splits
        ],
        in_specs=[whole, whole] + [anywhere] * (1 + len(after)),
        out_specs=[whole] * len(splits),
        scratch_shapes=[
            pltpu.VMEM((hidden, width), jnp.bfloat16),
            pltpu.SemaphoreType.DMA((width // DOWN_STEP,)),
        ],
        compiler_params=pltpu.CompilerParams(vmem_limit_bytes=32 * MIB),
        cost_estimate=cost(2 * rows * width * hidden, 2 * width * hidden),
        name="expert_results",
    )(units, scale, down, *after)


def on_device(
    queries,
    new_kv,
    prompt_kv,
    prompt_lens,
    sample_prompt,
    hidden,
    norm_gain,
    route_ids,
    route_logits,
    w_gate,
    w_up,
    w_down,
):
    chips = lax.axis_size("ep")
    count, _, q_width = queries.shape
    rows = count * STEPS

    def swap(value, by_fan):
        pairs = [
            ((e * 2 + f), ((e ^ by_fan[f]) * 2 + f)) for e in range(chips) for f in range(2)
        ]
        return lax.ppermute(value, ("ep", "fan"), pairs)

    def near(value):
        return swap(value, (1, 2))

    def cross(value):
        return swap(value, (2, 1))

    def hold(value, *after):
        return lax.optimization_barrier((value, *after))[0]

    def far(value, layer):
        return swap(value, (4 * layer, 4 * layer))

    def beside(value):
        return lax.ppermute(value, "fan", [(0, 1), (1, 0)])

    token = norm_message(hidden, norm_gain, route_ids, route_logits)
    opposite = far(token, 2)
    pair_b = jnp.concatenate([token, far(token, 1)], axis=0)
    turned = far(opposite, 1)

    marks = jnp.broadcast_to(sample_prompt.astype(jnp.bfloat16)[:, None, None], (count, STEPS, LANES))
    q_mine = queries.reshape(rows, q_width)
    own_mine = jnp.concatenate([new_kv, marks], axis=2).reshape(rows, -1)
    q_both = (q_mine, beside(q_mine))
    own_both = (own_mine, beside(own_mine))

    def add_cores(result, *after):
        keep, send, away = result
        back = hold(beside(away), *after)
        half = send.shape[0]
        there = (send.astype(jnp.float32) + back[half:].astype(jnp.float32)).astype(jnp.bfloat16)
        return keep, back, there

    def add_cross(keep, back, there, *after):
        single = keep.shape[0] // 2
        total = keep.astype(jnp.float32) + back[: 2 * single].astype(jnp.float32)
        total = total + hold(cross(there), *after).astype(jnp.float32)
        return total[:single], total[single:].astype(jnp.bfloat16)

    def add_near(held, passed, *after):
        return held + hold(near(passed), *after).astype(jnp.float32)

    def add_far(total, layer):
        return far(total.astype(jnp.bfloat16), layer).astype(jnp.float32)

    tokens = hidden.shape[0]
    both = 2 * tokens
    whole = [
        [(0, 2 * both)],
        [(2 * both, 2 * both)],
        [(4 * both, 4 * both)],
    ]

    def single(at):
        def rows_of(first, amount):
            return [((first + i) * both + at * tokens, tokens) for i in range(amount)]

        return [rows_of(0, 2), rows_of(2, 2), rows_of(4, 4)]

    gate, up, down = w_gate[0], w_up[0], w_down[0]
    first_b = near(pair_b)
    cross_b = cross(pair_b)
    context_0 = attend(0, prompt_lens, q_both, own_both, prompt_kv, (pair_b, opposite))
    first_b = hold(first_b, context_0)
    four_b = [pair_b, first_b, cross_b, cross(first_b)]
    pieces_b = four_b + [beside(piece) for piece in four_b]
    pair_a = jnp.concatenate([opposite, hold(turned, context_0)], axis=0)
    units_b, scale_b = expert_units(pieces_b, gate, up, (context_0, pair_a))
    first_a = hold(near(pair_a), units_b)
    cross_a = hold(cross(pair_a), units_b)
    four_a = [pair_a, first_a, cross_a, cross(first_a)]
    pieces_a = four_a + [beside(piece) for piece in four_a]
    result_b = expert_results(units_b, scale_b, down, whole, (first_a, cross_a))
    units_a, scale_a = expert_units(pieces_a, gate, up, (result_b[0],))
    cores_b = add_cores(result_b, units_a)
    result_3 = expert_results(units_a, scale_a, down, single(1), (cores_b[2],))
    result_2 = expert_results(units_a, scale_a, down, single(0), (result_3[0],))
    cores_3 = add_cores(result_3, result_2[0])
    cores_2 = add_cores(result_2, cores_3[2])
    cross_b = add_cross(*cores_b, cores_2[2])
    context_1 = attend(1, prompt_lens, q_both, own_both, prompt_kv, (cross_b[1],))
    cross_3 = add_cross(*cores_3, context_1)
    near_b = add_near(*cross_b, cross_3[1])
    far_1 = add_far(near_b[tokens:], 1)
    cross_2 = add_cross(*cores_2, cross_3[1])

    context_mine = [context_0, context_1]
    context_other = [beside(value) for value in context_mine]
    own_late = hold(own_mine, cross_2[1])
    context = place_context(own_late, context_mine, context_other).reshape(count, STEPS, q_width)

    near_3 = add_near(*cross_3, context)
    far_3 = add_far(near_3, 1)
    near_2 = add_near(*cross_2, near_3)
    far_2 = add_far(near_2 + far_3, 2)
    expert_out = (near_b[:tokens] + far_1 + far_2).astype(jnp.bfloat16)
    return (context, expert_out)


def solution(mesh):
    placed = (
        P(("parts", "ep", "fan"), None, None),
        P(("parts", "ep", "fan"), None, None),
        P(("parts", "ep", "fan"), None, None),
        P(("parts", "ep")),
        P(("parts", "ep", "fan")),
        P(("parts", "ep", "fan"), None),
        P(),
        P(("parts", "ep", "fan"), None),
        P(("parts", "ep", "fan"), None),
        P("ep", None, "fan"),
        P("ep", None, "fan"),
        P("ep", "fan", None),
    )
    return jax.shard_map(
        on_device,
        mesh=mesh,
        in_specs=placed,
        out_specs=(P(("parts", "ep", "fan"), None, None), P(("parts", "ep", "fan"), None)),
        check_vma=False,
    )
```

```python
import functools

import jax
import jax.numpy as jnp
from jax import lax
from jax.experimental import pallas as pl
from jax.experimental.pallas import tpu as pltpu
from jax.sharding import PartitionSpec as P

KVH = 4
HD = 128
STEPS = 2
SAMP = 16
TOP = 8
GROUP = SAMP * STEPS
LANES = 128
BAND = 64
WIDE = 256
DEEP = 1024
LOG2E = 1.4426950408889634
MIB = 1 << 20


def dot(a, b, contract=((1,), (0,))):
    return lax.dot_general(a, b, (contract, ((), ())), preferred_element_type=jnp.float32)


def cost(flops, moved):
    return pl.CostEstimate(flops=int(flops), bytes_accessed=int(moved), transcendentals=0)


def norm_kernel(hidden_ref, gain_ref, ids_ref, logits_ref, out_ref):
    rows, width = hidden_ref.shape
    hidden = hidden_ref[...].astype(jnp.float32)
    meansq = jnp.mean(hidden * hidden, axis=-1, keepdims=True)
    gain = gain_ref[...].astype(jnp.float32)
    out_ref[:, :width] = (hidden * lax.rsqrt(meansq + 1e-06) * gain).astype(jnp.bfloat16)
    logits = logits_ref[...]
    raised = jnp.exp(logits - jnp.max(logits, axis=0, keepdims=True))
    weights = raised / jnp.sum(raised, axis=0, keepdims=True)
    ids = ids_ref[...]
    number = lax.broadcasted_iota(jnp.int32, (LANES, rows), 0)
    total = jnp.zeros((LANES, rows), jnp.float32)
    for choice in range(TOP):
        picked = (number % 16) == ids[choice : choice + 1, :]
        total = total + jnp.where(picked, weights[choice : choice + 1, :], 0.0)
    high = total.astype(jnp.bfloat16).astype(jnp.float32)
    middle = (total - high).astype(jnp.bfloat16).astype(jnp.float32)
    low = total - high - middle
    piece = number // 16
    parts = jnp.where(
        piece == 0, high, jnp.where(piece == 1, middle, jnp.where(piece == 2, low, 0.0))
    ).astype(jnp.bfloat16)
    first = lax.broadcasted_iota(jnp.int32, (LANES, LANES), 0)
    second = lax.broadcasted_iota(jnp.int32, (LANES, LANES), 1)
    identity = jnp.where(first == second, 1.0, 0.0).astype(jnp.bfloat16)
    out_ref[:, width:] = dot(parts, identity, ((0,), (0,))).astype(jnp.bfloat16)


def norm_message(hidden, gain, ids, logits):
    rows, width = hidden.shape
    return pl.pallas_call(
        norm_kernel,
        out_shape=jax.ShapeDtypeStruct((rows, width + LANES), jnp.bfloat16),
        cost_estimate=cost(1e6, rows * width * 4),
        name="norm_message",
    )(hidden, gain.reshape(1, width), ids.T, logits.T)


def rank_rows(match, rows):
    first = lax.broadcasted_iota(jnp.int32, (rows, rows), 0)
    second = lax.broadcasted_iota(jnp.int32, (rows, rows), 1)
    below = jnp.where(second < first, 1.0, 0.0).astype(jnp.bfloat16)
    return dot(below, match)


def attend_kernel(local, heads, lens_ref, q_mine, q_other, o_mine, o_other, cache, *refs):
    out_ref, keys, values, q_ref, score_ref, weight_ref, total_ref, k_sem, v_sem = refs[-9:]
    copies = []
    for i, head in enumerate(heads):
        at = pl.ds(head * HD, HD)
        copies.append(pltpu.make_async_copy(cache.at[local, :, at], keys.at[i], k_sem.at[i]))
        at = pl.ds((KVH + head) * HD, HD)
        copies.append(pltpu.make_async_copy(cache.at[local, :, at], values.at[i], v_sem.at[i]))
    for copy in copies:
        copy.start()
    number = lax.axis_index("fan") * 2 + local
    length = lens_ref[number]
    span = keys.shape[1]
    head_width = q_mine.shape[1] // KVH
    group = head_width // HD
    marks = 2 * KVH * HD
    prompts = jnp.concatenate([o_mine[:, marks:], o_other[:, marks:]], axis=0).astype(jnp.float32)
    chosen = prompts == number.astype(jnp.float32)
    rank = rank_rows(jnp.where(chosen, 1.0, 0.0).astype(jnp.bfloat16), LANES)
    lane = lax.broadcasted_iota(jnp.int32, (LANES, LANES), 1)
    here = chosen & (rank == lane.astype(jnp.float32))
    select = jnp.where(here, 1.0, 0.0).astype(jnp.bfloat16)

    def pick(mine, other, first, amount, rows):
        at = slice(first, first + amount)
        both = jnp.concatenate([mine[:, at], other[:, at]], axis=0)
        return dot(select[:, :rows], both, ((0,), (0,))).astype(jnp.bfloat16)

    factor = HD**-0.5 * LOG2E
    usable = lax.broadcasted_iota(jnp.int32, (1, span), 1) < length
    row = lax.broadcasted_iota(jnp.int32, (LANES, LANES), 0) % GROUP
    causal = ((row // STEPS == lane // STEPS) & (lane <= row))[:BAND]
    bands = group * GROUP // WIDE
    items = [(i, band) for i in range(len(heads)) for band in range(bands)]
    own = {}

    def products(step):
        i, band = items[step]
        head, slot = heads[i], step % 2
        if band == 0:
            queries = pick(q_mine, q_other, head * head_width, head_width, GROUP)
            for j in range(group):
                q_ref[i, j * GROUP : (j + 1) * GROUP] = queries[:, j * HD : (j + 1) * HD]
            own[i] = (
                pick(o_mine, o_other, head * HD, HD, LANES),
                pick(o_mine, o_other, (KVH + head) * HD, HD, LANES),
            )
            copies[2 * i].wait()
        queries = q_ref[i, band * WIDE : (band + 1) * WIDE]
        score_ref[slot, :, :span] = dot(queries, keys[i], ((1,), (1,)))
        score_ref[slot, :, span:] = dot(queries, own[i][0], ((1,), (1,)))

    products(0)
    for step, (i, band) in enumerate(items):
        slot = step % 2
        if step + 1 < len(items):
            products(step + 1)
        for base in range(0, WIDE, BAND):
            at = slice(base, base + BAND)
            scores = jnp.where(usable, score_ref[slot, at, :span], -1e30)
            mine = jnp.where(causal, score_ref[slot, at, span:], -1e30)
            highest = jnp.maximum(
                jnp.max(scores, axis=-1, keepdims=True), jnp.max(mine, axis=-1, keepdims=True)
            )
            raised = jnp.exp2((scores - highest) * factor)
            own_raised = jnp.exp2((mine - highest) * factor)
            total = jnp.sum(raised, axis=-1, keepdims=True) + jnp.sum(
                own_raised, axis=-1, keepdims=True
            )
            weight_ref[slot, at, :span] = raised.astype(jnp.bfloat16)
            weight_ref[slot, at, span:] = own_raised.astype(jnp.bfloat16)
            total_ref[slot, at] = jnp.broadcast_to(1.0 / total, (BAND, HD))
        if band == 0:
            copies[2 * i + 1].wait()
        mixed = dot(weight_ref[slot, :, :span], values[i])
        mixed = mixed + dot(weight_ref[slot, :, span:], own[i][1])
        mixed = (mixed * total_ref[slot]).astype(jnp.bfloat16)
        for j in range(WIDE // GROUP):
            first = i * head_width + (band * (WIDE // GROUP) + j) * HD
            out_ref[:, first : first + HD] = mixed[j * GROUP : (j + 1) * GROUP]


def attend(local, heads, lens, queries, own, cache, *after):
    rows, q_width = queries[0].shape
    span = cache.shape[1]
    head = q_width // KVH
    band = head // HD * GROUP
    some = len(heads)
    whole = pl.BlockSpec(memory_space=pltpu.VMEM)
    return pl.pallas_call(
        functools.partial(attend_kernel, local, heads),
        out_shape=jax.ShapeDtypeStruct((GROUP, some * head), jnp.bfloat16),
        in_specs=[pl.BlockSpec(memory_space=pltpu.SMEM)]
        + [whole] * 4
        + [pl.BlockSpec(memory_space=pltpu.HBM)]
        + [pl.BlockSpec(memory_space=pl.ANY)] * len(after),
        out_specs=whole,
        scratch_shapes=[
            pltpu.VMEM((some, span, HD), jnp.bfloat16),
            pltpu.VMEM((some, span, HD), jnp.bfloat16),
            pltpu.VMEM((some, band, HD), jnp.bfloat16),
            pltpu.VMEM((2, WIDE, span + LANES), jnp.float32),
            pltpu.VMEM((2, WIDE, span + LANES), jnp.bfloat16),
            pltpu.VMEM((2, WIDE, HD), jnp.float32),
            pltpu.SemaphoreType.DMA((some,)),
            pltpu.SemaphoreType.DMA((some,)),
        ],
        compiler_params=pltpu.CompilerParams(vmem_limit_bytes=24 * MIB),
        cost_estimate=cost(2.5e9, 3 * MIB),
        name="attend",
    )(lens, *queries, *own, cache, *after)


def place_kernel(halves, o_mine, *refs):
    out_ref = refs[-1]
    rows = o_mine.shape[0]
    lane = lax.broadcasted_iota(jnp.int32, (rows, LANES), 1)
    part = lane // GROUP
    side, local = part // 2, part % 2
    fan = lax.axis_index("fan")
    number = jnp.where(side == 0, fan, 1 - fan) * 2 + local
    prompts = o_mine[:, 2 * KVH * HD :].astype(jnp.float32)
    chosen = prompts == number.astype(jnp.float32)
    match = jnp.where(chosen, 1.0, 0.0).astype(jnp.bfloat16)
    rank = rank_rows(match, rows)
    ahead = GROUP - dot(jnp.ones((rows, rows), jnp.bfloat16), match)
    rank = rank + jnp.where(side == 1, ahead, 0.0)
    here = chosen & (rank == (lane % GROUP).astype(jnp.float32))
    place = jnp.where(here, 1.0, 0.0).astype(jnp.bfloat16)
    width = refs[0].shape[1]
    for half in range(halves):
        stacked = jnp.concatenate([ref[...] for ref in refs[4 * half : 4 * half + 4]], axis=0)
        result = dot(place, stacked).astype(jnp.bfloat16)
        at = slice(half * width, (half + 1) * width)
        out_ref[:, :, at] = result.reshape(rows // STEPS, STEPS, width)


def place_context(own, contexts, out_shape):
    whole = pl.BlockSpec(memory_space=pltpu.VMEM)
    return pl.pallas_call(
        functools.partial(place_kernel, len(contexts) // 4),
        out_shape=out_shape,
        in_specs=[whole] * (1 + len(contexts)),
        out_specs=whole,
        compiler_params=pltpu.CompilerParams(vmem_limit_bytes=24 * MIB),
        cost_estimate=cost(1e8, 3 * MIB),
        name="place_context",
    )(own, *contexts)


def expert_kernel(count, at_row, tokens, *refs):
    xs, (gate, up, down) = refs[:count], refs[count : count + 3]
    keep, send, other = refs[-14:-11]
    x, w_gate, w_up, w_down, opened, raised, units, x_sem, g_sem, u_sem, d_sem = refs[-11:]
    width, hidden = gate.shape
    copies, gates, ups, downs = [], [], [], []
    for i in range(count):
        copies.append(
            pltpu.make_async_copy(
                xs[i].at[pl.ds(at_row, tokens)], x.at[pl.ds(i * tokens, tokens)], x_sem.at[i]
            )
        )
    for i in range(width // DEEP):
        at = pl.ds(i * DEEP, DEEP)
        gates.append(pltpu.make_async_copy(gate.at[at], w_gate.at[at], g_sem.at[i]))
        ups.append(pltpu.make_async_copy(up.at[at], w_up.at[at], u_sem.at[i]))
        downs.append(pltpu.make_async_copy(down.at[:, at], w_down.at[:, at], d_sem.at[i]))
    for copy in copies:
        copy.start()
    for i in range(width // DEEP):
        gates[i].start()
        ups[i].start()
    for copy in downs:
        copy.start()
    for copy in copies:
        copy.wait()
    for i in range(width // DEEP):
        at = slice(i * DEEP, (i + 1) * DEEP)
        gates[i].wait()
        product = dot(x[:, at], w_gate[at])
        opened[...] = product if i == 0 else opened[...] + product
        ups[i].wait()
        product = dot(x[:, at], w_up[at])
        raised[...] = product if i == 0 else raised[...] + product
    through = opened[...]
    units[...] = (through * jax.nn.sigmoid(through) * raised[...]).astype(jnp.bfloat16)
    marks = x[:, width:].astype(jnp.float32)
    lane = lax.broadcasted_iota(jnp.int32, marks.shape, 1)
    mine = (lane % 16 == lax.axis_index("ep")) & (lane < 48)
    weight = jnp.sum(jnp.where(mine, marks, 0.0), axis=1, keepdims=True)
    half = count // 2 * tokens
    for i in range(width // DEEP):
        downs[i].wait()
        at = slice(i * DEEP, (i + 1) * DEEP)
        result = (dot(units[...], w_down[:, at]) * weight).astype(jnp.bfloat16)
        keep[:, at] = result[: half // 2]
        send[:, at] = result[half // 2 : half]
        other[:, at] = result[half:]


def expert_chunk(pieces, at_row, tokens, gate, up, down, *after):
    count = len(pieces)
    message = pieces[0].shape[1]
    width, hidden = gate.shape
    rows = count * tokens
    whole = pl.BlockSpec(memory_space=pltpu.VMEM)
    steps = width // DEEP
    return pl.pallas_call(
        functools.partial(expert_kernel, count, at_row, tokens),
        out_shape=(
            jax.ShapeDtypeStruct((rows // 4, width), jnp.bfloat16),
            jax.ShapeDtypeStruct((rows // 4, width), jnp.bfloat16),
            jax.ShapeDtypeStruct((rows // 2, width), jnp.bfloat16),
        ),
        in_specs=[pl.BlockSpec(memory_space=pl.ANY)] * count
        + [pl.BlockSpec(memory_space=pltpu.HBM)] * 3
        + [pl.BlockSpec(memory_space=pl.ANY)] * len(after),
        out_specs=(whole, whole, whole),
        scratch_shapes=[
            pltpu.VMEM((rows, message), jnp.bfloat16),
            pltpu.VMEM((width, hidden), jnp.bfloat16),
            pltpu.VMEM((width, hidden), jnp.bfloat16),
            pltpu.VMEM((hidden, width), jnp.bfloat16),
            pltpu.VMEM((rows, hidden), jnp.float32),
            pltpu.VMEM((rows, hidden), jnp.float32),
            pltpu.VMEM((rows, hidden), jnp.bfloat16),
            pltpu.SemaphoreType.DMA((count,)),
            pltpu.SemaphoreType.DMA((steps,)),
            pltpu.SemaphoreType.DMA((steps,)),
            pltpu.SemaphoreType.DMA((steps,)),
        ],
        compiler_params=pltpu.CompilerParams(vmem_limit_bytes=40 * MIB),
        cost_estimate=cost(6 * rows * width * hidden, 6 * width * hidden),
        name="expert_chunk",
    )(*pieces, gate, up, down, *after)


def on_device(
    queries,
    new_kv,
    prompt_kv,
    prompt_lens,
    sample_prompt,
    hidden,
    norm_gain,
    route_ids,
    route_logits,
    w_gate,
    w_up,
    w_down,
):
    chips = lax.axis_size("ep")
    count, _, q_width = queries.shape
    rows = count * STEPS

    def swap(value, by_fan):
        pairs = [
            ((e * 2 + f), ((e ^ by_fan[f]) * 2 + f)) for e in range(chips) for f in range(2)
        ]
        return lax.ppermute(value, ("ep", "fan"), pairs)

    def near(value):
        return swap(value, (1, 2))

    def cross(value):
        return swap(value, (2, 1))

    def far(value, layer):
        return swap(value, (4 * layer, 4 * layer))

    def beside(value):
        return lax.ppermute(value, "fan", [(0, 1), (1, 0)])

    gate, up, down = w_gate[0], w_up[0], w_down[0]
    tokens = hidden.shape[0]
    marks = jnp.broadcast_to(sample_prompt.astype(jnp.bfloat16)[:, None, None], (count, STEPS, LANES))
    q_mine = queries.reshape(rows, q_width)
    own_mine = jnp.concatenate([new_kv, marks], axis=2).reshape(rows, -1)
    q_both = (q_mine, beside(q_mine))
    own_both = (own_mine, beside(own_mine))

    def attend_half(local, half, *after):
        heads = tuple(range(half * KVH // 2, (half + 1) * KVH // 2))
        return attend(local, heads, prompt_lens, q_both, own_both, prompt_kv, *after)

    def expert(pieces, at_row, *after):
        return expert_chunk(pieces, at_row, tokens, gate, up, down, *after)

    def with_fan(pieces):
        return pieces + [beside(piece) for piece in pieces]

    def sum_cores(result, back):
        send = result[1]
        half = send.shape[0]
        return (send.astype(jnp.float32) + back[half:].astype(jnp.float32)).astype(jnp.bfloat16)

    def sum_cross(result, back, turned):
        single = tokens

        def total(at):
            mine = result[0][at].astype(jnp.float32) + back[at].astype(jnp.float32)
            return mine + turned[at].astype(jnp.float32)

        return total(slice(0, single)), total(slice(single, 2 * single)).astype(jnp.bfloat16)

    def widen(value):
        return value.astype(jnp.float32)

    def narrow(value):
        return value.astype(jnp.bfloat16)

    sync = lax.optimization_barrier

    token = norm_message(hidden, norm_gain, route_ids, route_logits)
    first_0, cross_0 = near(token), cross(token)
    level_2, level_1 = far(token, 2), far(token, 1)
    context_0a = attend_half(0, 0, first_0)
    third_0 = cross(first_0)
    context_0a, third_0, cross_0, level_1, level_2 = sync(
        (context_0a, third_0, cross_0, level_1, level_2)
    )
    pieces_0 = with_fan([token, first_0, cross_0, third_0])
    pair = jnp.concatenate([level_2, level_1], axis=0)
    level_3 = far(level_2, 1)
    context_0b = attend_half(0, 1, context_0a, pair)
    context_0b, level_3, *pieces_0 = sync((context_0b, level_3, *pieces_0))
    result_0 = expert(pieces_0, 0, context_0b)

    first_p, cross_p, result_0 = sync((near(pair), cross(pair), result_0))
    back_0 = beside(result_0[2])
    third_p = cross(first_p)
    context_1a = attend_half(1, 0, first_p)
    context_1a, third_p, back_0 = sync((context_1a, third_p, back_0))
    pieces_p = with_fan([pair, first_p, cross_p, third_p])
    there_0 = sum_cores(result_0, back_0)
    result_2 = expert(pieces_p, 0, context_1a, there_0)

    first_3, cross_3, turned_0, result_2 = sync(
        (near(level_3), cross(level_3), cross(there_0), result_2)
    )
    back_2 = beside(result_2[2])
    third_3 = cross(first_3)
    held_0, passed_0 = sum_cross(result_0, back_0, turned_0)
    context_1b = attend_half(1, 1, first_3, passed_0)
    context_1b, third_3, back_2 = sync((context_1b, third_3, back_2))
    pieces_3 = with_fan([level_3, first_3, cross_3, third_3])
    there_2 = sum_cores(result_2, back_2)
    result_3 = expert(pieces_3, 0, context_1b, there_2)

    ended_0, turned_2, result_3 = sync((near(passed_0), cross(there_2), result_3))
    back_3 = beside(result_3[2])
    held_2, passed_2 = sum_cross(result_2, back_2, turned_2)
    there_3 = sum_cores(result_3, back_3)
    result_1 = expert(pieces_p, tokens, there_3, passed_2)

    contexts = [context_0a, context_0b, context_1a, context_1b]
    sent = [beside(value) for value in contexts]
    ended_2, turned_3, result_1, sent = sync((near(passed_2), cross(there_3), result_1, sent))
    back_1 = beside(result_1[2])
    held_3, passed_3 = sum_cross(result_3, back_3, turned_3)
    ordered = [contexts[0], contexts[2], sent[0], sent[2], contexts[1], contexts[3], sent[1], sent[3]]
    own_late, _ = sync((own_mine, passed_3))
    context = place_context(own_late, ordered, jax.ShapeDtypeStruct(queries.shape, jnp.bfloat16))
    context, ended_3, back_1 = sync((context, near(passed_3), back_1))
    there_1 = sum_cores(result_1, back_1)
    total_3 = narrow(held_3 + widen(ended_3))
    total_2 = held_2 + widen(ended_2) + widen(far(total_3, 1))
    held_1, passed_1 = sum_cross(result_1, back_1, cross(there_1))
    far_2 = far(narrow(total_2), 2)
    far_1 = far(narrow(held_1 + widen(near(passed_1))), 1)
    expert_out = narrow(held_0 + widen(ended_0) + widen(far_1) + widen(far_2))
    return (context, expert_out)


def solution(mesh):
    placed = (
        P(("parts", "ep", "fan"), None, None),
        P(("parts", "ep", "fan"), None, None),
        P(("parts", "ep", "fan"), None, None),
        P(("parts", "ep")),
        P(("parts", "ep", "fan")),
        P(("parts", "ep", "fan"), None),
        P(),
        P(("parts", "ep", "fan"), None),
        P(("parts", "ep", "fan"), None),
        P("ep", None, "fan"),
        P("ep", None, "fan"),
        P("ep", "fan", None),
    )
    return jax.shard_map(
        on_device,
        mesh=mesh,
        in_specs=placed,
        out_specs=(P(("parts", "ep", "fan"), None, None), P(("parts", "ep", "fan"), None)),
        check_vma=False,
    )
```

```python
import functools

import jax
import jax.numpy as jnp
from jax import lax
from jax.experimental import pallas as pl
from jax.experimental.pallas import tpu as pltpu
from jax.sharding import PartitionSpec as P

KVH = 4
HD = 128
STEPS = 2
SAMP = 16
TOP = 8
GROUP = SAMP * STEPS
LANES = 128
BAND = 64
WIDE = 256
DEEP = 1024
LOG2E = 1.4426950408889634
MIB = 1 << 20


def dot(a, b, contract=((1,), (0,))):
    return lax.dot_general(a, b, (contract, ((), ())), preferred_element_type=jnp.float32)


SMALL = pl.CostEstimate(flops=1 << 20, bytes_accessed=1 << 14, transcendentals=0)


def norm_kernel(hidden_ref, gain_ref, ids_ref, logits_ref, out_ref):
    rows, width = hidden_ref.shape
    hidden = hidden_ref[...].astype(jnp.float32)
    meansq = jnp.mean(hidden * hidden, axis=-1, keepdims=True)
    gain = gain_ref[...].astype(jnp.float32).reshape(1, width)
    out_ref[:, :width] = (hidden * lax.rsqrt(meansq + 1e-06) * gain).astype(jnp.bfloat16)
    logits = logits_ref[...]
    raised = jnp.exp(logits - jnp.max(logits, axis=0, keepdims=True))
    weights = raised / jnp.sum(raised, axis=0, keepdims=True)
    ids = ids_ref[...]
    number = lax.broadcasted_iota(jnp.int32, (LANES, rows), 0)
    total = jnp.zeros((LANES, rows), jnp.float32)
    for choice in range(TOP):
        picked = (number % 16) == ids[choice : choice + 1, :]
        total = total + jnp.where(picked, weights[choice : choice + 1, :], 0.0)
    high = total.astype(jnp.bfloat16).astype(jnp.float32)
    middle = (total - high).astype(jnp.bfloat16).astype(jnp.float32)
    low = total - high - middle
    piece = number // 16
    parts = jnp.where(
        piece == 0, high, jnp.where(piece == 1, middle, jnp.where(piece == 2, low, 0.0))
    ).astype(jnp.bfloat16)
    first = lax.broadcasted_iota(jnp.int32, (LANES, LANES), 0)
    second = lax.broadcasted_iota(jnp.int32, (LANES, LANES), 1)
    identity = jnp.where(first == second, 1.0, 0.0).astype(jnp.bfloat16)
    out_ref[:, width:] = dot(parts, identity, ((0,), (0,))).astype(jnp.bfloat16)


def norm_message(hidden, gain, ids, logits):
    rows, width = hidden.shape
    return pl.pallas_call(
        norm_kernel,
        out_shape=jax.ShapeDtypeStruct((rows, width + LANES), jnp.bfloat16),
        cost_estimate=SMALL,
        name="norm_message",
    )(hidden, gain, ids.T, logits.T)


def rank_rows(match, rows):
    first = lax.broadcasted_iota(jnp.int32, (rows, rows), 0)
    second = lax.broadcasted_iota(jnp.int32, (rows, rows), 1)
    below = jnp.where(second < first, 1.0, 0.0).astype(jnp.bfloat16)
    return dot(below, match)


def attend_kernel(local, heads, lens_ref, q_mine, q_other, o_mine, o_other, cache, *refs):
    out_ref, keys, values, q_ref, score_ref, weight_ref, total_ref, k_sem, v_sem = refs[-9:]
    copies = []
    for i, head in enumerate(heads):
        at = pl.ds(head * HD, HD)
        copies.append(pltpu.make_async_copy(cache.at[local, :, at], keys.at[i], k_sem.at[i]))
        at = pl.ds((KVH + head) * HD, HD)
        copies.append(pltpu.make_async_copy(cache.at[local, :, at], values.at[i], v_sem.at[i]))
    for copy in copies:
        copy.start()
    number = lax.axis_index("fan") * 2 + local
    length = lens_ref[number]
    span = keys.shape[1]
    head_width = q_mine.shape[1] // KVH
    group = head_width // HD
    marks = 2 * KVH * HD
    prompts = jnp.concatenate([o_mine[:, marks:], o_other[:, marks:]], axis=0).astype(jnp.float32)
    chosen = prompts == number.astype(jnp.float32)
    rank = rank_rows(jnp.where(chosen, 1.0, 0.0).astype(jnp.bfloat16), LANES)
    lane = lax.broadcasted_iota(jnp.int32, (LANES, LANES), 1)
    here = chosen & (rank == lane.astype(jnp.float32))
    select = jnp.where(here, 1.0, 0.0).astype(jnp.bfloat16)

    def pick(mine, other, first, amount, rows):
        at = slice(first, first + amount)
        both = jnp.concatenate([mine[:, at], other[:, at]], axis=0)
        return dot(select[:, :rows], both, ((0,), (0,))).astype(jnp.bfloat16)

    factor = HD**-0.5 * LOG2E
    usable = lax.broadcasted_iota(jnp.int32, (1, span), 1) < length
    row = lax.broadcasted_iota(jnp.int32, (LANES, LANES), 0) % GROUP
    causal = ((row // STEPS == lane // STEPS) & (lane <= row))[:BAND]
    bands = group * GROUP // WIDE
    items = [(i, band) for i in range(len(heads)) for band in range(bands)]
    own = {}

    def products(step):
        i, band = items[step]
        head, slot = heads[i], step % 2
        if band == 0:
            queries = pick(q_mine, q_other, head * head_width, head_width, GROUP)
            for j in range(group):
                q_ref[i, j * GROUP : (j + 1) * GROUP] = queries[:, j * HD : (j + 1) * HD]
            own[i] = (
                pick(o_mine, o_other, head * HD, HD, LANES),
                pick(o_mine, o_other, (KVH + head) * HD, HD, LANES),
            )
            copies[2 * i].wait()
        queries = q_ref[i, band * WIDE : (band + 1) * WIDE]
        score_ref[slot, :, :span] = dot(queries, keys[i], ((1,), (1,)))
        score_ref[slot, :, span:] = dot(queries, own[i][0], ((1,), (1,)))

    products(0)
    for step, (i, band) in enumerate(items):
        slot = step % 2
        if step + 1 < len(items):
            products(step + 1)
        for base in range(0, WIDE, BAND):
            at = slice(base, base + BAND)
            scores = jnp.where(usable, score_ref[slot, at, :span], -1e30)
            mine = jnp.where(causal, score_ref[slot, at, span:], -1e30)
            highest = jnp.maximum(
                jnp.max(scores, axis=-1, keepdims=True), jnp.max(mine, axis=-1, keepdims=True)
            )
            raised = jnp.exp2((scores - highest) * factor)
            own_raised = jnp.exp2((mine - highest) * factor)
            total = jnp.sum(raised, axis=-1, keepdims=True) + jnp.sum(
                own_raised, axis=-1, keepdims=True
            )
            weight_ref[slot, at, :span] = raised.astype(jnp.bfloat16)
            weight_ref[slot, at, span:] = own_raised.astype(jnp.bfloat16)
            total_ref[slot, at] = jnp.broadcast_to(1.0 / total, (BAND, HD))
        if band == 0:
            copies[2 * i + 1].wait()
        mixed = dot(weight_ref[slot, :, :span], values[i])
        mixed = mixed + dot(weight_ref[slot, :, span:], own[i][1])
        mixed = (mixed * total_ref[slot]).astype(jnp.bfloat16)
        for j in range(WIDE // GROUP):
            first = i * head_width + (band * (WIDE // GROUP) + j) * HD
            out_ref[:, first : first + HD] = mixed[j * GROUP : (j + 1) * GROUP]


def attend(local, heads, lens, queries, own, cache, *after):
    rows, q_width = queries[0].shape
    span = cache.shape[1]
    head = q_width // KVH
    band = head // HD * GROUP
    some = len(heads)
    whole = pl.BlockSpec(memory_space=pltpu.VMEM)
    return pl.pallas_call(
        functools.partial(attend_kernel, local, heads),
        out_shape=jax.ShapeDtypeStruct((GROUP, some * head), jnp.bfloat16),
        in_specs=[pl.BlockSpec(memory_space=pltpu.SMEM)]
        + [whole] * 4
        + [pl.BlockSpec(memory_space=pltpu.HBM)]
        + [pl.BlockSpec(memory_space=pl.ANY)] * len(after),
        out_specs=whole,
        scratch_shapes=[
            pltpu.VMEM((some, span, HD), jnp.bfloat16),
            pltpu.VMEM((some, span, HD), jnp.bfloat16),
            pltpu.VMEM((some, band, HD), jnp.bfloat16),
            pltpu.VMEM((2, WIDE, span + LANES), jnp.float32),
            pltpu.VMEM((2, WIDE, span + LANES), jnp.bfloat16),
            pltpu.VMEM((2, WIDE, HD), jnp.float32),
            pltpu.SemaphoreType.DMA((some,)),
            pltpu.SemaphoreType.DMA((some,)),
        ],
        compiler_params=pltpu.CompilerParams(vmem_limit_bytes=50 * MIB),
        cost_estimate=SMALL,
        name="attend",
    )(lens, *queries, *own, cache, *after)


def place_kernel(halves, o_mine, *refs):
    out_ref = refs[-1]
    rows = o_mine.shape[0]
    lane = lax.broadcasted_iota(jnp.int32, (rows, LANES), 1)
    part = lane // GROUP
    side, local = part // 2, part % 2
    fan = lax.axis_index("fan")
    number = jnp.where(side == 0, fan, 1 - fan) * 2 + local
    prompts = o_mine[:, 2 * KVH * HD :].astype(jnp.float32)
    chosen = prompts == number.astype(jnp.float32)
    match = jnp.where(chosen, 1.0, 0.0).astype(jnp.bfloat16)
    rank = rank_rows(match, rows)
    ahead = GROUP - dot(jnp.ones((rows, rows), jnp.bfloat16), match)
    rank = rank + jnp.where(side == 1, ahead, 0.0)
    here = chosen & (rank == (lane % GROUP).astype(jnp.float32))
    place = jnp.where(here, 1.0, 0.0).astype(jnp.bfloat16)
    width = refs[0].shape[1]
    for half in range(halves):
        stacked = jnp.concatenate([ref[...] for ref in refs[4 * half : 4 * half + 4]], axis=0)
        result = dot(place, stacked).astype(jnp.bfloat16)
        at = slice(half * width, (half + 1) * width)
        out_ref[:, :, at] = result.reshape(rows // STEPS, STEPS, width)


def place_context(own, contexts, out_shape):
    whole = pl.BlockSpec(memory_space=pltpu.VMEM)
    return pl.pallas_call(
        functools.partial(place_kernel, len(contexts) // 4),
        out_shape=out_shape,
        in_specs=[whole] * (1 + len(contexts)),
        out_specs=whole,
        compiler_params=pltpu.CompilerParams(vmem_limit_bytes=12 * MIB),
        cost_estimate=SMALL,
        name="place_context",
    )(own, *contexts)


def expert_kernel(count, at_row, tokens, *refs):
    xs, (gate, up, down) = refs[:count], refs[count : count + 3]
    keep, send, other = refs[-14:-11]
    x, w_gate, w_up, w_down, opened, raised, units, x_sem, g_sem, u_sem, d_sem = refs[-11:]
    width, hidden = gate.shape
    copies, gates, ups, downs = [], [], [], []
    for i in range(count):
        copies.append(
            pltpu.make_async_copy(
                xs[i].at[pl.ds(at_row, tokens)], x.at[pl.ds(i * tokens, tokens)], x_sem.at[i]
            )
        )
    for i in range(width // DEEP):
        at = pl.ds(i * DEEP, DEEP)
        gates.append(pltpu.make_async_copy(gate.at[at], w_gate.at[at], g_sem.at[i]))
        ups.append(pltpu.make_async_copy(up.at[at], w_up.at[at], u_sem.at[i]))
        downs.append(pltpu.make_async_copy(down.at[:, at], w_down.at[:, at], d_sem.at[i]))
    for copy in copies:
        copy.start()
    for i in range(width // DEEP):
        gates[i].start()
        ups[i].start()
    for copy in downs:
        copy.start()
    for copy in copies:
        copy.wait()
    for i in range(width // DEEP):
        at = slice(i * DEEP, (i + 1) * DEEP)
        gates[i].wait()
        product = dot(x[:, at], w_gate[at])
        opened[...] = product if i == 0 else opened[...] + product
        ups[i].wait()
        product = dot(x[:, at], w_up[at])
        raised[...] = product if i == 0 else raised[...] + product
    through = opened[...]
    units[...] = (through * jax.nn.sigmoid(through) * raised[...]).astype(jnp.bfloat16)
    marks = x[:, width:].astype(jnp.float32)
    lane = lax.broadcasted_iota(jnp.int32, marks.shape, 1)
    mine = (lane % 16 == lax.axis_index("ep")) & (lane < 48)
    weight = jnp.sum(jnp.where(mine, marks, 0.0), axis=1, keepdims=True)
    half = count // 2 * tokens
    for i in range(width // DEEP):
        downs[i].wait()
        at = slice(i * DEEP, (i + 1) * DEEP)
        result = (dot(units[...], w_down[:, at]) * weight).astype(jnp.bfloat16)
        keep[:, at] = result[: half // 2]
        send[:, at] = result[half // 2 : half]
        other[:, at] = result[half:]


def expert_chunk(pieces, at_row, tokens, gate, up, down, *after):
    count = len(pieces)
    message = pieces[0].shape[1]
    width, hidden = gate.shape
    rows = count * tokens
    whole = pl.BlockSpec(memory_space=pltpu.VMEM)
    steps = width // DEEP
    return pl.pallas_call(
        functools.partial(expert_kernel, count, at_row, tokens),
        out_shape=(
            jax.ShapeDtypeStruct((rows // 4, width), jnp.bfloat16),
            jax.ShapeDtypeStruct((rows // 4, width), jnp.bfloat16),
            jax.ShapeDtypeStruct((rows // 2, width), jnp.bfloat16),
        ),
        in_specs=[pl.BlockSpec(memory_space=pl.ANY)] * count
        + [pl.BlockSpec(memory_space=pltpu.HBM)] * 3
        + [pl.BlockSpec(memory_space=pl.ANY)] * len(after),
        out_specs=(whole, whole, whole),
        scratch_shapes=[
            pltpu.VMEM((rows, message), jnp.bfloat16),
            pltpu.VMEM((width, hidden), jnp.bfloat16),
            pltpu.VMEM((width, hidden), jnp.bfloat16),
            pltpu.VMEM((hidden, width), jnp.bfloat16),
            pltpu.VMEM((rows, hidden), jnp.float32),
            pltpu.VMEM((rows, hidden), jnp.float32),
            pltpu.VMEM((rows, hidden), jnp.bfloat16),
            pltpu.SemaphoreType.DMA((count,)),
            pltpu.SemaphoreType.DMA((steps,)),
            pltpu.SemaphoreType.DMA((steps,)),
            pltpu.SemaphoreType.DMA((steps,)),
        ],
        compiler_params=pltpu.CompilerParams(vmem_limit_bytes=50 * MIB),
        cost_estimate=SMALL,
        name="expert_chunk",
    )(*pieces, gate, up, down, *after)


def on_device(
    queries,
    new_kv,
    prompt_kv,
    prompt_lens,
    sample_prompt,
    hidden,
    norm_gain,
    route_ids,
    route_logits,
    w_gate,
    w_up,
    w_down,
):
    chips = lax.axis_size("ep")
    count, _, q_width = queries.shape
    rows = count * STEPS

    def swap(value, by_fan):
        pairs = [
            ((e * 2 + f), ((e ^ by_fan[f]) * 2 + f)) for e in range(chips) for f in range(2)
        ]
        return lax.ppermute(value, ("ep", "fan"), pairs)

    def near(value):
        return swap(value, (1, 2))

    def cross(value):
        return swap(value, (2, 1))

    def far(value, layer):
        return swap(value, (4 * layer, 4 * layer))

    def beside(value):
        return lax.ppermute(value, "fan", [(0, 1), (1, 0)])

    gate, up, down = w_gate[0], w_up[0], w_down[0]
    tokens = hidden.shape[0]
    sync = lax.optimization_barrier
    token = norm_message(hidden, norm_gain, route_ids, route_logits)
    token, queries, new_kv = sync((token, queries, new_kv))
    marks = jnp.broadcast_to(sample_prompt.astype(jnp.bfloat16)[:, None, None], (count, STEPS, LANES))
    q_mine = queries.reshape(rows, q_width)
    own_mine = jnp.concatenate([new_kv, marks], axis=2).reshape(rows, -1)
    q_both = (q_mine, beside(q_mine))
    own_both = (own_mine, beside(own_mine))

    def attend_half(local, half, *after):
        heads = tuple(range(half * KVH // 2, (half + 1) * KVH // 2))
        return attend(local, heads, prompt_lens, q_both, own_both, prompt_kv, *after)

    def expert(pieces, at_row, *after):
        return expert_chunk(pieces, at_row, tokens, gate, up, down, *after)

    def with_fan(pieces):
        return pieces + [beside(piece) for piece in pieces]

    def sum_cores(result, back):
        send = result[1]
        half = send.shape[0]
        return (send.astype(jnp.float32) + back[half:].astype(jnp.float32)).astype(jnp.bfloat16)

    def sum_cross(result, back, turned):
        single = tokens

        def total(at):
            mine = result[0][at].astype(jnp.float32) + back[at].astype(jnp.float32)
            return mine + turned[at].astype(jnp.float32)

        return total(slice(0, single)), total(slice(single, 2 * single)).astype(jnp.bfloat16)

    def widen(value):
        return value.astype(jnp.float32)

    def narrow(value):
        return value.astype(jnp.bfloat16)

    level_2, level_1 = far(token, 2), far(token, 1)
    first_0, cross_0 = near(token), cross(token)
    pair = jnp.concatenate([level_2, level_1], axis=0)
    level_3 = far(level_2, 1)
    third_0 = cross(first_0)
    context_0a = attend_half(0, 0, pair, first_0, cross_0)
    context_0a, third_0 = sync((context_0a, third_0))
    pieces_0 = with_fan([token, first_0, cross_0, third_0])
    context_0b = attend_half(0, 1, context_0a)
    context_0b, level_3, first_p, cross_p, *pieces_0 = sync(
        (context_0b, level_3, near(pair), cross(pair), *pieces_0)
    )
    third_p = cross(first_p)
    first_3, cross_3 = near(level_3), cross(level_3)
    result_0 = expert(pieces_0, 0, context_0b, first_p)

    third_p, first_3, cross_3, result_0 = sync((third_p, first_3, cross_3, result_0))
    back_0 = beside(result_0[2])
    pieces_p = with_fan([pair, first_p, cross_p, third_p])
    third_3 = cross(first_3)
    context_1a = attend_half(1, 0, third_p, first_3)
    context_1a, back_0, third_3, *pieces_p = sync((context_1a, back_0, third_3, *pieces_p))
    there_0 = sum_cores(result_0, back_0)
    pieces_3 = with_fan([level_3, first_3, cross_3, third_3])
    result_2 = expert(pieces_p, 0, context_1a, there_0)

    turned_0, result_2, *pieces_3 = sync((cross(there_0), result_2, *pieces_3))
    back_2 = beside(result_2[2])
    held_0, passed_0 = sum_cross(result_0, back_0, turned_0)
    there_2 = sum_cores(result_2, back_2)
    result_3 = expert(pieces_3, 0, there_2, passed_0)

    ended_0, turned_2, result_3 = sync((near(passed_0), cross(there_2), result_3))
    back_3 = beside(result_3[2])
    held_2, passed_2 = sum_cross(result_2, back_2, turned_2)
    context_1b = attend_half(1, 1, passed_2)
    context_1b, back_3 = sync((context_1b, back_3))
    there_3 = sum_cores(result_3, back_3)
    result_1 = expert(pieces_p, tokens, there_3, passed_2)

    contexts = [context_0a, context_0b, context_1a, context_1b]
    sent = [beside(value) for value in contexts]
    ended_2, turned_3, result_1, sent = sync((near(passed_2), cross(there_3), result_1, sent))
    back_1 = beside(result_1[2])
    held_3, passed_3 = sum_cross(result_3, back_3, turned_3)
    ordered = [contexts[0], contexts[2], sent[0], sent[2], contexts[1], contexts[3], sent[1], sent[3]]
    far_2 = far(narrow(held_2 + widen(ended_2)), 2)
    there_1 = sum_cores(result_1, back_1)
    own_late, _ = sync((own_mine, there_1))
    context = place_context(own_late, ordered, jax.ShapeDtypeStruct(queries.shape, jnp.bfloat16))
    context, ended_3 = sync((context, near(passed_3)))
    far_3 = far(narrow(held_3 + widen(ended_3)), 3)
    held_1, passed_1 = sum_cross(result_1, back_1, cross(there_1))
    far_1 = far(narrow(held_1 + widen(near(passed_1))), 1)
    total = held_0 + widen(ended_0) + widen(far_1)
    expert_out = narrow(total + widen(far_2) + widen(far_3))
    return (context, expert_out)


def solution(mesh):
    placed = (
        P(("parts", "ep", "fan"), None, None),
        P(("parts", "ep", "fan"), None, None),
        P(("parts", "ep", "fan"), None, None),
        P(("parts", "ep")),
        P(("parts", "ep", "fan")),
        P(("parts", "ep", "fan"), None),
        P(),
        P(("parts", "ep", "fan"), None),
        P(("parts", "ep", "fan"), None),
        P("ep", None, "fan"),
        P("ep", None, "fan"),
        P("ep", "fan", None),
    )
    return jax.shard_map(
        on_device,
        mesh=mesh,
        in_specs=placed,
        out_specs=(P(("parts", "ep", "fan"), None, None), P(("parts", "ep", "fan"), None)),
        check_vma=False,
    )
```

```python
import functools

import jax
import jax.numpy as jnp
from jax import lax
from jax.experimental import pallas as pl
from jax.experimental.pallas import tpu as pltpu
from jax.sharding import PartitionSpec as P

KVH = 4
HD = 128
STEPS = 2
SAMP = 16
TOP = 8
GROUP = SAMP * STEPS
LANES = 128
BAND = 64
WIDE = 256
DEEP = 1024
EXPERT_VMEM = 12
ATTEND_VMEM = 16
LOG2E = 1.4426950408889634
MIB = 1 << 20


def dot(a, b, contract=((1,), (0,))):
    return lax.dot_general(a, b, (contract, ((), ())), preferred_element_type=jnp.float32)


SMALL = pl.CostEstimate(flops=1 << 20, bytes_accessed=1 << 14, transcendentals=0)


def norm_kernel(hidden_ref, gain_ref, ids_ref, logits_ref, out_ref):
    rows, width = hidden_ref.shape
    hidden = hidden_ref[...].astype(jnp.float32)
    meansq = jnp.mean(hidden * hidden, axis=-1, keepdims=True)
    gain = gain_ref[...].astype(jnp.float32).reshape(1, width)
    out_ref[:, :width] = (hidden * lax.rsqrt(meansq + 1e-06) * gain).astype(jnp.bfloat16)
    logits = logits_ref[...]
    raised = jnp.exp(logits - jnp.max(logits, axis=0, keepdims=True))
    weights = raised / jnp.sum(raised, axis=0, keepdims=True)
    ids = ids_ref[...]
    number = lax.broadcasted_iota(jnp.int32, (LANES, rows), 0)
    total = jnp.zeros((LANES, rows), jnp.float32)
    for choice in range(TOP):
        picked = (number % 16) == ids[choice : choice + 1, :]
        total = total + jnp.where(picked, weights[choice : choice + 1, :], 0.0)
    high = total.astype(jnp.bfloat16).astype(jnp.float32)
    middle = (total - high).astype(jnp.bfloat16).astype(jnp.float32)
    low = total - high - middle
    piece = number // 16
    parts = jnp.where(
        piece == 0, high, jnp.where(piece == 1, middle, jnp.where(piece == 2, low, 0.0))
    ).astype(jnp.bfloat16)
    first = lax.broadcasted_iota(jnp.int32, (LANES, LANES), 0)
    second = lax.broadcasted_iota(jnp.int32, (LANES, LANES), 1)
    identity = jnp.where(first == second, 1.0, 0.0).astype(jnp.bfloat16)
    out_ref[:, width:] = dot(parts, identity, ((0,), (0,))).astype(jnp.bfloat16)


def norm_message(hidden, gain, ids, logits):
    rows, width = hidden.shape
    return pl.pallas_call(
        norm_kernel,
        out_shape=jax.ShapeDtypeStruct((rows, width + LANES), jnp.bfloat16),
        cost_estimate=SMALL,
        name="norm_message",
    )(hidden, gain, ids.T, logits.T)


def rank_rows(match, rows):
    first = lax.broadcasted_iota(jnp.int32, (rows, rows), 0)
    second = lax.broadcasted_iota(jnp.int32, (rows, rows), 1)
    below = jnp.where(second < first, 1.0, 0.0).astype(jnp.bfloat16)
    return dot(below, match)


def attend_kernel(local, heads, lens_ref, q_mine, q_other, o_mine, o_other, cache, *refs):
    out_ref, keys, values, q_ref, score_ref, weight_ref, total_ref, k_sem, v_sem = refs[-9:]
    copies = []
    for i, head in enumerate(heads):
        at = pl.ds(head * HD, HD)
        copies.append(pltpu.make_async_copy(cache.at[local, :, at], keys.at[i], k_sem.at[i]))
        at = pl.ds((KVH + head) * HD, HD)
        copies.append(pltpu.make_async_copy(cache.at[local, :, at], values.at[i], v_sem.at[i]))
    for copy in copies:
        copy.start()
    number = lax.axis_index("fan") * 2 + local
    length = lens_ref[number]
    span = keys.shape[1]
    head_width = q_mine.shape[1] // KVH
    group = head_width // HD
    marks = 2 * KVH * HD
    prompts = jnp.concatenate([o_mine[:, marks:], o_other[:, marks:]], axis=0).astype(jnp.float32)
    chosen = prompts == number.astype(jnp.float32)
    rank = rank_rows(jnp.where(chosen, 1.0, 0.0).astype(jnp.bfloat16), LANES)
    lane = lax.broadcasted_iota(jnp.int32, (LANES, LANES), 1)
    here = chosen & (rank == lane.astype(jnp.float32))
    select = jnp.where(here, 1.0, 0.0).astype(jnp.bfloat16)

    def pick(mine, other, first, amount, rows):
        at = slice(first, first + amount)
        both = jnp.concatenate([mine[:, at], other[:, at]], axis=0)
        return dot(select[:, :rows], both, ((0,), (0,))).astype(jnp.bfloat16)

    factor = HD**-0.5 * LOG2E
    usable = lax.broadcasted_iota(jnp.int32, (1, span), 1) < length
    row = lax.broadcasted_iota(jnp.int32, (LANES, LANES), 0) % GROUP
    causal = ((row // STEPS == lane // STEPS) & (lane <= row))[:BAND]
    bands = group * GROUP // WIDE
    items = [(i, band) for i in range(len(heads)) for band in range(bands)]
    own = {}

    def products(step):
        i, band = items[step]
        head, slot = heads[i], step % 2
        if band == 0:
            queries = pick(q_mine, q_other, head * head_width, head_width, GROUP)
            for j in range(group):
                q_ref[i, j * GROUP : (j + 1) * GROUP] = queries[:, j * HD : (j + 1) * HD]
            own[i] = (
                pick(o_mine, o_other, head * HD, HD, LANES),
                pick(o_mine, o_other, (KVH + head) * HD, HD, LANES),
            )
            copies[2 * i].wait()
        queries = q_ref[i, band * WIDE : (band + 1) * WIDE]
        score_ref[slot, :, :span] = dot(queries, keys[i], ((1,), (1,)))
        score_ref[slot, :, span:] = dot(queries, own[i][0], ((1,), (1,)))

    products(0)
    for step, (i, band) in enumerate(items):
        slot = step % 2
        if step + 1 < len(items):
            products(step + 1)
        for base in range(0, WIDE, BAND):
            at = slice(base, base + BAND)
            scores = jnp.where(usable, score_ref[slot, at, :span], -1e30)
            mine = jnp.where(causal, score_ref[slot, at, span:], -1e30)
            highest = jnp.maximum(
                jnp.max(scores, axis=-1, keepdims=True), jnp.max(mine, axis=-1, keepdims=True)
            )
            raised = jnp.exp2((scores - highest) * factor)
            own_raised = jnp.exp2((mine - highest) * factor)
            total = jnp.sum(raised, axis=-1, keepdims=True) + jnp.sum(
                own_raised, axis=-1, keepdims=True
            )
            weight_ref[slot, at, :span] = raised.astype(jnp.bfloat16)
            weight_ref[slot, at, span:] = own_raised.astype(jnp.bfloat16)
            total_ref[slot, at] = jnp.broadcast_to(1.0 / total, (BAND, HD))
        if band == 0:
            copies[2 * i + 1].wait()
        mixed = dot(weight_ref[slot, :, :span], values[i])
        mixed = mixed + dot(weight_ref[slot, :, span:], own[i][1])
        mixed = (mixed * total_ref[slot]).astype(jnp.bfloat16)
        for j in range(WIDE // GROUP):
            first = i * head_width + (band * (WIDE // GROUP) + j) * HD
            out_ref[:, first : first + HD] = mixed[j * GROUP : (j + 1) * GROUP]


def attend(local, heads, lens, queries, own, cache, *after):
    rows, q_width = queries[0].shape
    span = cache.shape[1]
    head = q_width // KVH
    band = head // HD * GROUP
    some = len(heads)
    whole = pl.BlockSpec(memory_space=pltpu.VMEM)
    return pl.pallas_call(
        functools.partial(attend_kernel, local, heads),
        out_shape=jax.ShapeDtypeStruct((GROUP, some * head), jnp.bfloat16),
        in_specs=[pl.BlockSpec(memory_space=pltpu.SMEM)]
        + [whole] * 4
        + [pl.BlockSpec(memory_space=pltpu.HBM)]
        + [pl.BlockSpec(memory_space=pl.ANY)] * len(after),
        out_specs=whole,
        scratch_shapes=[
            pltpu.VMEM((some, span, HD), jnp.bfloat16),
            pltpu.VMEM((some, span, HD), jnp.bfloat16),
            pltpu.VMEM((some, band, HD), jnp.bfloat16),
            pltpu.VMEM((2, WIDE, span + LANES), jnp.float32),
            pltpu.VMEM((2, WIDE, span + LANES), jnp.bfloat16),
            pltpu.VMEM((2, WIDE, HD), jnp.float32),
            pltpu.SemaphoreType.DMA((some,)),
            pltpu.SemaphoreType.DMA((some,)),
        ],
        compiler_params=pltpu.CompilerParams(vmem_limit_bytes=ATTEND_VMEM * MIB),
        cost_estimate=SMALL,
        name="attend",
    )(lens, *queries, *own, cache, *after)


def place_kernel(halves, o_mine, *refs):
    out_ref = refs[-1]
    rows = o_mine.shape[0]
    lane = lax.broadcasted_iota(jnp.int32, (rows, LANES), 1)
    part = lane // GROUP
    side, local = part // 2, part % 2
    fan = lax.axis_index("fan")
    number = jnp.where(side == 0, fan, 1 - fan) * 2 + local
    prompts = o_mine[:, 2 * KVH * HD :].astype(jnp.float32)
    chosen = prompts == number.astype(jnp.float32)
    match = jnp.where(chosen, 1.0, 0.0).astype(jnp.bfloat16)
    rank = rank_rows(match, rows)
    ahead = GROUP - dot(jnp.ones((rows, rows), jnp.bfloat16), match)
    rank = rank + jnp.where(side == 1, ahead, 0.0)
    here = chosen & (rank == (lane % GROUP).astype(jnp.float32))
    place = jnp.where(here, 1.0, 0.0).astype(jnp.bfloat16)
    width = refs[0].shape[1]
    for half in range(halves):
        stacked = jnp.concatenate([ref[...] for ref in refs[4 * half : 4 * half + 4]], axis=0)
        result = dot(place, stacked).astype(jnp.bfloat16)
        at = slice(half * width, (half + 1) * width)
        out_ref[:, :, at] = result.reshape(rows // STEPS, STEPS, width)


def place_context(own, contexts, out_shape):
    whole = pl.BlockSpec(memory_space=pltpu.VMEM)
    return pl.pallas_call(
        functools.partial(place_kernel, len(contexts) // 4),
        out_shape=out_shape,
        in_specs=[whole] * (1 + len(contexts)),
        out_specs=whole,
        compiler_params=pltpu.CompilerParams(vmem_limit_bytes=12 * MIB),
        cost_estimate=SMALL,
        name="place_context",
    )(own, *contexts)


def expert_kernel(count, at_row, tokens, *refs):
    xs, (gate, up, down) = refs[:count], refs[count : count + 3]
    keep, send, other = refs[-8:-5]
    x, opened, raised, units, x_sem = refs[-5:]
    width, hidden = gate.shape
    copies = []
    for i in range(count):
        copies.append(
            pltpu.make_async_copy(
                xs[i].at[pl.ds(at_row, tokens)], x.at[pl.ds(i * tokens, tokens)], x_sem.at[i]
            )
        )
    for copy in copies:
        copy.start()
    for copy in copies:
        copy.wait()
    for i in range(width // DEEP):
        at = slice(i * DEEP, (i + 1) * DEEP)
        product = dot(x[:, at], gate[at])
        opened[...] = product if i == 0 else opened[...] + product
        product = dot(x[:, at], up[at])
        raised[...] = product if i == 0 else raised[...] + product
    through = opened[...]
    units[...] = (through * jax.nn.sigmoid(through) * raised[...]).astype(jnp.bfloat16)
    marks = x[:, width:].astype(jnp.float32)
    lane = lax.broadcasted_iota(jnp.int32, marks.shape, 1)
    mine = (lane % 16 == lax.axis_index("ep")) & (lane < 48)
    weight = jnp.sum(jnp.where(mine, marks, 0.0), axis=1, keepdims=True)
    half = count // 2 * tokens
    for i in range(width // DEEP):
        at = slice(i * DEEP, (i + 1) * DEEP)
        result = (dot(units[...], down[:, at]) * weight).astype(jnp.bfloat16)
        keep[:, at] = result[: half // 2]
        send[:, at] = result[half // 2 : half]
        other[:, at] = result[half:]


def expert_chunk(pieces, at_row, tokens, gate, up, down, *after):
    count = len(pieces)
    message = pieces[0].shape[1]
    width, hidden = gate.shape
    rows = count * tokens
    whole = pl.BlockSpec(memory_space=pltpu.VMEM)
    return pl.pallas_call(
        functools.partial(expert_kernel, count, at_row, tokens),
        out_shape=(
            jax.ShapeDtypeStruct((rows // 4, width), jnp.bfloat16),
            jax.ShapeDtypeStruct((rows // 4, width), jnp.bfloat16),
            jax.ShapeDtypeStruct((rows // 2, width), jnp.bfloat16),
        ),
        in_specs=[pl.BlockSpec(memory_space=pl.ANY)] * count
        + [whole] * 3
        + [pl.BlockSpec(memory_space=pl.ANY)] * len(after),
        out_specs=(whole, whole, whole),
        scratch_shapes=[
            pltpu.VMEM((rows, message), jnp.bfloat16),
            pltpu.VMEM((rows, hidden), jnp.float32),
            pltpu.VMEM((rows, hidden), jnp.float32),
            pltpu.VMEM((rows, hidden), jnp.bfloat16),
            pltpu.SemaphoreType.DMA((count,)),
        ],
        compiler_params=pltpu.CompilerParams(vmem_limit_bytes=EXPERT_VMEM * MIB),
        cost_estimate=SMALL,
        name="expert_chunk",
    )(*pieces, gate, up, down, *after)


def on_device(
    queries,
    new_kv,
    prompt_kv,
    prompt_lens,
    sample_prompt,
    hidden,
    norm_gain,
    route_ids,
    route_logits,
    w_gate,
    w_up,
    w_down,
):
    chips = lax.axis_size("ep")
    count, _, q_width = queries.shape
    rows = count * STEPS

    def swap(value, by_fan):
        pairs = [
            ((e * 2 + f), ((e ^ by_fan[f]) * 2 + f)) for e in range(chips) for f in range(2)
        ]
        return lax.ppermute(value, ("ep", "fan"), pairs)

    def near(value):
        return swap(value, (1, 2))

    def cross(value):
        return swap(value, (2, 1))

    def far(value, layer):
        return swap(value, (4 * layer, 4 * layer))

    def beside(value):
        return lax.ppermute(value, "fan", [(0, 1), (1, 0)])

    gate, up, down = w_gate[0], w_up[0], w_down[0]
    tokens = hidden.shape[0]
    sync = lax.optimization_barrier
    token = norm_message(hidden, norm_gain, route_ids, route_logits)
    token, queries, new_kv = sync((token, queries, new_kv))
    marks = jnp.broadcast_to(sample_prompt.astype(jnp.bfloat16)[:, None, None], (count, STEPS, LANES))
    q_mine = queries.reshape(rows, q_width)
    own_mine = jnp.concatenate([new_kv, marks], axis=2).reshape(rows, -1)
    q_both = (q_mine, beside(q_mine))
    own_both = (own_mine, beside(own_mine))

    def attend_half(local, half, *after):
        heads = tuple(range(half * KVH // 2, (half + 1) * KVH // 2))
        return attend(local, heads, prompt_lens, q_both, own_both, prompt_kv, *after)

    def expert(pieces, at_row, *after):
        return expert_chunk(pieces, at_row, tokens, gate, up, down, *after)

    def with_fan(pieces):
        return pieces + [beside(piece) for piece in pieces]

    def sum_cores(result, back):
        send = result[1]
        half = send.shape[0]
        return (send.astype(jnp.float32) + back[half:].astype(jnp.float32)).astype(jnp.bfloat16)

    def sum_cross(result, back, turned):
        single = tokens

        def total(at):
            mine = result[0][at].astype(jnp.float32) + back[at].astype(jnp.float32)
            return mine + turned[at].astype(jnp.float32)

        return total(slice(0, single)), total(slice(single, 2 * single)).astype(jnp.bfloat16)

    def widen(value):
        return value.astype(jnp.float32)

    def narrow(value):
        return value.astype(jnp.bfloat16)

    level_2, level_1 = far(token, 2), far(token, 1)
    first_0, cross_0 = near(token), cross(token)
    pair = jnp.concatenate([level_2, level_1], axis=0)
    level_3 = far(level_2, 1)
    third_0 = cross(first_0)
    context_0a = attend_half(0, 0, pair, first_0, cross_0)
    context_0a, third_0 = sync((context_0a, third_0))
    pieces_0 = with_fan([token, first_0, cross_0, third_0])
    context_0b = attend_half(0, 1, context_0a)
    context_0b, level_3, first_p, cross_p, *pieces_0 = sync(
        (context_0b, level_3, near(pair), cross(pair), *pieces_0)
    )
    third_p = cross(first_p)
    first_3, cross_3 = near(level_3), cross(level_3)
    result_0 = expert(pieces_0, 0, context_0b, first_p)

    third_p, first_3, cross_3, result_0 = sync((third_p, first_3, cross_3, result_0))
    back_0 = beside(result_0[2])
    pieces_p = with_fan([pair, first_p, cross_p, third_p])
    third_3 = cross(first_3)
    context_1a = attend_half(1, 0, third_p, first_3)
    context_1a, back_0, third_3, *pieces_p = sync((context_1a, back_0, third_3, *pieces_p))
    there_0 = sum_cores(result_0, back_0)
    pieces_3 = with_fan([level_3, first_3, cross_3, third_3])
    result_2 = expert(pieces_p, 0, context_1a, there_0)

    turned_0, result_2, *pieces_3 = sync((cross(there_0), result_2, *pieces_3))
    back_2 = beside(result_2[2])
    held_0, passed_0 = sum_cross(result_0, back_0, turned_0)
    there_2 = sum_cores(result_2, back_2)
    result_3 = expert(pieces_3, 0, there_2, passed_0)

    ended_0, turned_2, result_3 = sync((near(passed_0), cross(there_2), result_3))
    back_3 = beside(result_3[2])
    held_2, passed_2 = sum_cross(result_2, back_2, turned_2)
    context_1b = attend_half(1, 1, passed_2)
    context_1b, back_3 = sync((context_1b, back_3))
    there_3 = sum_cores(result_3, back_3)
    result_1 = expert(pieces_p, tokens, there_3, passed_2)

    contexts = [context_0a, context_0b, context_1a, context_1b]
    sent = [beside(value) for value in contexts]
    ended_2, turned_3, result_1, sent = sync((near(passed_2), cross(there_3), result_1, sent))
    back_1 = beside(result_1[2])
    held_3, passed_3 = sum_cross(result_3, back_3, turned_3)
    ordered = [contexts[0], contexts[2], sent[0], sent[2], contexts[1], contexts[3], sent[1], sent[3]]
    far_2 = far(narrow(held_2 + widen(ended_2)), 2)
    there_1 = sum_cores(result_1, back_1)
    own_late, _ = sync((own_mine, there_1))
    context = place_context(own_late, ordered, jax.ShapeDtypeStruct(queries.shape, jnp.bfloat16))
    context, ended_3 = sync((context, near(passed_3)))
    far_3 = far(narrow(held_3 + widen(ended_3)), 3)
    held_1, passed_1 = sum_cross(result_1, back_1, cross(there_1))
    far_1 = far(narrow(held_1 + widen(near(passed_1))), 1)
    total = held_0 + widen(ended_0) + widen(far_1)
    expert_out = narrow(total + widen(far_2) + widen(far_3))
    return (context, expert_out)


def solution(mesh):
    placed = (
        P(("parts", "ep", "fan"), None, None),
        P(("parts", "ep", "fan"), None, None),
        P(("parts", "ep", "fan"), None, None),
        P(("parts", "ep")),
        P(("parts", "ep", "fan")),
        P(("parts", "ep", "fan"), None),
        P(),
        P(("parts", "ep", "fan"), None),
        P(("parts", "ep", "fan"), None),
        P("ep", None, "fan"),
        P("ep", None, "fan"),
        P("ep", "fan", None),
    )
    return jax.shard_map(
        on_device,
        mesh=mesh,
        in_specs=placed,
        out_specs=(P(("parts", "ep", "fan"), None, None), P(("parts", "ep", "fan"), None)),
        check_vma=False,
    )
```

```python
import functools

import jax
import jax.numpy as jnp
from jax import lax
from jax.experimental import pallas as pl
from jax.experimental.pallas import tpu as pltpu
from jax.sharding import PartitionSpec as P

KVH = 4
HD = 128
STEPS = 2
SAMP = 16
TOP = 8
GROUP = SAMP * STEPS
LANES = 128
BAND = 64
WIDE = 256
DEEP = 1024
EXPERT_VMEM = 12
ATTEND_VMEM = 16
LOG2E = 1.4426950408889634
MIB = 1 << 20


def dot(a, b, contract=((1,), (0,))):
    return lax.dot_general(a, b, (contract, ((), ())), preferred_element_type=jnp.float32)


SMALL = pl.CostEstimate(flops=1 << 20, bytes_accessed=1 << 14, transcendentals=0)


LARGE = pl.CostEstimate(flops=20 << 30, bytes_accessed=1 << 20, transcendentals=0)


def norm_kernel(hidden_ref, gain_ref, ids_ref, logits_ref, out_ref):
    rows, width = hidden_ref.shape
    hidden = hidden_ref[...].astype(jnp.float32)
    meansq = jnp.mean(hidden * hidden, axis=-1, keepdims=True)
    gain = gain_ref[...].astype(jnp.float32).reshape(1, width)
    out_ref[:, :width] = (hidden * lax.rsqrt(meansq + 1e-06) * gain).astype(jnp.bfloat16)
    logits = logits_ref[...]
    raised = jnp.exp(logits - jnp.max(logits, axis=0, keepdims=True))
    weights = raised / jnp.sum(raised, axis=0, keepdims=True)
    ids = ids_ref[...]
    number = lax.broadcasted_iota(jnp.int32, (LANES, rows), 0)
    total = jnp.zeros((LANES, rows), jnp.float32)
    for choice in range(TOP):
        picked = (number % 16) == ids[choice : choice + 1, :]
        total = total + jnp.where(picked, weights[choice : choice + 1, :], 0.0)
    high = total.astype(jnp.bfloat16).astype(jnp.float32)
    middle = (total - high).astype(jnp.bfloat16).astype(jnp.float32)
    low = total - high - middle
    piece = number // 16
    parts = jnp.where(
        piece == 0, high, jnp.where(piece == 1, middle, jnp.where(piece == 2, low, 0.0))
    ).astype(jnp.bfloat16)
    first = lax.broadcasted_iota(jnp.int32, (LANES, LANES), 0)
    second = lax.broadcasted_iota(jnp.int32, (LANES, LANES), 1)
    identity = jnp.where(first == second, 1.0, 0.0).astype(jnp.bfloat16)
    out_ref[:, width:] = dot(parts, identity, ((0,), (0,))).astype(jnp.bfloat16)


def norm_message(hidden, gain, ids, logits):
    rows, width = hidden.shape
    return pl.pallas_call(
        norm_kernel,
        out_shape=jax.ShapeDtypeStruct((rows, width + LANES), jnp.bfloat16),
        cost_estimate=LARGE,
        name="norm_message",
    )(hidden, gain, ids.T, logits.T)


def stack_kernel(top, bottom, out, sem):
    rows = top.shape[0]
    upper = pltpu.make_async_copy(top, out.at[pl.ds(0, rows)], sem.at[0])
    lower = pltpu.make_async_copy(bottom, out.at[pl.ds(rows, rows)], sem.at[1])
    upper.start()
    lower.start()
    upper.wait()
    lower.wait()


def stack(top, bottom):
    rows, width = top.shape
    anywhere = pl.BlockSpec(memory_space=pl.ANY)
    return pl.pallas_call(
        stack_kernel,
        out_shape=jax.ShapeDtypeStruct((2 * rows, width), top.dtype),
        in_specs=[anywhere, anywhere],
        out_specs=anywhere,
        scratch_shapes=[pltpu.SemaphoreType.DMA((2,))],
        cost_estimate=SMALL,
        name="stack",
    )(top, bottom)


def rank_rows(match, rows):
    first = lax.broadcasted_iota(jnp.int32, (rows, rows), 0)
    second = lax.broadcasted_iota(jnp.int32, (rows, rows), 1)
    below = jnp.where(second < first, 1.0, 0.0).astype(jnp.bfloat16)
    return dot(below, match)


def attend_kernel(local, heads, lens_ref, q_mine, q_other, o_mine, o_other, cache, *refs):
    out_ref, keys, values, q_ref, score_ref, weight_ref, total_ref, k_sem, v_sem = refs[-9:]
    copies = []
    for i, head in enumerate(heads):
        at = pl.ds(head * HD, HD)
        copies.append(pltpu.make_async_copy(cache.at[local, :, at], keys.at[i], k_sem.at[i]))
        at = pl.ds((KVH + head) * HD, HD)
        copies.append(pltpu.make_async_copy(cache.at[local, :, at], values.at[i], v_sem.at[i]))
    for copy in copies:
        copy.start()
    number = lax.axis_index("fan") * 2 + local
    length = lens_ref[number]
    span = keys.shape[1]
    head_width = q_mine.shape[1] // KVH
    group = head_width // HD
    marks = 2 * KVH * HD
    prompts = jnp.concatenate([o_mine[:, marks:], o_other[:, marks:]], axis=0).astype(jnp.float32)
    chosen = prompts == number.astype(jnp.float32)
    rank = rank_rows(jnp.where(chosen, 1.0, 0.0).astype(jnp.bfloat16), LANES)
    lane = lax.broadcasted_iota(jnp.int32, (LANES, LANES), 1)
    here = chosen & (rank == lane.astype(jnp.float32))
    select = jnp.where(here, 1.0, 0.0).astype(jnp.bfloat16)

    def pick(mine, other, first, amount, rows):
        at = slice(first, first + amount)
        both = jnp.concatenate([mine[:, at], other[:, at]], axis=0)
        return dot(select[:, :rows], both, ((0,), (0,))).astype(jnp.bfloat16)

    factor = HD**-0.5 * LOG2E
    usable = lax.broadcasted_iota(jnp.int32, (1, span), 1) < length
    row = lax.broadcasted_iota(jnp.int32, (LANES, LANES), 0) % GROUP
    causal = ((row // STEPS == lane // STEPS) & (lane <= row))[:BAND]
    bands = group * GROUP // WIDE
    items = [(i, band) for i in range(len(heads)) for band in range(bands)]
    own = {}

    def products(step):
        i, band = items[step]
        head, slot = heads[i], step % 2
        if band == 0:
            queries = pick(q_mine, q_other, head * head_width, head_width, GROUP)
            for j in range(group):
                q_ref[i, j * GROUP : (j + 1) * GROUP] = queries[:, j * HD : (j + 1) * HD]
            own[i] = (
                pick(o_mine, o_other, head * HD, HD, LANES),
                pick(o_mine, o_other, (KVH + head) * HD, HD, LANES),
            )
            copies[2 * i].wait()
        queries = q_ref[i, band * WIDE : (band + 1) * WIDE]
        score_ref[slot, :, :span] = dot(queries, keys[i], ((1,), (1,)))
        score_ref[slot, :, span:] = dot(queries, own[i][0], ((1,), (1,)))

    products(0)
    for step, (i, band) in enumerate(items):
        slot = step % 2
        if step + 1 < len(items):
            products(step + 1)
        for base in range(0, WIDE, BAND):
            at = slice(base, base + BAND)
            scores = jnp.where(usable, score_ref[slot, at, :span], -1e30)
            mine = jnp.where(causal, score_ref[slot, at, span:], -1e30)
            highest = jnp.maximum(
                jnp.max(scores, axis=-1, keepdims=True), jnp.max(mine, axis=-1, keepdims=True)
            )
            raised = jnp.exp2((scores - highest) * factor)
            own_raised = jnp.exp2((mine - highest) * factor)
            total = jnp.sum(raised, axis=-1, keepdims=True) + jnp.sum(
                own_raised, axis=-1, keepdims=True
            )
            weight_ref[slot, at, :span] = raised.astype(jnp.bfloat16)
            weight_ref[slot, at, span:] = own_raised.astype(jnp.bfloat16)
            total_ref[slot, at] = jnp.broadcast_to(1.0 / total, (BAND, HD))
        if band == 0:
            copies[2 * i + 1].wait()
        mixed = dot(weight_ref[slot, :, :span], values[i])
        mixed = mixed + dot(weight_ref[slot, :, span:], own[i][1])
        mixed = (mixed * total_ref[slot]).astype(jnp.bfloat16)
        for j in range(WIDE // GROUP):
            first = i * head_width + (band * (WIDE // GROUP) + j) * HD
            out_ref[:, first : first + HD] = mixed[j * GROUP : (j + 1) * GROUP]


def attend(local, heads, lens, queries, own, cache, *after):
    rows, q_width = queries[0].shape
    span = cache.shape[1]
    head = q_width // KVH
    band = head // HD * GROUP
    some = len(heads)
    whole = pl.BlockSpec(memory_space=pltpu.VMEM)
    return pl.pallas_call(
        functools.partial(attend_kernel, local, heads),
        out_shape=jax.ShapeDtypeStruct((GROUP, some * head), jnp.bfloat16),
        in_specs=[pl.BlockSpec(memory_space=pltpu.SMEM)]
        + [whole] * 4
        + [pl.BlockSpec(memory_space=pltpu.HBM)]
        + [pl.BlockSpec(memory_space=pl.ANY)] * len(after),
        out_specs=whole,
        scratch_shapes=[
            pltpu.VMEM((some, span, HD), jnp.bfloat16),
            pltpu.VMEM((some, span, HD), jnp.bfloat16),
            pltpu.VMEM((some, band, HD), jnp.bfloat16),
            pltpu.VMEM((2, WIDE, span + LANES), jnp.float32),
            pltpu.VMEM((2, WIDE, span + LANES), jnp.bfloat16),
            pltpu.VMEM((2, WIDE, HD), jnp.float32),
            pltpu.SemaphoreType.DMA((some,)),
            pltpu.SemaphoreType.DMA((some,)),
        ],
        compiler_params=pltpu.CompilerParams(vmem_limit_bytes=ATTEND_VMEM * MIB),
        cost_estimate=SMALL,
        name="attend",
    )(lens, *queries, *own, cache, *after)


def place_kernel(halves, o_mine, *refs):
    out_ref = refs[-1]
    rows = o_mine.shape[0]
    lane = lax.broadcasted_iota(jnp.int32, (rows, LANES), 1)
    part = lane // GROUP
    side, local = part // 2, part % 2
    fan = lax.axis_index("fan")
    number = jnp.where(side == 0, fan, 1 - fan) * 2 + local
    prompts = o_mine[:, 2 * KVH * HD :].astype(jnp.float32)
    chosen = prompts == number.astype(jnp.float32)
    match = jnp.where(chosen, 1.0, 0.0).astype(jnp.bfloat16)
    rank = rank_rows(match, rows)
    ahead = GROUP - dot(jnp.ones((rows, rows), jnp.bfloat16), match)
    rank = rank + jnp.where(side == 1, ahead, 0.0)
    here = chosen & (rank == (lane % GROUP).astype(jnp.float32))
    place = jnp.where(here, 1.0, 0.0).astype(jnp.bfloat16)
    width = refs[0].shape[1]
    for half in range(halves):
        stacked = jnp.concatenate([ref[...] for ref in refs[4 * half : 4 * half + 4]], axis=0)
        result = dot(place, stacked).astype(jnp.bfloat16)
        at = slice(half * width, (half + 1) * width)
        out_ref[:, :, at] = result.reshape(rows // STEPS, STEPS, width)


def place_context(own, contexts, out_shape):
    whole = pl.BlockSpec(memory_space=pltpu.VMEM)
    return pl.pallas_call(
        functools.partial(place_kernel, len(contexts) // 4),
        out_shape=out_shape,
        in_specs=[whole] * (1 + len(contexts)),
        out_specs=whole,
        compiler_params=pltpu.CompilerParams(vmem_limit_bytes=12 * MIB),
        cost_estimate=SMALL,
        name="place_context",
    )(own, *contexts)


def expert_kernel(count, at_row, tokens, *refs):
    xs, (gate, up, down) = refs[:count], refs[count : count + 3]
    keep, send, other = refs[-8:-5]
    x, opened, raised, units, x_sem = refs[-5:]
    width, hidden = gate.shape
    copies = []
    for i in range(count):
        copies.append(
            pltpu.make_async_copy(
                xs[i].at[pl.ds(at_row, tokens)], x.at[pl.ds(i * tokens, tokens)], x_sem.at[i]
            )
        )
    for copy in copies:
        copy.start()
    for copy in copies:
        copy.wait()
    for i in range(width // DEEP):
        at = slice(i * DEEP, (i + 1) * DEEP)
        product = dot(x[:, at], gate[at])
        opened[...] = product if i == 0 else opened[...] + product
        product = dot(x[:, at], up[at])
        raised[...] = product if i == 0 else raised[...] + product
    through = opened[...]
    units[...] = (through * jax.nn.sigmoid(through) * raised[...]).astype(jnp.bfloat16)
    marks = x[:, width:].astype(jnp.float32)
    lane = lax.broadcasted_iota(jnp.int32, marks.shape, 1)
    mine = (lane % 16 == lax.axis_index("ep")) & (lane < 48)
    weight = jnp.sum(jnp.where(mine, marks, 0.0), axis=1, keepdims=True)
    half = count // 2 * tokens
    for i in range(width // DEEP):
        at = slice(i * DEEP, (i + 1) * DEEP)
        result = (dot(units[...], down[:, at]) * weight).astype(jnp.bfloat16)
        keep[:, at] = result[: half // 2]
        send[:, at] = result[half // 2 : half]
        other[:, at] = result[half:]


def expert_chunk(pieces, at_row, tokens, gate, up, down, *after):
    count = len(pieces)
    message = pieces[0].shape[1]
    width, hidden = gate.shape
    rows = count * tokens
    whole = pl.BlockSpec(memory_space=pltpu.VMEM)
    return pl.pallas_call(
        functools.partial(expert_kernel, count, at_row, tokens),
        out_shape=(
            jax.ShapeDtypeStruct((rows // 4, width), jnp.bfloat16),
            jax.ShapeDtypeStruct((rows // 4, width), jnp.bfloat16),
            jax.ShapeDtypeStruct((rows // 2, width), jnp.bfloat16),
        ),
        in_specs=[pl.BlockSpec(memory_space=pl.ANY)] * count
        + [whole] * 3
        + [pl.BlockSpec(memory_space=pl.ANY)] * len(after),
        out_specs=(whole, whole, whole),
        scratch_shapes=[
            pltpu.VMEM((rows, message), jnp.bfloat16),
            pltpu.VMEM((rows, hidden), jnp.float32),
            pltpu.VMEM((rows, hidden), jnp.float32),
            pltpu.VMEM((rows, hidden), jnp.bfloat16),
            pltpu.SemaphoreType.DMA((count,)),
        ],
        compiler_params=pltpu.CompilerParams(vmem_limit_bytes=EXPERT_VMEM * MIB),
        cost_estimate=SMALL,
        name="expert_chunk",
    )(*pieces, gate, up, down, *after)


def on_device(
    queries,
    new_kv,
    prompt_kv,
    prompt_lens,
    sample_prompt,
    hidden,
    norm_gain,
    route_ids,
    route_logits,
    w_gate,
    w_up,
    w_down,
):
    chips = lax.axis_size("ep")
    count, _, q_width = queries.shape
    rows = count * STEPS

    def swap(value, by_fan):
        pairs = [
            ((e * 2 + f), ((e ^ by_fan[f]) * 2 + f)) for e in range(chips) for f in range(2)
        ]
        return lax.ppermute(value, ("ep", "fan"), pairs)

    def near(value):
        return swap(value, (1, 2))

    def cross(value):
        return swap(value, (2, 1))

    def far(value, layer):
        return swap(value, (4 * layer, 4 * layer))

    def beside(value):
        return lax.ppermute(value, "fan", [(0, 1), (1, 0)])

    gate, up, down = w_gate[0], w_up[0], w_down[0]
    tokens = hidden.shape[0]
    sync = lax.optimization_barrier
    token = norm_message(hidden, norm_gain, route_ids, route_logits)
    token, queries, new_kv = sync((token, queries, new_kv))
    marks = jnp.broadcast_to(sample_prompt.astype(jnp.bfloat16)[:, None, None], (count, STEPS, LANES))
    q_mine = queries.reshape(rows, q_width)
    own_mine = jnp.concatenate([new_kv, marks], axis=2).reshape(rows, -1)
    q_both = (q_mine, beside(q_mine))
    own_both = (own_mine, beside(own_mine))

    def attend_half(local, half, *after):
        heads = tuple(range(half * KVH // 2, (half + 1) * KVH // 2))
        return attend(local, heads, prompt_lens, q_both, own_both, prompt_kv, *after)

    def expert(pieces, at_row, *after):
        return expert_chunk(pieces, at_row, tokens, gate, up, down, *after)

    def with_fan(pieces):
        return pieces + [beside(piece) for piece in pieces]

    def sum_cores(result, back):
        send = result[1]
        half = send.shape[0]
        return (send.astype(jnp.float32) + back[half:].astype(jnp.float32)).astype(jnp.bfloat16)

    def sum_cross(result, back, turned):
        single = tokens

        def total(at):
            mine = result[0][at].astype(jnp.float32) + back[at].astype(jnp.float32)
            return mine + turned[at].astype(jnp.float32)

        return total(slice(0, single)), total(slice(single, 2 * single)).astype(jnp.bfloat16)

    def widen(value):
        return value.astype(jnp.float32)

    def narrow(value):
        return value.astype(jnp.bfloat16)

    level_2, level_1 = far(token, 2), far(token, 1)
    first_0, cross_0 = near(token), cross(token)
    third_0 = cross(first_0)
    pair = stack(level_2, level_1)
    level_3 = far(level_2, 1)
    context_0a = attend_half(0, 0, pair, first_0, cross_0)
    context_0a, third_0, level_3 = sync((context_0a, third_0, level_3))
    pieces_0 = with_fan([token, first_0, cross_0, third_0])
    context_0b = attend_half(0, 1, context_0a)
    context_0b, first_p, cross_p, *pieces_0 = sync(
        (context_0b, near(pair), cross(pair), *pieces_0)
    )
    third_p = cross(first_p)
    first_3, cross_3 = near(level_3), cross(level_3)
    fans_p = [beside(value) for value in (pair, first_p, cross_p)]
    result_0 = expert(pieces_0, 0, context_0b, first_p)

    third_p, result_0, *fans_p = sync((third_p, result_0, *fans_p))
    back_0 = beside(result_0[2])
    pieces_p = [pair, first_p, cross_p, third_p, *fans_p, beside(third_p)]
    result_2 = expert(pieces_p, 0, result_0[0])

    first_3, cross_3, back_0, result_2 = sync((first_3, cross_3, back_0, result_2))
    back_2 = beside(result_2[2])
    third_3 = cross(first_3)
    fans_3 = [beside(value) for value in (level_3, first_3, cross_3)]
    context_1a = attend_half(1, 0, first_3, cross_3)
    context_1a, third_3, back_2, *fans_3 = sync((context_1a, third_3, back_2, *fans_3))
    pieces_3 = [level_3, first_3, cross_3, third_3, *fans_3, beside(third_3)]
    there_2 = sum_cores(result_2, back_2)
    result_3 = expert(pieces_3, 0, there_2, context_1a)

    turned_2, result_3 = sync((cross(there_2), result_3))
    back_3 = beside(result_3[2])
    held_2, passed_2 = sum_cross(result_2, back_2, turned_2)
    there_3 = sum_cores(result_3, back_3)
    there_0 = sum_cores(result_0, back_0)
    total_2 = narrow(held_2 + widen(near(passed_2)))
    far_2 = far(total_2, 2)
    result_1 = expert(pieces_p, tokens, there_3, there_0, total_2)

    contexts = [context_0a, context_0b, context_1a]
    sent = [beside(value) for value in contexts]
    turned_0, turned_3, result_1, *sent = sync((cross(there_0), cross(there_3), result_1, *sent))
    back_1 = beside(result_1[2])
    held_3, passed_3 = sum_cross(result_3, back_3, turned_3)
    held_0, passed_0 = sum_cross(result_0, back_0, turned_0)
    there_1 = sum_cores(result_1, back_1)
    total_3 = narrow(held_3 + widen(near(passed_3)))
    far_3 = far(total_3, 3)
    held_1, passed_1 = sum_cross(result_1, back_1, cross(there_1))
    context_1b = attend_half(1, 1, total_3, passed_1)

    far_1 = far(narrow(held_1 + widen(near(passed_1))), 1)
    contexts, sent = contexts + [context_1b], sent + [beside(context_1b)]
    ordered = [contexts[0], contexts[2], sent[0], sent[2], contexts[1], contexts[3], sent[1], sent[3]]
    own_late, far_2 = sync((own_mine, far_2))
    context = place_context(own_late, ordered, jax.ShapeDtypeStruct(queries.shape, jnp.bfloat16))
    context, far_1, far_3 = sync((context, far_1, far_3))
    total = held_0 + widen(near(passed_0)) + widen(far_1)
    expert_out = narrow(total + widen(far_2) + widen(far_3))
    return (context, expert_out)


def solution(mesh):
    placed = (
        P(("parts", "ep", "fan"), None, None),
        P(("parts", "ep", "fan"), None, None),
        P(("parts", "ep", "fan"), None, None),
        P(("parts", "ep")),
        P(("parts", "ep", "fan")),
        P(("parts", "ep", "fan"), None),
        P(),
        P(("parts", "ep", "fan"), None),
        P(("parts", "ep", "fan"), None),
        P("ep", None, "fan"),
        P("ep", None, "fan"),
        P("ep", "fan", None),
    )
    return jax.shard_map(
        on_device,
        mesh=mesh,
        in_specs=placed,
        out_specs=(P(("parts", "ep", "fan"), None, None), P(("parts", "ep", "fan"), None)),
        check_vma=False,
    )
```

```python
import functools

import jax
import jax.numpy as jnp
from jax import lax
from jax.experimental import pallas as pl
from jax.experimental.pallas import tpu as pltpu
from jax.sharding import PartitionSpec as P

KVH = 4
HD = 128
STEPS = 2
SAMP = 16
TOP = 8
GROUP = SAMP * STEPS
LANES = 128
BAND = 64
WIDE = 256
DEEP = 1024
EXPERT_VMEM = 12
ATTEND_VMEM = 16
LOG2E = 1.4426950408889634
MIB = 1 << 20


def dot(a, b, contract=((1,), (0,))):
    return lax.dot_general(a, b, (contract, ((), ())), preferred_element_type=jnp.float32)


SMALL = pl.CostEstimate(flops=1 << 20, bytes_accessed=1 << 14, transcendentals=0)


def norm_kernel(hidden_ref, gain_ref, ids_ref, logits_ref, out_ref):
    rows, width = hidden_ref.shape
    hidden = hidden_ref[...].astype(jnp.float32)
    meansq = jnp.mean(hidden * hidden, axis=-1, keepdims=True)
    gain = gain_ref[...].astype(jnp.float32).reshape(1, width)
    out_ref[:, :width] = (hidden * lax.rsqrt(meansq + 1e-06) * gain).astype(jnp.bfloat16)
    logits = logits_ref[...]
    raised = jnp.exp(logits - jnp.max(logits, axis=0, keepdims=True))
    weights = raised / jnp.sum(raised, axis=0, keepdims=True)
    ids = ids_ref[...]
    number = lax.broadcasted_iota(jnp.int32, (LANES, rows), 0)
    total = jnp.zeros((LANES, rows), jnp.float32)
    for choice in range(TOP):
        picked = (number % 16) == ids[choice : choice + 1, :]
        total = total + jnp.where(picked, weights[choice : choice + 1, :], 0.0)
    high = total.astype(jnp.bfloat16).astype(jnp.float32)
    middle = (total - high).astype(jnp.bfloat16).astype(jnp.float32)
    low = total - high - middle
    piece = number // 16
    parts = jnp.where(
        piece == 0, high, jnp.where(piece == 1, middle, jnp.where(piece == 2, low, 0.0))
    ).astype(jnp.bfloat16)
    first = lax.broadcasted_iota(jnp.int32, (LANES, LANES), 0)
    second = lax.broadcasted_iota(jnp.int32, (LANES, LANES), 1)
    identity = jnp.where(first == second, 1.0, 0.0).astype(jnp.bfloat16)
    out_ref[:, width:] = dot(parts, identity, ((0,), (0,))).astype(jnp.bfloat16)


def norm_message(hidden, gain, ids, logits):
    rows, width = hidden.shape
    return pl.pallas_call(
        norm_kernel,
        out_shape=jax.ShapeDtypeStruct((rows, width + LANES), jnp.bfloat16),
        cost_estimate=SMALL,
        name="norm_message",
    )(hidden, gain, ids.T, logits.T)


def stack_kernel(top, bottom, out):
    rows = top.shape[0]
    out[:rows] = top[...]
    out[rows:] = bottom[...]


def stack(top, bottom):
    rows, width = top.shape
    whole = pl.BlockSpec(memory_space=pltpu.VMEM)
    return pl.pallas_call(
        stack_kernel,
        out_shape=jax.ShapeDtypeStruct((2 * rows, width), top.dtype),
        in_specs=[whole, whole],
        out_specs=whole,
        compiler_params=pltpu.CompilerParams(vmem_limit_bytes=8 * MIB),
        cost_estimate=SMALL,
        name="stack",
    )(top, bottom)


def touch_kernel(lens, *refs):
    out = refs[-1]
    for i in range(lens.shape[0]):
        out[i] = lens[i]


def touch(lens, *arrays):
    scalars = pl.BlockSpec(memory_space=pltpu.SMEM)
    return pl.pallas_call(
        touch_kernel,
        out_shape=jax.ShapeDtypeStruct(lens.shape, lens.dtype),
        in_specs=[scalars] + [pl.BlockSpec(memory_space=pl.ANY)] * len(arrays),
        out_specs=scalars,
        cost_estimate=SMALL,
        name="touch",
    )(lens, *arrays)


def rank_rows(match, rows):
    first = lax.broadcasted_iota(jnp.int32, (rows, rows), 0)
    second = lax.broadcasted_iota(jnp.int32, (rows, rows), 1)
    below = jnp.where(second < first, 1.0, 0.0).astype(jnp.bfloat16)
    return dot(below, match)


def attend_kernel(local, heads, lens_ref, q_mine, q_other, o_mine, o_other, cache, *refs):
    out_ref, keys, values, q_ref, score_ref, weight_ref, total_ref, k_sem, v_sem = refs[-9:]
    copies = []
    for i, head in enumerate(heads):
        at = pl.ds(head * HD, HD)
        copies.append(pltpu.make_async_copy(cache.at[local, :, at], keys.at[i], k_sem.at[i]))
        at = pl.ds((KVH + head) * HD, HD)
        copies.append(pltpu.make_async_copy(cache.at[local, :, at], values.at[i], v_sem.at[i]))
    for copy in copies:
        copy.start()
    number = lax.axis_index("fan") * 2 + local
    length = lens_ref[number]
    span = keys.shape[1]
    head_width = q_mine.shape[1] // KVH
    group = head_width // HD
    marks = 2 * KVH * HD
    prompts = jnp.concatenate([o_mine[:, marks:], o_other[:, marks:]], axis=0).astype(jnp.float32)
    chosen = prompts == number.astype(jnp.float32)
    rank = rank_rows(jnp.where(chosen, 1.0, 0.0).astype(jnp.bfloat16), LANES)
    lane = lax.broadcasted_iota(jnp.int32, (LANES, LANES), 1)
    here = chosen & (rank == lane.astype(jnp.float32))
    select = jnp.where(here, 1.0, 0.0).astype(jnp.bfloat16)

    def pick(mine, other, first, amount, rows):
        at = slice(first, first + amount)
        both = jnp.concatenate([mine[:, at], other[:, at]], axis=0)
        return dot(select[:, :rows], both, ((0,), (0,))).astype(jnp.bfloat16)

    factor = HD**-0.5 * LOG2E
    usable = lax.broadcasted_iota(jnp.int32, (1, span), 1) < length
    row = lax.broadcasted_iota(jnp.int32, (LANES, LANES), 0) % GROUP
    causal = ((row // STEPS == lane // STEPS) & (lane <= row))[:BAND]
    bands = group * GROUP // WIDE
    items = [(i, band) for i in range(len(heads)) for band in range(bands)]
    own = {}

    def products(step):
        i, band = items[step]
        head, slot = heads[i], step % 2
        if band == 0:
            queries = pick(q_mine, q_other, head * head_width, head_width, GROUP)
            for j in range(group):
                q_ref[i, j * GROUP : (j + 1) * GROUP] = queries[:, j * HD : (j + 1) * HD]
            own[i] = (
                pick(o_mine, o_other, head * HD, HD, LANES),
                pick(o_mine, o_other, (KVH + head) * HD, HD, LANES),
            )
            copies[2 * i].wait()
        queries = q_ref[i, band * WIDE : (band + 1) * WIDE]
        score_ref[slot, :, :span] = dot(queries, keys[i], ((1,), (1,)))
        score_ref[slot, :, span:] = dot(queries, own[i][0], ((1,), (1,)))

    products(0)
    for step, (i, band) in enumerate(items):
        slot = step % 2
        if step + 1 < len(items):
            products(step + 1)
        for base in range(0, WIDE, BAND):
            at = slice(base, base + BAND)
            scores = jnp.where(usable, score_ref[slot, at, :span], -1e30)
            mine = jnp.where(causal, score_ref[slot, at, span:], -1e30)
            highest = jnp.maximum(
                jnp.max(scores, axis=-1, keepdims=True), jnp.max(mine, axis=-1, keepdims=True)
            )
            raised = jnp.exp2((scores - highest) * factor)
            own_raised = jnp.exp2((mine - highest) * factor)
            total = jnp.sum(raised, axis=-1, keepdims=True) + jnp.sum(
                own_raised, axis=-1, keepdims=True
            )
            weight_ref[slot, at, :span] = raised.astype(jnp.bfloat16)
            weight_ref[slot, at, span:] = own_raised.astype(jnp.bfloat16)
            total_ref[slot, at] = jnp.broadcast_to(1.0 / total, (BAND, HD))
        if band == 0:
            copies[2 * i + 1].wait()
        mixed = dot(weight_ref[slot, :, :span], values[i])
        mixed = mixed + dot(weight_ref[slot, :, span:], own[i][1])
        mixed = (mixed * total_ref[slot]).astype(jnp.bfloat16)
        for j in range(WIDE // GROUP):
            first = i * head_width + (band * (WIDE // GROUP) + j) * HD
            out_ref[:, first : first + HD] = mixed[j * GROUP : (j + 1) * GROUP]


def attend(local, heads, lens, queries, own, cache, *after):
    rows, q_width = queries[0].shape
    span = cache.shape[1]
    head = q_width // KVH
    band = head // HD * GROUP
    some = len(heads)
    whole = pl.BlockSpec(memory_space=pltpu.VMEM)
    return pl.pallas_call(
        functools.partial(attend_kernel, local, heads),
        out_shape=jax.ShapeDtypeStruct((GROUP, some * head), jnp.bfloat16),
        in_specs=[pl.BlockSpec(memory_space=pltpu.SMEM)]
        + [whole] * 4
        + [pl.BlockSpec(memory_space=pltpu.HBM)]
        + [pl.BlockSpec(memory_space=pl.ANY)] * len(after),
        out_specs=whole,
        scratch_shapes=[
            pltpu.VMEM((some, span, HD), jnp.bfloat16),
            pltpu.VMEM((some, span, HD), jnp.bfloat16),
            pltpu.VMEM((some, band, HD), jnp.bfloat16),
            pltpu.VMEM((2, WIDE, span + LANES), jnp.float32),
            pltpu.VMEM((2, WIDE, span + LANES), jnp.bfloat16),
            pltpu.VMEM((2, WIDE, HD), jnp.float32),
            pltpu.SemaphoreType.DMA((some,)),
            pltpu.SemaphoreType.DMA((some,)),
        ],
        compiler_params=pltpu.CompilerParams(vmem_limit_bytes=ATTEND_VMEM * MIB),
        cost_estimate=SMALL,
        name="attend",
    )(lens, *queries, *own, cache, *after)


def place_kernel(halves, o_mine, *refs):
    out_ref = refs[-1]
    rows = o_mine.shape[0]
    lane = lax.broadcasted_iota(jnp.int32, (rows, LANES), 1)
    part = lane // GROUP
    side, local = part // 2, part % 2
    fan = lax.axis_index("fan")
    number = jnp.where(side == 0, fan, 1 - fan) * 2 + local
    prompts = o_mine[:, 2 * KVH * HD :].astype(jnp.float32)
    chosen = prompts == number.astype(jnp.float32)
    match = jnp.where(chosen, 1.0, 0.0).astype(jnp.bfloat16)
    rank = rank_rows(match, rows)
    ahead = GROUP - dot(jnp.ones((rows, rows), jnp.bfloat16), match)
    rank = rank + jnp.where(side == 1, ahead, 0.0)
    here = chosen & (rank == (lane % GROUP).astype(jnp.float32))
    place = jnp.where(here, 1.0, 0.0).astype(jnp.bfloat16)
    width = refs[0].shape[1]
    for half in range(halves):
        stacked = jnp.concatenate([ref[...] for ref in refs[4 * half : 4 * half + 4]], axis=0)
        result = dot(place, stacked).astype(jnp.bfloat16)
        at = slice(half * width, (half + 1) * width)
        out_ref[:, :, at] = result.reshape(rows // STEPS, STEPS, width)


def place_context(own, contexts, out_shape):
    whole = pl.BlockSpec(memory_space=pltpu.VMEM)
    return pl.pallas_call(
        functools.partial(place_kernel, len(contexts) // 4),
        out_shape=out_shape,
        in_specs=[whole] * (1 + len(contexts)),
        out_specs=whole,
        compiler_params=pltpu.CompilerParams(vmem_limit_bytes=12 * MIB),
        cost_estimate=SMALL,
        name="place_context",
    )(own, *contexts)


def expert_kernel(count, at_row, tokens, *refs):
    xs, (gate, up, down) = refs[:count], refs[count : count + 3]
    keep, send, other = refs[-8:-5]
    x, opened, raised, units, x_sem = refs[-5:]
    width, hidden = gate.shape
    copies = []
    for i in range(count):
        copies.append(
            pltpu.make_async_copy(
                xs[i].at[pl.ds(at_row, tokens)], x.at[pl.ds(i * tokens, tokens)], x_sem.at[i]
            )
        )
    for copy in copies:
        copy.start()
    for copy in copies:
        copy.wait()
    for i in range(width // DEEP):
        at = slice(i * DEEP, (i + 1) * DEEP)
        product = dot(x[:, at], gate[at])
        opened[...] = product if i == 0 else opened[...] + product
        product = dot(x[:, at], up[at])
        raised[...] = product if i == 0 else raised[...] + product
    through = opened[...]
    units[...] = (through * jax.nn.sigmoid(through) * raised[...]).astype(jnp.bfloat16)
    marks = x[:, width:].astype(jnp.float32)
    lane = lax.broadcasted_iota(jnp.int32, marks.shape, 1)
    mine = (lane % 16 == lax.axis_index("ep")) & (lane < 48)
    weight = jnp.sum(jnp.where(mine, marks, 0.0), axis=1, keepdims=True)
    half = count // 2 * tokens
    for i in range(width // DEEP):
        at = slice(i * DEEP, (i + 1) * DEEP)
        result = (dot(units[...], down[:, at]) * weight).astype(jnp.bfloat16)
        keep[:, at] = result[: half // 2]
        send[:, at] = result[half // 2 : half]
        other[:, at] = result[half:]


def expert_chunk(pieces, at_row, tokens, gate, up, down, *after):
    count = len(pieces)
    message = pieces[0].shape[1]
    width, hidden = gate.shape
    rows = count * tokens
    whole = pl.BlockSpec(memory_space=pltpu.VMEM)
    return pl.pallas_call(
        functools.partial(expert_kernel, count, at_row, tokens),
        out_shape=(
            jax.ShapeDtypeStruct((rows // 4, width), jnp.bfloat16),
            jax.ShapeDtypeStruct((rows // 4, width), jnp.bfloat16),
            jax.ShapeDtypeStruct((rows // 2, width), jnp.bfloat16),
        ),
        in_specs=[pl.BlockSpec(memory_space=pl.ANY)] * count
        + [whole] * 3
        + [pl.BlockSpec(memory_space=pl.ANY)] * len(after),
        out_specs=(whole, whole, whole),
        scratch_shapes=[
            pltpu.VMEM((rows, message), jnp.bfloat16),
            pltpu.VMEM((rows, hidden), jnp.float32),
            pltpu.VMEM((rows, hidden), jnp.float32),
            pltpu.VMEM((rows, hidden), jnp.bfloat16),
            pltpu.SemaphoreType.DMA((count,)),
        ],
        compiler_params=pltpu.CompilerParams(vmem_limit_bytes=EXPERT_VMEM * MIB),
        cost_estimate=SMALL,
        name="expert_chunk",
    )(*pieces, gate, up, down, *after)


def on_device(
    queries,
    new_kv,
    prompt_kv,
    prompt_lens,
    sample_prompt,
    hidden,
    norm_gain,
    route_ids,
    route_logits,
    w_gate,
    w_up,
    w_down,
):
    chips = lax.axis_size("ep")
    count, _, q_width = queries.shape
    rows = count * STEPS

    def swap(value, by_fan):
        pairs = [
            ((e * 2 + f), ((e ^ by_fan[f]) * 2 + f)) for e in range(chips) for f in range(2)
        ]
        return lax.ppermute(value, ("ep", "fan"), pairs)

    def near(value):
        return swap(value, (1, 2))

    def cross(value):
        return swap(value, (2, 1))

    def far(value, layer):
        return swap(value, (4 * layer, 4 * layer))

    def beside(value):
        return lax.ppermute(value, "fan", [(0, 1), (1, 0)])

    gate, up, down = w_gate[0], w_up[0], w_down[0]
    tokens = hidden.shape[0]
    sync = lax.optimization_barrier
    token = norm_message(hidden, norm_gain, route_ids, route_logits)
    token, queries, new_kv = sync((token, queries, new_kv))
    prompt_lens = touch(prompt_lens, token, prompt_kv, down)
    new_kv, prompt_lens = sync((new_kv, prompt_lens))
    marks = jnp.broadcast_to(sample_prompt.astype(jnp.bfloat16)[:, None, None], (count, STEPS, LANES))
    q_mine = queries.reshape(rows, q_width)
    own_mine = jnp.concatenate([new_kv, marks], axis=2).reshape(rows, -1)
    q_both = (q_mine, beside(q_mine))
    own_both = (own_mine, beside(own_mine))

    def attend_half(local, half, *after):
        heads = tuple(range(half * KVH // 2, (half + 1) * KVH // 2))
        return attend(local, heads, prompt_lens, q_both, own_both, prompt_kv, *after)

    def expert(pieces, at_row, *after):
        return expert_chunk(pieces, at_row, tokens, gate, up, down, *after)

    def with_fan(pieces):
        return pieces + [beside(piece) for piece in pieces]

    def sum_cores(result, back):
        send = result[1]
        half = send.shape[0]
        return (send.astype(jnp.float32) + back[half:].astype(jnp.float32)).astype(jnp.bfloat16)

    def sum_cross(result, back, turned):
        single = tokens

        def total(at):
            mine = result[0][at].astype(jnp.float32) + back[at].astype(jnp.float32)
            return mine + turned[at].astype(jnp.float32)

        return total(slice(0, single)), total(slice(single, 2 * single)).astype(jnp.bfloat16)

    def widen(value):
        return value.astype(jnp.float32)

    def narrow(value):
        return value.astype(jnp.bfloat16)

    level_2, level_1 = far(token, 2), far(token, 1)
    first_0, cross_0 = near(token), cross(token)
    third_0 = cross(first_0)
    level_2, level_1, prompt_lens = sync((level_2, level_1, prompt_lens))
    pair = stack(level_2, level_1)
    level_3 = far(level_2, 1)
    context_0a = attend_half(0, 0, pair, first_0, cross_0)
    context_0a, third_0, level_3 = sync((context_0a, third_0, level_3))
    pieces_0 = with_fan([token, first_0, cross_0, third_0])
    context_0b = attend_half(0, 1, context_0a)
    context_0b, first_p, cross_p, *pieces_0 = sync(
        (context_0b, near(pair), cross(pair), *pieces_0)
    )
    third_p = cross(first_p)
    first_3, cross_3 = near(level_3), cross(level_3)
    fans_p = [beside(value) for value in (pair, first_p, cross_p)]
    result_0 = expert(pieces_0, 0, context_0b, first_p)

    third_p, result_0, *fans_p = sync((third_p, result_0, *fans_p))
    back_0 = beside(result_0[2])
    pieces_p = [pair, first_p, cross_p, third_p, *fans_p, beside(third_p)]
    result_2 = expert(pieces_p, 0, result_0[0])

    first_3, cross_3, back_0, result_2 = sync((first_3, cross_3, back_0, result_2))
    back_2 = beside(result_2[2])
    third_3 = cross(first_3)
    fans_3 = [beside(value) for value in (level_3, first_3, cross_3)]
    there_0 = sum_cores(result_0, back_0)
    context_1a = attend_half(1, 0, first_3, cross_3, there_0)
    context_1a, third_3, back_2, *fans_3 = sync((context_1a, third_3, back_2, *fans_3))
    pieces_3 = [level_3, first_3, cross_3, third_3, *fans_3, beside(third_3)]
    there_2 = sum_cores(result_2, back_2)
    result_3 = expert(pieces_3, 0, there_2, context_1a)

    turned_0, turned_2, result_3 = sync((cross(there_0), cross(there_2), result_3))
    back_3 = beside(result_3[2])
    held_2, passed_2 = sum_cross(result_2, back_2, turned_2)
    there_3 = sum_cores(result_3, back_3)
    held_0, passed_0 = sum_cross(result_0, back_0, turned_0)
    result_1 = expert(pieces_p, tokens, there_3, passed_2, passed_0)

    contexts = [context_0a, context_0b, context_1a]
    sent = [beside(value) for value in contexts]
    turned_3, ended_2, result_1, *sent = sync((cross(there_3), near(passed_2), result_1, *sent))
    far_2 = far(narrow(held_2 + widen(ended_2)), 2)
    back_1 = beside(result_1[2])
    held_3, passed_3 = sum_cross(result_3, back_3, turned_3)
    there_1 = sum_cores(result_1, back_1)
    total_3 = narrow(held_3 + widen(near(passed_3)))
    far_3 = far(total_3, 3)
    held_1, passed_1 = sum_cross(result_1, back_1, cross(there_1))
    context_1b = attend_half(1, 1, total_3, passed_1)

    far_1 = far(narrow(held_1 + widen(near(passed_1))), 1)
    contexts, sent = contexts + [context_1b], sent + [beside(context_1b)]
    ordered = [contexts[0], contexts[2], sent[0], sent[2], contexts[1], contexts[3], sent[1], sent[3]]
    own_late, far_2 = sync((own_mine, far_2))
    context = place_context(own_late, ordered, jax.ShapeDtypeStruct(queries.shape, jnp.bfloat16))
    context, far_1, far_3 = sync((context, far_1, far_3))
    total = held_0 + widen(near(passed_0)) + widen(far_1)
    expert_out = narrow(total + widen(far_2) + widen(far_3))
    return (context, expert_out)


def solution(mesh):
    placed = (
        P(("parts", "ep", "fan"), None, None),
        P(("parts", "ep", "fan"), None, None),
        P(("parts", "ep", "fan"), None, None),
        P(("parts", "ep")),
        P(("parts", "ep", "fan")),
        P(("parts", "ep", "fan"), None),
        P(),
        P(("parts", "ep", "fan"), None),
        P(("parts", "ep", "fan"), None),
        P("ep", None, "fan"),
        P("ep", None, "fan"),
        P("ep", "fan", None),
    )
    return jax.shard_map(
        on_device,
        mesh=mesh,
        in_specs=placed,
        out_specs=(P(("parts", "ep", "fan"), None, None), P(("parts", "ep", "fan"), None)),
        check_vma=False,
    )
```

```python
import functools

import jax
import jax.numpy as jnp
from jax import lax
from jax.experimental import pallas as pl
from jax.experimental.pallas import tpu as pltpu
from jax.sharding import PartitionSpec as P

KVH = 4
HD = 128
STEPS = 2
SAMP = 16
TOP = 8
GROUP = SAMP * STEPS
LANES = 128
BAND = 64
WIDE = 256
DEEP = 1024
EXPERT_VMEM = 12
ATTEND_VMEM = 16
LOG2E = 1.4426950408889634
MIB = 1 << 20


def dot(a, b, contract=((1,), (0,))):
    return lax.dot_general(a, b, (contract, ((), ())), preferred_element_type=jnp.float32)


SMALL = pl.CostEstimate(flops=1 << 20, bytes_accessed=1 << 14, transcendentals=0)


def norm_kernel(hidden_ref, gain_ref, ids_ref, logits_ref, out_ref):
    rows, width = hidden_ref.shape
    hidden = hidden_ref[...].astype(jnp.float32)
    meansq = jnp.mean(hidden * hidden, axis=-1, keepdims=True)
    gain = gain_ref[...].astype(jnp.float32).reshape(1, width)
    out_ref[:, :width] = (hidden * lax.rsqrt(meansq + 1e-06) * gain).astype(jnp.bfloat16)
    logits = logits_ref[...]
    raised = jnp.exp(logits - jnp.max(logits, axis=0, keepdims=True))
    weights = raised / jnp.sum(raised, axis=0, keepdims=True)
    ids = ids_ref[...]
    number = lax.broadcasted_iota(jnp.int32, (LANES, rows), 0)
    total = jnp.zeros((LANES, rows), jnp.float32)
    for choice in range(TOP):
        picked = (number % 16) == ids[choice : choice + 1, :]
        total = total + jnp.where(picked, weights[choice : choice + 1, :], 0.0)
    high = total.astype(jnp.bfloat16).astype(jnp.float32)
    middle = (total - high).astype(jnp.bfloat16).astype(jnp.float32)
    low = total - high - middle
    piece = number // 16
    parts = jnp.where(
        piece == 0, high, jnp.where(piece == 1, middle, jnp.where(piece == 2, low, 0.0))
    ).astype(jnp.bfloat16)
    first = lax.broadcasted_iota(jnp.int32, (LANES, LANES), 0)
    second = lax.broadcasted_iota(jnp.int32, (LANES, LANES), 1)
    identity = jnp.where(first == second, 1.0, 0.0).astype(jnp.bfloat16)
    out_ref[:, width:] = dot(parts, identity, ((0,), (0,))).astype(jnp.bfloat16)


def norm_message(hidden, gain, ids, logits):
    rows, width = hidden.shape
    return pl.pallas_call(
        norm_kernel,
        out_shape=jax.ShapeDtypeStruct((rows, width + LANES), jnp.bfloat16),
        cost_estimate=SMALL,
        name="norm_message",
    )(hidden, gain, ids.T, logits.T)


def pack_kernel(queries, new_kv, prompt, q_out, own_out):
    rows = q_out.shape[0]
    count = rows // STEPS
    kv_width = new_kv.shape[2]
    q_out[...] = queries[...].reshape(rows, q_out.shape[1])
    own_out[:, :kv_width] = new_kv[...].reshape(rows, kv_width)
    row = lax.broadcasted_iota(jnp.int32, (rows, count), 0) // STEPS
    column = lax.broadcasted_iota(jnp.int32, (rows, count), 1)
    prompts = prompt[...].reshape(1, count).astype(jnp.float32)
    spread = jnp.where(row == column, prompts, 0.0).astype(jnp.bfloat16)
    ones = jnp.ones((count, LANES), jnp.bfloat16)
    own_out[:, kv_width:] = dot(spread, ones).astype(jnp.bfloat16)


def pack(queries, new_kv, prompt, *after):
    count, steps, q_width = queries.shape
    rows = count * steps
    whole = pl.BlockSpec(memory_space=pltpu.VMEM)

    def kernel(q, kv, p, *refs):
        pack_kernel(q, kv, p, *refs[-2:])

    return pl.pallas_call(
        kernel,
        out_shape=(
            jax.ShapeDtypeStruct((rows, q_width), queries.dtype),
            jax.ShapeDtypeStruct((rows, new_kv.shape[2] + LANES), queries.dtype),
        ),
        in_specs=[whole] * 3 + [pl.BlockSpec(memory_space=pl.ANY)] * len(after),
        out_specs=(whole, whole),
        compiler_params=pltpu.CompilerParams(vmem_limit_bytes=10 * MIB),
        cost_estimate=SMALL,
        name="pack",
    )(queries, new_kv, prompt, *after)


def stack_kernel(top, bottom, out):
    rows = top.shape[0]
    out[:rows] = top[...]
    out[rows:] = bottom[...]


def stack(top, bottom):
    rows, width = top.shape
    whole = pl.BlockSpec(memory_space=pltpu.VMEM)
    return pl.pallas_call(
        stack_kernel,
        out_shape=jax.ShapeDtypeStruct((2 * rows, width), top.dtype),
        in_specs=[whole, whole],
        out_specs=whole,
        compiler_params=pltpu.CompilerParams(vmem_limit_bytes=8 * MIB),
        cost_estimate=SMALL,
        name="stack",
    )(top, bottom)


def rank_rows(match, rows):
    first = lax.broadcasted_iota(jnp.int32, (rows, rows), 0)
    second = lax.broadcasted_iota(jnp.int32, (rows, rows), 1)
    below = jnp.where(second < first, 1.0, 0.0).astype(jnp.bfloat16)
    return dot(below, match)


def attend_kernel(local, heads, lens_ref, q_mine, q_other, o_mine, o_other, cache, *refs):
    out_ref, keys, values, q_ref, score_ref, weight_ref, total_ref, k_sem, v_sem = refs[-9:]
    copies = []
    for i, head in enumerate(heads):
        at = pl.ds(head * HD, HD)
        copies.append(pltpu.make_async_copy(cache.at[local, :, at], keys.at[i], k_sem.at[i]))
        at = pl.ds((KVH + head) * HD, HD)
        copies.append(pltpu.make_async_copy(cache.at[local, :, at], values.at[i], v_sem.at[i]))
    for copy in copies:
        copy.start()
    number = lax.axis_index("fan") * 2 + local
    length = lens_ref[number]
    span = keys.shape[1]
    head_width = q_mine.shape[1] // KVH
    group = head_width // HD
    marks = 2 * KVH * HD
    prompts = jnp.concatenate([o_mine[:, marks:], o_other[:, marks:]], axis=0).astype(jnp.float32)
    chosen = prompts == number.astype(jnp.float32)
    rank = rank_rows(jnp.where(chosen, 1.0, 0.0).astype(jnp.bfloat16), LANES)
    lane = lax.broadcasted_iota(jnp.int32, (LANES, LANES), 1)
    here = chosen & (rank == lane.astype(jnp.float32))
    select = jnp.where(here, 1.0, 0.0).astype(jnp.bfloat16)

    def pick(mine, other, first, amount, rows):
        at = slice(first, first + amount)
        both = jnp.concatenate([mine[:, at], other[:, at]], axis=0)
        return dot(select[:, :rows], both, ((0,), (0,))).astype(jnp.bfloat16)

    factor = HD**-0.5 * LOG2E
    usable = lax.broadcasted_iota(jnp.int32, (1, span), 1) < length
    row = lax.broadcasted_iota(jnp.int32, (LANES, LANES), 0) % GROUP
    causal = ((row // STEPS == lane // STEPS) & (lane <= row))[:BAND]
    bands = group * GROUP // WIDE
    items = [(i, band) for i in range(len(heads)) for band in range(bands)]
    own = {}

    def products(step):
        i, band = items[step]
        head, slot = heads[i], step % 2
        if band == 0:
            queries = pick(q_mine, q_other, head * head_width, head_width, GROUP)
            for j in range(group):
                q_ref[i, j * GROUP : (j + 1) * GROUP] = queries[:, j * HD : (j + 1) * HD]
            own[i] = (
                pick(o_mine, o_other, head * HD, HD, LANES),
                pick(o_mine, o_other, (KVH + head) * HD, HD, LANES),
            )
            copies[2 * i].wait()
        queries = q_ref[i, band * WIDE : (band + 1) * WIDE]
        score_ref[slot, :, :span] = dot(queries, keys[i], ((1,), (1,)))
        score_ref[slot, :, span:] = dot(queries, own[i][0], ((1,), (1,)))

    products(0)
    for step, (i, band) in enumerate(items):
        slot = step % 2
        if step + 1 < len(items):
            products(step + 1)
        for base in range(0, WIDE, BAND):
            at = slice(base, base + BAND)
            scores = jnp.where(usable, score_ref[slot, at, :span], -1e30)
            mine = jnp.where(causal, score_ref[slot, at, span:], -1e30)
            highest = jnp.maximum(
                jnp.max(scores, axis=-1, keepdims=True), jnp.max(mine, axis=-1, keepdims=True)
            )
            raised = jnp.exp2((scores - highest) * factor)
            own_raised = jnp.exp2((mine - highest) * factor)
            total = jnp.sum(raised, axis=-1, keepdims=True) + jnp.sum(
                own_raised, axis=-1, keepdims=True
            )
            weight_ref[slot, at, :span] = raised.astype(jnp.bfloat16)
            weight_ref[slot, at, span:] = own_raised.astype(jnp.bfloat16)
            total_ref[slot, at] = jnp.broadcast_to(1.0 / total, (BAND, HD))
        if band == 0:
            copies[2 * i + 1].wait()
        mixed = dot(weight_ref[slot, :, :span], values[i])
        mixed = mixed + dot(weight_ref[slot, :, span:], own[i][1])
        mixed = (mixed * total_ref[slot]).astype(jnp.bfloat16)
        for j in range(WIDE // GROUP):
            first = i * head_width + (band * (WIDE // GROUP) + j) * HD
            out_ref[:, first : first + HD] = mixed[j * GROUP : (j + 1) * GROUP]


def attend(local, heads, lens, queries, own, cache, *after):
    rows, q_width = queries[0].shape
    span = cache.shape[1]
    head = q_width // KVH
    band = head // HD * GROUP
    some = len(heads)
    whole = pl.BlockSpec(memory_space=pltpu.VMEM)
    return pl.pallas_call(
        functools.partial(attend_kernel, local, heads),
        out_shape=jax.ShapeDtypeStruct((GROUP, some * head), jnp.bfloat16),
        in_specs=[pl.BlockSpec(memory_space=pltpu.SMEM)]
        + [whole] * 4
        + [pl.BlockSpec(memory_space=pltpu.HBM)]
        + [pl.BlockSpec(memory_space=pl.ANY)] * len(after),
        out_specs=whole,
        scratch_shapes=[
            pltpu.VMEM((some, span, HD), jnp.bfloat16),
            pltpu.VMEM((some, span, HD), jnp.bfloat16),
            pltpu.VMEM((some, band, HD), jnp.bfloat16),
            pltpu.VMEM((2, WIDE, span + LANES), jnp.float32),
            pltpu.VMEM((2, WIDE, span + LANES), jnp.bfloat16),
            pltpu.VMEM((2, WIDE, HD), jnp.float32),
            pltpu.SemaphoreType.DMA((some,)),
            pltpu.SemaphoreType.DMA((some,)),
        ],
        compiler_params=pltpu.CompilerParams(vmem_limit_bytes=ATTEND_VMEM * MIB),
        cost_estimate=SMALL,
        name="attend",
    )(lens, *queries, *own, cache, *after)


def place_kernel(halves, o_mine, *refs):
    out_ref = refs[-1]
    rows = o_mine.shape[0]
    lane = lax.broadcasted_iota(jnp.int32, (rows, LANES), 1)
    part = lane // GROUP
    side, local = part // 2, part % 2
    fan = lax.axis_index("fan")
    number = jnp.where(side == 0, fan, 1 - fan) * 2 + local
    prompts = o_mine[:, 2 * KVH * HD :].astype(jnp.float32)
    chosen = prompts == number.astype(jnp.float32)
    match = jnp.where(chosen, 1.0, 0.0).astype(jnp.bfloat16)
    rank = rank_rows(match, rows)
    ahead = GROUP - dot(jnp.ones((rows, rows), jnp.bfloat16), match)
    rank = rank + jnp.where(side == 1, ahead, 0.0)
    here = chosen & (rank == (lane % GROUP).astype(jnp.float32))
    place = jnp.where(here, 1.0, 0.0).astype(jnp.bfloat16)
    width = refs[0].shape[1]
    for half in range(halves):
        stacked = jnp.concatenate([ref[...] for ref in refs[4 * half : 4 * half + 4]], axis=0)
        result = dot(place, stacked).astype(jnp.bfloat16)
        at = slice(half * width, (half + 1) * width)
        out_ref[:, :, at] = result.reshape(rows // STEPS, STEPS, width)


def place_context(own, contexts, out_shape):
    whole = pl.BlockSpec(memory_space=pltpu.VMEM)
    return pl.pallas_call(
        functools.partial(place_kernel, len(contexts) // 4),
        out_shape=out_shape,
        in_specs=[whole] * (1 + len(contexts)),
        out_specs=whole,
        compiler_params=pltpu.CompilerParams(vmem_limit_bytes=12 * MIB),
        cost_estimate=SMALL,
        name="place_context",
    )(own, *contexts)


def expert_kernel(count, at_row, tokens, *refs):
    xs, (gate, up, down) = refs[:count], refs[count : count + 3]
    keep, send, other = refs[-8:-5]
    x, opened, raised, units, x_sem = refs[-5:]
    width, hidden = gate.shape
    copies = []
    for i in range(count):
        copies.append(
            pltpu.make_async_copy(
                xs[i].at[pl.ds(at_row, tokens)], x.at[pl.ds(i * tokens, tokens)], x_sem.at[i]
            )
        )
    for copy in copies:
        copy.start()
    for copy in copies:
        copy.wait()
    for i in range(width // DEEP):
        at = slice(i * DEEP, (i + 1) * DEEP)
        product = dot(x[:, at], gate[at])
        opened[...] = product if i == 0 else opened[...] + product
        product = dot(x[:, at], up[at])
        raised[...] = product if i == 0 else raised[...] + product
    through = opened[...]
    units[...] = (through * jax.nn.sigmoid(through) * raised[...]).astype(jnp.bfloat16)
    marks = x[:, width:].astype(jnp.float32)
    lane = lax.broadcasted_iota(jnp.int32, marks.shape, 1)
    mine = (lane % 16 == lax.axis_index("ep")) & (lane < 48)
    weight = jnp.sum(jnp.where(mine, marks, 0.0), axis=1, keepdims=True)
    half = count // 2 * tokens
    for i in range(width // DEEP):
        at = slice(i * DEEP, (i + 1) * DEEP)
        result = (dot(units[...], down[:, at]) * weight).astype(jnp.bfloat16)
        keep[:, at] = result[: half // 2]
        send[:, at] = result[half // 2 : half]
        other[:, at] = result[half:]


def expert_chunk(pieces, at_row, tokens, gate, up, down, *after):
    count = len(pieces)
    message = pieces[0].shape[1]
    width, hidden = gate.shape
    rows = count * tokens
    whole = pl.BlockSpec(memory_space=pltpu.VMEM)
    return pl.pallas_call(
        functools.partial(expert_kernel, count, at_row, tokens),
        out_shape=(
            jax.ShapeDtypeStruct((rows // 4, width), jnp.bfloat16),
            jax.ShapeDtypeStruct((rows // 4, width), jnp.bfloat16),
            jax.ShapeDtypeStruct((rows // 2, width), jnp.bfloat16),
        ),
        in_specs=[pl.BlockSpec(memory_space=pl.ANY)] * count
        + [whole] * 3
        + [pl.BlockSpec(memory_space=pl.ANY)] * len(after),
        out_specs=(whole, whole, whole),
        scratch_shapes=[
            pltpu.VMEM((rows, message), jnp.bfloat16),
            pltpu.VMEM((rows, hidden), jnp.float32),
            pltpu.VMEM((rows, hidden), jnp.float32),
            pltpu.VMEM((rows, hidden), jnp.bfloat16),
            pltpu.SemaphoreType.DMA((count,)),
        ],
        compiler_params=pltpu.CompilerParams(vmem_limit_bytes=EXPERT_VMEM * MIB),
        cost_estimate=SMALL,
        name="expert_chunk",
    )(*pieces, gate, up, down, *after)


def on_device(
    queries,
    new_kv,
    prompt_kv,
    prompt_lens,
    sample_prompt,
    hidden,
    norm_gain,
    route_ids,
    route_logits,
    w_gate,
    w_up,
    w_down,
):
    chips = lax.axis_size("ep")
    count, _, q_width = queries.shape
    rows = count * STEPS

    def swap(value, by_fan):
        pairs = [
            ((e * 2 + f), ((e ^ by_fan[f]) * 2 + f)) for e in range(chips) for f in range(2)
        ]
        return lax.ppermute(value, ("ep", "fan"), pairs)

    def near(value):
        return swap(value, (1, 2))

    def cross(value):
        return swap(value, (2, 1))

    def far(value, layer):
        return swap(value, (4 * layer, 4 * layer))

    def beside(value):
        return lax.ppermute(value, "fan", [(0, 1), (1, 0)])

    gate, up, down = w_gate[0], w_up[0], w_down[0]
    tokens = hidden.shape[0]
    sync = lax.optimization_barrier
    token = norm_message(hidden, norm_gain, route_ids, route_logits)
    level_2, level_1 = far(token, 2), far(token, 1)
    first_0, cross_0 = near(token), cross(token)
    third_0 = cross(first_0)
    q_mine, own_mine = pack(queries, new_kv, sample_prompt, token)
    q_both = (q_mine, beside(q_mine))
    own_both = (own_mine, beside(own_mine))

    def attend_half(local, half, *after):
        heads = tuple(range(half * KVH // 2, (half + 1) * KVH // 2))
        return attend(local, heads, prompt_lens, q_both, own_both, prompt_kv, *after)

    def expert(pieces, at_row, *after):
        return expert_chunk(pieces, at_row, tokens, gate, up, down, *after)

    def with_fan(pieces):
        return pieces + [beside(piece) for piece in pieces]

    def sum_cores(result, back):
        send = result[1]
        half = send.shape[0]
        return (send.astype(jnp.float32) + back[half:].astype(jnp.float32)).astype(jnp.bfloat16)

    def sum_cross(result, back, turned):
        single = tokens

        def total(at):
            mine = result[0][at].astype(jnp.float32) + back[at].astype(jnp.float32)
            return mine + turned[at].astype(jnp.float32)

        return total(slice(0, single)), total(slice(single, 2 * single)).astype(jnp.bfloat16)

    def widen(value):
        return value.astype(jnp.float32)

    def narrow(value):
        return value.astype(jnp.bfloat16)

    context_0a = attend_half(0, 0)
    own_0 = token
    context_0a, level_2, level_1, own_0, first_0, third_0 = sync(
        (context_0a, level_2, level_1, own_0, first_0, third_0)
    )
    pair = stack(level_2, level_1)
    level_3 = far(level_2, 1)
    pieces_0 = with_fan([own_0, first_0, cross_0, third_0])
    context_0b = attend_half(0, 1, context_0a, pair)
    context_0b, level_3, *pieces_0 = sync((context_0b, level_3, *pieces_0))
    result_0 = expert(pieces_0, 0, context_0b)

    first_p, cross_p, result_0 = sync((near(pair), cross(pair), result_0))
    back_0 = beside(result_0[2])
    third_p = cross(first_p)
    first_3, cross_3 = near(level_3), cross(level_3)
    fans_p = [beside(value) for value in (pair, first_p, cross_p)]
    context_1a = attend_half(1, 0, first_p)
    context_1a, third_p, *fans_p = sync((context_1a, third_p, *fans_p))
    pieces_p = [pair, first_p, cross_p, third_p, *fans_p, beside(third_p)]
    result_2 = expert(pieces_p, 0, context_1a)

    sent = [beside(value) for value in (context_0a, context_0b)]
    first_3, cross_3, back_0, result_2, *sent = sync(
        (first_3, cross_3, back_0, result_2, *sent)
    )
    back_2 = beside(result_2[2])
    third_3 = cross(first_3)
    fans_3 = [beside(value) for value in (level_3, first_3, cross_3)]
    context_1b = attend_half(1, 1, first_3, cross_3)
    context_1b, third_3, back_2, *fans_3 = sync((context_1b, third_3, back_2, *fans_3))
    pieces_3 = [level_3, first_3, cross_3, third_3, *fans_3, beside(third_3)]
    there_2 = sum_cores(result_2, back_2)
    back_0, there_2 = sync((back_0, there_2))
    there_0 = sum_cores(result_0, back_0)
    result_3 = expert(pieces_3, 0, there_2, there_0)

    turned_2, result_3, sent_1a = sync((cross(there_2), result_3, beside(context_1a)))
    back_3 = beside(result_3[2])
    held_2, passed_2 = sum_cross(result_2, back_2, turned_2)
    there_3 = sum_cores(result_3, back_3)
    result_1 = expert(pieces_p, tokens, there_3, passed_2)

    contexts = [context_0a, context_0b, context_1a, context_1b]
    turned_0, turned_3, ended_2, result_1, sent_1b = sync(
        (cross(there_0), cross(there_3), near(passed_2), result_1, beside(context_1b))
    )
    sent = [*sent, sent_1a, sent_1b]
    far_2 = far(narrow(held_2 + widen(ended_2)), 2)
    back_1 = beside(result_1[2])
    held_3, passed_3 = sum_cross(result_3, back_3, turned_3)
    held_0, passed_0 = sum_cross(result_0, back_0, turned_0)
    there_1 = sum_cores(result_1, back_1)
    total_3 = narrow(held_3 + widen(near(passed_3)))
    far_3 = far(total_3, 3)
    ordered = [contexts[0], contexts[2], sent[0], sent[2], contexts[1], contexts[3], sent[1], sent[3]]
    own_late, _ = sync((own_mine, total_3))
    context = place_context(own_late, ordered, jax.ShapeDtypeStruct(queries.shape, jnp.bfloat16))
    turned_1, context, far_2 = sync((cross(there_1), context, far_2))
    held_1, passed_1 = sum_cross(result_1, back_1, turned_1)
    passed_1, passed_0 = sync((passed_1, passed_0))
    far_1 = far(narrow(held_1 + widen(near(passed_1))), 1)
    total = held_0 + widen(near(passed_0)) + widen(far_1)
    expert_out = narrow(total + widen(far_2) + widen(far_3))
    return (context, expert_out)


def solution(mesh):
    placed = (
        P(("parts", "ep", "fan"), None, None),
        P(("parts", "ep", "fan"), None, None),
        P(("parts", "ep", "fan"), None, None),
        P(("parts", "ep")),
        P(("parts", "ep", "fan")),
        P(("parts", "ep", "fan"), None),
        P(),
        P(("parts", "ep", "fan"), None),
        P(("parts", "ep", "fan"), None),
        P("ep", None, "fan"),
        P("ep", None, "fan"),
        P("ep", "fan", None),
    )
    return jax.shard_map(
        on_device,
        mesh=mesh,
        in_specs=placed,
        out_specs=(P(("parts", "ep", "fan"), None, None), P(("parts", "ep", "fan"), None)),
        check_vma=False,
    )
```

```python
import functools

import jax
import jax.numpy as jnp
from jax import lax
from jax.experimental import pallas as pl
from jax.experimental.pallas import tpu as pltpu
from jax.sharding import PartitionSpec as P

KVH = 4
HD = 128
STEPS = 2
SAMP = 16
TOP = 8
GROUP = SAMP * STEPS
LANES = 128
BAND = 64
WIDE = 256
DEEP = 1024
EXPERT_VMEM = 12
ATTEND_VMEM = 16
LOG2E = 1.4426950408889634
MIB = 1 << 20


def dot(a, b, contract=((1,), (0,))):
    return lax.dot_general(a, b, (contract, ((), ())), preferred_element_type=jnp.float32)


SMALL = pl.CostEstimate(flops=1 << 20, bytes_accessed=1 << 14, transcendentals=0)


def norm_kernel(hidden_ref, gain_ref, ids_ref, logits_ref, out_ref):
    rows, width = hidden_ref.shape
    hidden = hidden_ref[...].astype(jnp.float32)
    meansq = jnp.mean(hidden * hidden, axis=-1, keepdims=True)
    gain = gain_ref[...].astype(jnp.float32).reshape(1, width)
    out_ref[:, :width] = (hidden * lax.rsqrt(meansq + 1e-06) * gain).astype(jnp.bfloat16)
    logits = logits_ref[...]
    raised = jnp.exp(logits - jnp.max(logits, axis=0, keepdims=True))
    weights = raised / jnp.sum(raised, axis=0, keepdims=True)
    ids = ids_ref[...]
    number = lax.broadcasted_iota(jnp.int32, (LANES, rows), 0)
    total = jnp.zeros((LANES, rows), jnp.float32)
    for choice in range(TOP):
        picked = (number % 16) == ids[choice : choice + 1, :]
        total = total + jnp.where(picked, weights[choice : choice + 1, :], 0.0)
    high = total.astype(jnp.bfloat16).astype(jnp.float32)
    middle = (total - high).astype(jnp.bfloat16).astype(jnp.float32)
    low = total - high - middle
    piece = number // 16
    parts = jnp.where(
        piece == 0, high, jnp.where(piece == 1, middle, jnp.where(piece == 2, low, 0.0))
    ).astype(jnp.bfloat16)
    first = lax.broadcasted_iota(jnp.int32, (LANES, LANES), 0)
    second = lax.broadcasted_iota(jnp.int32, (LANES, LANES), 1)
    identity = jnp.where(first == second, 1.0, 0.0).astype(jnp.bfloat16)
    out_ref[:, width:] = dot(parts, identity, ((0,), (0,))).astype(jnp.bfloat16)


def norm_message(hidden, gain, ids, logits):
    rows, width = hidden.shape
    return pl.pallas_call(
        norm_kernel,
        out_shape=jax.ShapeDtypeStruct((rows, width + LANES), jnp.bfloat16),
        cost_estimate=SMALL,
        name="norm_message",
    )(hidden, gain, ids.T, logits.T)


def pack_kernel(queries, new_kv, prompt, q_out, own_out):
    rows = q_out.shape[0]
    count = rows // STEPS
    kv_width = new_kv.shape[2]
    q_out[...] = queries[...].reshape(rows, q_out.shape[1])
    own_out[:, :kv_width] = new_kv[...].reshape(rows, kv_width)
    row = lax.broadcasted_iota(jnp.int32, (rows, count), 0) // STEPS
    column = lax.broadcasted_iota(jnp.int32, (rows, count), 1)
    prompts = prompt[...].reshape(1, count).astype(jnp.float32)
    spread = jnp.where(row == column, prompts, 0.0).astype(jnp.bfloat16)
    ones = jnp.ones((count, LANES), jnp.bfloat16)
    own_out[:, kv_width:] = dot(spread, ones).astype(jnp.bfloat16)


def pack(queries, new_kv, prompt, *after):
    count, steps, q_width = queries.shape
    rows = count * steps
    whole = pl.BlockSpec(memory_space=pltpu.VMEM)

    def kernel(q, kv, p, *refs):
        pack_kernel(q, kv, p, *refs[-2:])

    return pl.pallas_call(
        kernel,
        out_shape=(
            jax.ShapeDtypeStruct((rows, q_width), queries.dtype),
            jax.ShapeDtypeStruct((rows, new_kv.shape[2] + LANES), queries.dtype),
        ),
        in_specs=[whole] * 3 + [pl.BlockSpec(memory_space=pl.ANY)] * len(after),
        out_specs=(whole, whole),
        compiler_params=pltpu.CompilerParams(vmem_limit_bytes=10 * MIB),
        cost_estimate=SMALL,
        name="pack",
    )(queries, new_kv, prompt, *after)


def stack_kernel(top, bottom, out):
    rows = top.shape[0]
    out[:rows] = top[...]
    out[rows:] = bottom[...]


def stack(top, bottom):
    rows, width = top.shape
    whole = pl.BlockSpec(memory_space=pltpu.VMEM)
    return pl.pallas_call(
        stack_kernel,
        out_shape=jax.ShapeDtypeStruct((2 * rows, width), top.dtype),
        in_specs=[whole, whole],
        out_specs=whole,
        compiler_params=pltpu.CompilerParams(vmem_limit_bytes=8 * MIB),
        cost_estimate=SMALL,
        name="stack",
    )(top, bottom)


def rank_rows(match, rows):
    first = lax.broadcasted_iota(jnp.int32, (rows, rows), 0)
    second = lax.broadcasted_iota(jnp.int32, (rows, rows), 1)
    below = jnp.where(second < first, 1.0, 0.0).astype(jnp.bfloat16)
    return dot(below, match)


def attend_kernel(local, heads, lens_ref, q_mine, q_other, o_mine, o_other, cache, *refs):
    out_ref, keys, values, q_ref, score_ref, weight_ref, total_ref, k_sem, v_sem = refs[-9:]
    copies = []
    for i, head in enumerate(heads):
        at = pl.ds(head * HD, HD)
        copies.append(pltpu.make_async_copy(cache.at[local, :, at], keys.at[i], k_sem.at[i]))
        at = pl.ds((KVH + head) * HD, HD)
        copies.append(pltpu.make_async_copy(cache.at[local, :, at], values.at[i], v_sem.at[i]))
    for copy in copies:
        copy.start()
    number = lax.axis_index("fan") * 2 + local
    length = lens_ref[number]
    span = keys.shape[1]
    head_width = q_mine.shape[1] // KVH
    group = head_width // HD
    marks = 2 * KVH * HD
    prompts = jnp.concatenate([o_mine[:, marks:], o_other[:, marks:]], axis=0).astype(jnp.float32)
    chosen = prompts == number.astype(jnp.float32)
    rank = rank_rows(jnp.where(chosen, 1.0, 0.0).astype(jnp.bfloat16), LANES)
    lane = lax.broadcasted_iota(jnp.int32, (LANES, LANES), 1)
    here = chosen & (rank == lane.astype(jnp.float32))
    select = jnp.where(here, 1.0, 0.0).astype(jnp.bfloat16)

    def pick(mine, other, first, amount, rows):
        at = slice(first, first + amount)
        both = jnp.concatenate([mine[:, at], other[:, at]], axis=0)
        return dot(select[:, :rows], both, ((0,), (0,))).astype(jnp.bfloat16)

    factor = HD**-0.5 * LOG2E
    usable = lax.broadcasted_iota(jnp.int32, (1, span), 1) < length
    row = lax.broadcasted_iota(jnp.int32, (LANES, LANES), 0) % GROUP
    causal = ((row // STEPS == lane // STEPS) & (lane <= row))[:BAND]
    bands = group * GROUP // WIDE
    items = [(i, band) for i in range(len(heads)) for band in range(bands)]
    own = {}

    def products(step):
        i, band = items[step]
        head, slot = heads[i], step % 2
        if band == 0:
            queries = pick(q_mine, q_other, head * head_width, head_width, GROUP)
            for j in range(group):
                q_ref[i, j * GROUP : (j + 1) * GROUP] = queries[:, j * HD : (j + 1) * HD]
            own[i] = (
                pick(o_mine, o_other, head * HD, HD, LANES),
                pick(o_mine, o_other, (KVH + head) * HD, HD, LANES),
            )
            copies[2 * i].wait()
        queries = q_ref[i, band * WIDE : (band + 1) * WIDE]
        score_ref[slot, :, :span] = dot(queries, keys[i], ((1,), (1,)))
        score_ref[slot, :, span:] = dot(queries, own[i][0], ((1,), (1,)))

    products(0)
    for step, (i, band) in enumerate(items):
        slot = step % 2
        if step + 1 < len(items):
            products(step + 1)
        for base in range(0, WIDE, BAND):
            at = slice(base, base + BAND)
            scores = jnp.where(usable, score_ref[slot, at, :span], -1e30)
            mine = jnp.where(causal, score_ref[slot, at, span:], -1e30)
            highest = jnp.maximum(
                jnp.max(scores, axis=-1, keepdims=True), jnp.max(mine, axis=-1, keepdims=True)
            )
            raised = jnp.exp2((scores - highest) * factor)
            own_raised = jnp.exp2((mine - highest) * factor)
            total = jnp.sum(raised, axis=-1, keepdims=True) + jnp.sum(
                own_raised, axis=-1, keepdims=True
            )
            weight_ref[slot, at, :span] = raised.astype(jnp.bfloat16)
            weight_ref[slot, at, span:] = own_raised.astype(jnp.bfloat16)
            total_ref[slot, at] = jnp.broadcast_to(1.0 / total, (BAND, HD))
        if band == 0:
            copies[2 * i + 1].wait()
        mixed = dot(weight_ref[slot, :, :span], values[i])
        mixed = mixed + dot(weight_ref[slot, :, span:], own[i][1])
        mixed = (mixed * total_ref[slot]).astype(jnp.bfloat16)
        for j in range(WIDE // GROUP):
            first = i * head_width + (band * (WIDE // GROUP) + j) * HD
            out_ref[:, first : first + HD] = mixed[j * GROUP : (j + 1) * GROUP]


def attend(local, heads, lens, queries, own, cache, *after):
    rows, q_width = queries[0].shape
    span = cache.shape[1]
    head = q_width // KVH
    band = head // HD * GROUP
    some = len(heads)
    whole = pl.BlockSpec(memory_space=pltpu.VMEM)
    return pl.pallas_call(
        functools.partial(attend_kernel, local, heads),
        out_shape=jax.ShapeDtypeStruct((GROUP, some * head), jnp.bfloat16),
        in_specs=[pl.BlockSpec(memory_space=pltpu.SMEM)]
        + [whole] * 4
        + [pl.BlockSpec(memory_space=pltpu.HBM)]
        + [pl.BlockSpec(memory_space=pl.ANY)] * len(after),
        out_specs=whole,
        scratch_shapes=[
            pltpu.VMEM((some, span, HD), jnp.bfloat16),
            pltpu.VMEM((some, span, HD), jnp.bfloat16),
            pltpu.VMEM((some, band, HD), jnp.bfloat16),
            pltpu.VMEM((2, WIDE, span + LANES), jnp.float32),
            pltpu.VMEM((2, WIDE, span + LANES), jnp.bfloat16),
            pltpu.VMEM((2, WIDE, HD), jnp.float32),
            pltpu.SemaphoreType.DMA((some,)),
            pltpu.SemaphoreType.DMA((some,)),
        ],
        compiler_params=pltpu.CompilerParams(vmem_limit_bytes=ATTEND_VMEM * MIB),
        cost_estimate=SMALL,
        name="attend",
    )(lens, *queries, *own, cache, *after)


def place_kernel(halves, o_mine, *refs):
    out_ref = refs[-1]
    rows = o_mine.shape[0]
    lane = lax.broadcasted_iota(jnp.int32, (rows, LANES), 1)
    part = lane // GROUP
    side, local = part // 2, part % 2
    fan = lax.axis_index("fan")
    number = jnp.where(side == 0, fan, 1 - fan) * 2 + local
    prompts = o_mine[:, 2 * KVH * HD :].astype(jnp.float32)
    chosen = prompts == number.astype(jnp.float32)
    match = jnp.where(chosen, 1.0, 0.0).astype(jnp.bfloat16)
    rank = rank_rows(match, rows)
    ahead = GROUP - dot(jnp.ones((rows, rows), jnp.bfloat16), match)
    rank = rank + jnp.where(side == 1, ahead, 0.0)
    here = chosen & (rank == (lane % GROUP).astype(jnp.float32))
    place = jnp.where(here, 1.0, 0.0).astype(jnp.bfloat16)
    width = refs[0].shape[1]
    for half in range(halves):
        stacked = jnp.concatenate([ref[...] for ref in refs[4 * half : 4 * half + 4]], axis=0)
        result = dot(place, stacked).astype(jnp.bfloat16)
        at = slice(half * width, (half + 1) * width)
        out_ref[:, :, at] = result.reshape(rows // STEPS, STEPS, width)


def place_context(own, contexts, out_shape):
    whole = pl.BlockSpec(memory_space=pltpu.VMEM)
    return pl.pallas_call(
        functools.partial(place_kernel, len(contexts) // 4),
        out_shape=out_shape,
        in_specs=[whole] * (1 + len(contexts)),
        out_specs=whole,
        compiler_params=pltpu.CompilerParams(vmem_limit_bytes=12 * MIB),
        cost_estimate=SMALL,
        name="place_context",
    )(own, *contexts)


def expert_kernel(count, at_row, tokens, *refs):
    xs, (gate, up, down) = refs[:count], refs[count : count + 3]
    keep, send, other = refs[-8:-5]
    x, opened, raised, units, x_sem = refs[-5:]
    width, hidden = gate.shape
    copies = []
    for i in range(count):
        copies.append(
            pltpu.make_async_copy(
                xs[i].at[pl.ds(at_row, tokens)], x.at[pl.ds(i * tokens, tokens)], x_sem.at[i]
            )
        )
    for copy in copies:
        copy.start()
    for copy in copies:
        copy.wait()
    for i in range(width // DEEP):
        at = slice(i * DEEP, (i + 1) * DEEP)
        product = dot(x[:, at], gate[at])
        opened[...] = product if i == 0 else opened[...] + product
        product = dot(x[:, at], up[at])
        raised[...] = product if i == 0 else raised[...] + product
    through = opened[...]
    units[...] = (through * jax.nn.sigmoid(through) * raised[...]).astype(jnp.bfloat16)
    marks = x[:, width:].astype(jnp.float32)
    lane = lax.broadcasted_iota(jnp.int32, marks.shape, 1)
    mine = (lane % 16 == lax.axis_index("ep")) & (lane < 48)
    weight = jnp.sum(jnp.where(mine, marks, 0.0), axis=1, keepdims=True)
    half = count // 2 * tokens
    for i in range(width // DEEP):
        at = slice(i * DEEP, (i + 1) * DEEP)
        result = (dot(units[...], down[:, at]) * weight).astype(jnp.bfloat16)
        keep[:, at] = result[: half // 2]
        send[:, at] = result[half // 2 : half]
        other[:, at] = result[half:]


def expert_chunk(pieces, at_row, tokens, gate, up, down, *after):
    count = len(pieces)
    message = pieces[0].shape[1]
    width, hidden = gate.shape
    rows = count * tokens
    whole = pl.BlockSpec(memory_space=pltpu.VMEM)
    return pl.pallas_call(
        functools.partial(expert_kernel, count, at_row, tokens),
        out_shape=(
            jax.ShapeDtypeStruct((rows // 4, width), jnp.bfloat16),
            jax.ShapeDtypeStruct((rows // 4, width), jnp.bfloat16),
            jax.ShapeDtypeStruct((rows // 2, width), jnp.bfloat16),
        ),
        in_specs=[pl.BlockSpec(memory_space=pl.ANY)] * count
        + [whole] * 3
        + [pl.BlockSpec(memory_space=pl.ANY)] * len(after),
        out_specs=(whole, whole, whole),
        scratch_shapes=[
            pltpu.VMEM((rows, message), jnp.bfloat16),
            pltpu.VMEM((rows, hidden), jnp.float32),
            pltpu.VMEM((rows, hidden), jnp.float32),
            pltpu.VMEM((rows, hidden), jnp.bfloat16),
            pltpu.SemaphoreType.DMA((count,)),
        ],
        compiler_params=pltpu.CompilerParams(vmem_limit_bytes=EXPERT_VMEM * MIB),
        cost_estimate=SMALL,
        name="expert_chunk",
    )(*pieces, gate, up, down, *after)


def on_device(
    queries,
    new_kv,
    prompt_kv,
    prompt_lens,
    sample_prompt,
    hidden,
    norm_gain,
    route_ids,
    route_logits,
    w_gate,
    w_up,
    w_down,
):
    chips = lax.axis_size("ep")
    count, _, q_width = queries.shape
    rows = count * STEPS

    def swap(value, by_fan):
        pairs = [
            ((e * 2 + f), ((e ^ by_fan[f]) * 2 + f)) for e in range(chips) for f in range(2)
        ]
        return lax.ppermute(value, ("ep", "fan"), pairs)

    def near(value):
        return swap(value, (1, 2))

    def cross(value):
        return swap(value, (2, 1))

    def far(value, layer):
        return swap(value, (4 * layer, 4 * layer))

    def beside(value):
        return lax.ppermute(value, "fan", [(0, 1), (1, 0)])

    gate, up, down = w_gate[0], w_up[0], w_down[0]
    tokens = hidden.shape[0]
    sync = lax.optimization_barrier
    token = norm_message(hidden, norm_gain, route_ids, route_logits)
    level_2, level_1 = far(token, 2), far(token, 1)
    first_0, cross_0 = near(token), cross(token)
    third_0 = cross(first_0)
    q_mine, own_mine = pack(queries, new_kv, sample_prompt, token)
    q_both = (q_mine, beside(q_mine))
    own_both = (own_mine, beside(own_mine))

    def attend_half(local, half, *after):
        heads = tuple(range(half * KVH // 2, (half + 1) * KVH // 2))
        return attend(local, heads, prompt_lens, q_both, own_both, prompt_kv, *after)

    def expert(pieces, at_row, *after):
        return expert_chunk(pieces, at_row, tokens, gate, up, down, *after)

    def with_fan(pieces):
        return pieces + [beside(piece) for piece in pieces]

    def sum_cores(result, back):
        send = result[1]
        half = send.shape[0]
        return (send.astype(jnp.float32) + back[half:].astype(jnp.float32)).astype(jnp.bfloat16)

    def sum_cross(result, back, turned):
        single = tokens

        def total(at):
            mine = result[0][at].astype(jnp.float32) + back[at].astype(jnp.float32)
            return mine + turned[at].astype(jnp.float32)

        return total(slice(0, single)), total(slice(single, 2 * single)).astype(jnp.bfloat16)

    def widen(value):
        return value.astype(jnp.float32)

    def narrow(value):
        return value.astype(jnp.bfloat16)

    context_0a = attend_half(0, 0)
    own_0 = token
    context_0a, level_2, level_1, own_0, first_0, third_0 = sync(
        (context_0a, level_2, level_1, own_0, first_0, third_0)
    )
    pair = stack(level_2, level_1)
    level_3 = far(level_2, 1)
    pieces_0 = with_fan([own_0, first_0, cross_0, third_0])
    context_0b = attend_half(0, 1, context_0a, pair)
    context_0b, level_3, first_p, cross_p, *pieces_0 = sync(
        (context_0b, level_3, near(pair), cross(pair), *pieces_0)
    )
    third_p = cross(first_p)
    first_3, cross_3 = near(level_3), cross(level_3)
    fans_p = [beside(value) for value in (pair, first_p, cross_p)]
    result_0 = expert(pieces_0, 0, context_0b, first_p)

    third_p, result_0, *fans_p = sync((third_p, result_0, *fans_p))
    back_0 = beside(result_0[2])
    pieces_p = [pair, first_p, cross_p, third_p, *fans_p, beside(third_p)]
    result_2 = expert(pieces_p, 0, result_0[0])

    first_3, cross_3, back_0, result_2, fan_3 = sync(
        (first_3, cross_3, back_0, result_2, beside(level_3))
    )
    back_2 = beside(result_2[2])
    third_3 = cross(first_3)
    fans_3 = [beside(value) for value in (first_3, cross_3)]
    there_0 = sum_cores(result_0, back_0)
    context_1a = attend_half(1, 0, first_3, cross_3, there_0)
    context_1a, third_3, back_2, *fans_3 = sync((context_1a, third_3, back_2, *fans_3))
    pieces_3 = [level_3, first_3, cross_3, third_3, fan_3, *fans_3, beside(third_3)]
    there_2 = sum_cores(result_2, back_2)
    result_3 = expert(pieces_3, 0, there_2)

    turned_0, turned_2, result_3 = sync((cross(there_0), cross(there_2), result_3))
    back_3 = beside(result_3[2])
    held_2, passed_2 = sum_cross(result_2, back_2, turned_2)
    there_3 = sum_cores(result_3, back_3)
    sent = [beside(value) for value in (context_0a, context_0b, context_1a)]
    held_0, passed_0 = sum_cross(result_0, back_0, turned_0)
    result_1 = expert(pieces_p, tokens, there_3, passed_2)

    turned_3, ended_2, result_1, *sent = sync((cross(there_3), near(passed_2), result_1, *sent))
    far_2 = far(narrow(held_2 + widen(ended_2)), 2)
    back_1 = beside(result_1[2])
    held_3, passed_3 = sum_cross(result_3, back_3, turned_3)
    passed_3, back_1 = sync((passed_3, back_1))
    there_1 = sum_cores(result_1, back_1)
    total_3 = narrow(held_3 + widen(near(passed_3)))
    far_3 = far(total_3, 3)
    turned_1, far_2 = sync((cross(there_1), far_2))
    held_1, passed_1 = sum_cross(result_1, back_1, turned_1)
    context_1b = attend_half(1, 1, total_3, passed_1)
    contexts = [context_0a, context_0b, context_1a, context_1b]
    sent = [*sent, beside(context_1b)]
    ordered = [contexts[0], contexts[2], sent[0], sent[2], contexts[1], contexts[3], sent[1], sent[3]]
    own_late, far_3 = sync((own_mine, far_3))
    context = place_context(own_late, ordered, jax.ShapeDtypeStruct(queries.shape, jnp.bfloat16))
    total_1, passed_0 = sync((narrow(held_1 + widen(near(passed_1))), passed_0))
    far_1 = far(total_1, 1)
    context, far_1 = sync((context, far_1))
    total = held_0 + widen(near(passed_0)) + widen(far_1)
    expert_out = narrow(total + widen(far_2) + widen(far_3))
    return (context, expert_out)


def solution(mesh):
    placed = (
        P(("parts", "ep", "fan"), None, None),
        P(("parts", "ep", "fan"), None, None),
        P(("parts", "ep", "fan"), None, None),
        P(("parts", "ep")),
        P(("parts", "ep", "fan")),
        P(("parts", "ep", "fan"), None),
        P(),
        P(("parts", "ep", "fan"), None),
        P(("parts", "ep", "fan"), None),
        P("ep", None, "fan"),
        P("ep", None, "fan"),
        P("ep", "fan", None),
    )
    return jax.shard_map(
        on_device,
        mesh=mesh,
        in_specs=placed,
        out_specs=(P(("parts", "ep", "fan"), None, None), P(("parts", "ep", "fan"), None)),
        check_vma=False,
    )
```

```python
import functools

import jax
import jax.numpy as jnp
from jax import lax
from jax.experimental import pallas as pl
from jax.experimental.pallas import tpu as pltpu
from jax.sharding import PartitionSpec as P

KVH = 4
HD = 128
STEPS = 2
SAMP = 16
TOP = 8
GROUP = SAMP * STEPS
LANES = 128
BAND = 64
WIDE = 256
DEEP = 1024
EXPERT_VMEM = 12
ATTEND_VMEM = 16
LOG2E = 1.4426950408889634
MIB = 1 << 20


def dot(a, b, contract=((1,), (0,))):
    return lax.dot_general(a, b, (contract, ((), ())), preferred_element_type=jnp.float32)


SMALL = pl.CostEstimate(flops=1 << 20, bytes_accessed=1 << 14, transcendentals=0)


def norm_kernel(hidden_ref, gain_ref, ids_ref, logits_ref, out_ref):
    rows, width = hidden_ref.shape
    hidden = hidden_ref[...].astype(jnp.float32)
    meansq = jnp.mean(hidden * hidden, axis=-1, keepdims=True)
    gain = gain_ref[...].astype(jnp.float32).reshape(1, width)
    out_ref[:, :width] = (hidden * lax.rsqrt(meansq + 1e-06) * gain).astype(jnp.bfloat16)
    logits = logits_ref[...]
    raised = jnp.exp(logits - jnp.max(logits, axis=0, keepdims=True))
    weights = raised / jnp.sum(raised, axis=0, keepdims=True)
    ids = ids_ref[...]
    number = lax.broadcasted_iota(jnp.int32, (LANES, rows), 0)
    total = jnp.zeros((LANES, rows), jnp.float32)
    for choice in range(TOP):
        picked = (number % 16) == ids[choice : choice + 1, :]
        total = total + jnp.where(picked, weights[choice : choice + 1, :], 0.0)
    high = total.astype(jnp.bfloat16).astype(jnp.float32)
    middle = (total - high).astype(jnp.bfloat16).astype(jnp.float32)
    low = total - high - middle
    piece = number // 16
    parts = jnp.where(
        piece == 0, high, jnp.where(piece == 1, middle, jnp.where(piece == 2, low, 0.0))
    ).astype(jnp.bfloat16)
    first = lax.broadcasted_iota(jnp.int32, (LANES, LANES), 0)
    second = lax.broadcasted_iota(jnp.int32, (LANES, LANES), 1)
    identity = jnp.where(first == second, 1.0, 0.0).astype(jnp.bfloat16)
    out_ref[:, width:] = dot(parts, identity, ((0,), (0,))).astype(jnp.bfloat16)


def norm_message(hidden, gain, ids, logits):
    rows, width = hidden.shape
    return pl.pallas_call(
        norm_kernel,
        out_shape=jax.ShapeDtypeStruct((rows, width + LANES), jnp.bfloat16),
        cost_estimate=SMALL,
        name="norm_message",
    )(hidden, gain, ids.T, logits.T)


def pack_kernel(queries, new_kv, prompt, q_out, own_out):
    rows = q_out.shape[0]
    count = rows // STEPS
    kv_width = new_kv.shape[2]
    q_out[...] = queries[...].reshape(rows, q_out.shape[1])
    own_out[:, :kv_width] = new_kv[...].reshape(rows, kv_width)
    row = lax.broadcasted_iota(jnp.int32, (rows, count), 0) // STEPS
    column = lax.broadcasted_iota(jnp.int32, (rows, count), 1)
    prompts = prompt[...].reshape(1, count).astype(jnp.float32)
    spread = jnp.where(row == column, prompts, 0.0).astype(jnp.bfloat16)
    ones = jnp.ones((count, LANES), jnp.bfloat16)
    own_out[:, kv_width:] = dot(spread, ones).astype(jnp.bfloat16)


def pack(queries, new_kv, prompt, *after):
    count, steps, q_width = queries.shape
    rows = count * steps
    whole = pl.BlockSpec(memory_space=pltpu.VMEM)

    def kernel(q, kv, p, *refs):
        pack_kernel(q, kv, p, *refs[-2:])

    return pl.pallas_call(
        kernel,
        out_shape=(
            jax.ShapeDtypeStruct((rows, q_width), queries.dtype),
            jax.ShapeDtypeStruct((rows, new_kv.shape[2] + LANES), queries.dtype),
        ),
        in_specs=[whole] * 3 + [pl.BlockSpec(memory_space=pl.ANY)] * len(after),
        out_specs=(whole, whole),
        compiler_params=pltpu.CompilerParams(vmem_limit_bytes=10 * MIB),
        cost_estimate=SMALL,
        name="pack",
    )(queries, new_kv, prompt, *after)


def stack_kernel(top, bottom, out):
    rows = top.shape[0]
    out[:rows] = top[...]
    out[rows:] = bottom[...]


def stack(top, bottom):
    rows, width = top.shape
    whole = pl.BlockSpec(memory_space=pltpu.VMEM)
    return pl.pallas_call(
        stack_kernel,
        out_shape=jax.ShapeDtypeStruct((2 * rows, width), top.dtype),
        in_specs=[whole, whole],
        out_specs=whole,
        compiler_params=pltpu.CompilerParams(vmem_limit_bytes=8 * MIB),
        cost_estimate=SMALL,
        name="stack",
    )(top, bottom)


def rank_rows(match, rows):
    first = lax.broadcasted_iota(jnp.int32, (rows, rows), 0)
    second = lax.broadcasted_iota(jnp.int32, (rows, rows), 1)
    below = jnp.where(second < first, 1.0, 0.0).astype(jnp.bfloat16)
    return dot(below, match)


def attend_kernel(local, heads, lens_ref, q_mine, q_other, o_mine, o_other, cache, *refs):
    out_ref, keys, values, q_ref, score_ref, weight_ref, total_ref, k_sem, v_sem = refs[-9:]
    copies = []
    for i, head in enumerate(heads):
        at = pl.ds(head * HD, HD)
        copies.append(pltpu.make_async_copy(cache.at[local, :, at], keys.at[i], k_sem.at[i]))
        at = pl.ds((KVH + head) * HD, HD)
        copies.append(pltpu.make_async_copy(cache.at[local, :, at], values.at[i], v_sem.at[i]))
    for copy in copies:
        copy.start()
    number = lax.axis_index("fan") * 2 + local
    length = lens_ref[number]
    span = keys.shape[1]
    head_width = q_mine.shape[1] // KVH
    group = head_width // HD
    marks = 2 * KVH * HD
    prompts = jnp.concatenate([o_mine[:, marks:], o_other[:, marks:]], axis=0).astype(jnp.float32)
    chosen = prompts == number.astype(jnp.float32)
    rank = rank_rows(jnp.where(chosen, 1.0, 0.0).astype(jnp.bfloat16), LANES)
    lane = lax.broadcasted_iota(jnp.int32, (LANES, LANES), 1)
    here = chosen & (rank == lane.astype(jnp.float32))
    select = jnp.where(here, 1.0, 0.0).astype(jnp.bfloat16)

    def pick(mine, other, first, amount, rows):
        at = slice(first, first + amount)
        both = jnp.concatenate([mine[:, at], other[:, at]], axis=0)
        return dot(select[:, :rows], both, ((0,), (0,))).astype(jnp.bfloat16)

    factor = HD**-0.5 * LOG2E
    usable = lax.broadcasted_iota(jnp.int32, (1, span), 1) < length
    row = lax.broadcasted_iota(jnp.int32, (LANES, LANES), 0) % GROUP
    causal = ((row // STEPS == lane // STEPS) & (lane <= row))[:BAND]
    bands = group * GROUP // WIDE
    items = [(i, band) for i in range(len(heads)) for band in range(bands)]
    own = {}

    def products(step):
        i, band = items[step]
        head, slot = heads[i], step % 2
        if band == 0:
            queries = pick(q_mine, q_other, head * head_width, head_width, GROUP)
            for j in range(group):
                q_ref[i, j * GROUP : (j + 1) * GROUP] = queries[:, j * HD : (j + 1) * HD]
            own[i] = (
                pick(o_mine, o_other, head * HD, HD, LANES),
                pick(o_mine, o_other, (KVH + head) * HD, HD, LANES),
            )
            copies[2 * i].wait()
        queries = q_ref[i, band * WIDE : (band + 1) * WIDE]
        score_ref[slot, :, :span] = dot(queries, keys[i], ((1,), (1,)))
        score_ref[slot, :, span:] = dot(queries, own[i][0], ((1,), (1,)))

    products(0)
    for step, (i, band) in enumerate(items):
        slot = step % 2
        if step + 1 < len(items):
            products(step + 1)
        for base in range(0, WIDE, BAND):
            at = slice(base, base + BAND)
            scores = jnp.where(usable, score_ref[slot, at, :span], -1e30)
            mine = jnp.where(causal, score_ref[slot, at, span:], -1e30)
            highest = jnp.maximum(
                jnp.max(scores, axis=-1, keepdims=True), jnp.max(mine, axis=-1, keepdims=True)
            )
            raised = jnp.exp2((scores - highest) * factor)
            own_raised = jnp.exp2((mine - highest) * factor)
            total = jnp.sum(raised, axis=-1, keepdims=True) + jnp.sum(
                own_raised, axis=-1, keepdims=True
            )
            weight_ref[slot, at, :span] = raised.astype(jnp.bfloat16)
            weight_ref[slot, at, span:] = own_raised.astype(jnp.bfloat16)
            total_ref[slot, at] = jnp.broadcast_to(1.0 / total, (BAND, HD))
        if band == 0:
            copies[2 * i + 1].wait()
        mixed = dot(weight_ref[slot, :, :span], values[i])
        mixed = mixed + dot(weight_ref[slot, :, span:], own[i][1])
        mixed = (mixed * total_ref[slot]).astype(jnp.bfloat16)
        for j in range(WIDE // GROUP):
            first = i * head_width + (band * (WIDE // GROUP) + j) * HD
            out_ref[:, first : first + HD] = mixed[j * GROUP : (j + 1) * GROUP]


def attend(local, heads, lens, queries, own, cache, *after):
    rows, q_width = queries[0].shape
    span = cache.shape[1]
    head = q_width // KVH
    band = head // HD * GROUP
    some = len(heads)
    whole = pl.BlockSpec(memory_space=pltpu.VMEM)
    return pl.pallas_call(
        functools.partial(attend_kernel, local, heads),
        out_shape=jax.ShapeDtypeStruct((GROUP, some * head), jnp.bfloat16),
        in_specs=[pl.BlockSpec(memory_space=pltpu.SMEM)]
        + [whole] * 4
        + [pl.BlockSpec(memory_space=pltpu.HBM)]
        + [pl.BlockSpec(memory_space=pl.ANY)] * len(after),
        out_specs=whole,
        scratch_shapes=[
            pltpu.VMEM((some, span, HD), jnp.bfloat16),
            pltpu.VMEM((some, span, HD), jnp.bfloat16),
            pltpu.VMEM((some, band, HD), jnp.bfloat16),
            pltpu.VMEM((2, WIDE, span + LANES), jnp.float32),
            pltpu.VMEM((2, WIDE, span + LANES), jnp.bfloat16),
            pltpu.VMEM((2, WIDE, HD), jnp.float32),
            pltpu.SemaphoreType.DMA((some,)),
            pltpu.SemaphoreType.DMA((some,)),
        ],
        compiler_params=pltpu.CompilerParams(vmem_limit_bytes=ATTEND_VMEM * MIB),
        cost_estimate=SMALL,
        name="attend",
    )(lens, *queries, *own, cache, *after)


def place_kernel(halves, o_mine, *refs):
    out_ref = refs[-1]
    rows = o_mine.shape[0]
    lane = lax.broadcasted_iota(jnp.int32, (rows, LANES), 1)
    part = lane // GROUP
    side, local = part // 2, part % 2
    fan = lax.axis_index("fan")
    number = jnp.where(side == 0, fan, 1 - fan) * 2 + local
    prompts = o_mine[:, 2 * KVH * HD :].astype(jnp.float32)
    chosen = prompts == number.astype(jnp.float32)
    match = jnp.where(chosen, 1.0, 0.0).astype(jnp.bfloat16)
    rank = rank_rows(match, rows)
    ahead = GROUP - dot(jnp.ones((rows, rows), jnp.bfloat16), match)
    rank = rank + jnp.where(side == 1, ahead, 0.0)
    here = chosen & (rank == (lane % GROUP).astype(jnp.float32))
    place = jnp.where(here, 1.0, 0.0).astype(jnp.bfloat16)
    width = refs[0].shape[1]
    for half in range(halves):
        stacked = jnp.concatenate([ref[...] for ref in refs[4 * half : 4 * half + 4]], axis=0)
        result = dot(place, stacked).astype(jnp.bfloat16)
        at = slice(half * width, (half + 1) * width)
        out_ref[:, :, at] = result.reshape(rows // STEPS, STEPS, width)


def place_context(own, contexts, out_shape):
    whole = pl.BlockSpec(memory_space=pltpu.VMEM)
    return pl.pallas_call(
        functools.partial(place_kernel, len(contexts) // 4),
        out_shape=out_shape,
        in_specs=[whole] * (1 + len(contexts)),
        out_specs=whole,
        compiler_params=pltpu.CompilerParams(vmem_limit_bytes=12 * MIB),
        cost_estimate=SMALL,
        name="place_context",
    )(own, *contexts)


def expert_kernel(count, at_row, tokens, *refs):
    xs, (gate, up, down) = refs[:count], refs[count : count + 3]
    keep, send, other = refs[-8:-5]
    x, opened, raised, units, x_sem = refs[-5:]
    width, hidden = gate.shape
    copies = []
    for i in range(count):
        copies.append(
            pltpu.make_async_copy(
                xs[i].at[pl.ds(at_row, tokens)], x.at[pl.ds(i * tokens, tokens)], x_sem.at[i]
            )
        )
    for copy in copies:
        copy.start()
    for copy in copies:
        copy.wait()
    for i in range(width // DEEP):
        at = slice(i * DEEP, (i + 1) * DEEP)
        product = dot(x[:, at], gate[at])
        opened[...] = product if i == 0 else opened[...] + product
        product = dot(x[:, at], up[at])
        raised[...] = product if i == 0 else raised[...] + product
    through = opened[...]
    units[...] = (through * jax.nn.sigmoid(through) * raised[...]).astype(jnp.bfloat16)
    marks = x[:, width:].astype(jnp.float32)
    lane = lax.broadcasted_iota(jnp.int32, marks.shape, 1)
    mine = (lane % 16 == lax.axis_index("ep")) & (lane < 48)
    weight = jnp.sum(jnp.where(mine, marks, 0.0), axis=1, keepdims=True)
    half = count // 2 * tokens
    for i in range(width // DEEP):
        at = slice(i * DEEP, (i + 1) * DEEP)
        result = (dot(units[...], down[:, at]) * weight).astype(jnp.bfloat16)
        keep[:, at] = result[: half // 2]
        send[:, at] = result[half // 2 : half]
        other[:, at] = result[half:]


def expert_chunk(pieces, at_row, tokens, gate, up, down, *after):
    count = len(pieces)
    message = pieces[0].shape[1]
    width, hidden = gate.shape
    rows = count * tokens
    whole = pl.BlockSpec(memory_space=pltpu.VMEM)
    return pl.pallas_call(
        functools.partial(expert_kernel, count, at_row, tokens),
        out_shape=(
            jax.ShapeDtypeStruct((rows // 4, width), jnp.bfloat16),
            jax.ShapeDtypeStruct((rows // 4, width), jnp.bfloat16),
            jax.ShapeDtypeStruct((rows // 2, width), jnp.bfloat16),
        ),
        in_specs=[pl.BlockSpec(memory_space=pl.ANY)] * count
        + [whole] * 3
        + [pl.BlockSpec(memory_space=pl.ANY)] * len(after),
        out_specs=(whole, whole, whole),
        scratch_shapes=[
            pltpu.VMEM((rows, message), jnp.bfloat16),
            pltpu.VMEM((rows, hidden), jnp.float32),
            pltpu.VMEM((rows, hidden), jnp.float32),
            pltpu.VMEM((rows, hidden), jnp.bfloat16),
            pltpu.SemaphoreType.DMA((count,)),
        ],
        compiler_params=pltpu.CompilerParams(vmem_limit_bytes=EXPERT_VMEM * MIB),
        cost_estimate=SMALL,
        name="expert_chunk",
    )(*pieces, gate, up, down, *after)


def on_device(
    queries,
    new_kv,
    prompt_kv,
    prompt_lens,
    sample_prompt,
    hidden,
    norm_gain,
    route_ids,
    route_logits,
    w_gate,
    w_up,
    w_down,
):
    chips = lax.axis_size("ep")
    count, _, q_width = queries.shape
    rows = count * STEPS

    def swap(value, by_fan):
        pairs = [
            ((e * 2 + f), ((e ^ by_fan[f]) * 2 + f)) for e in range(chips) for f in range(2)
        ]
        return lax.ppermute(value, ("ep", "fan"), pairs)

    def near(value):
        return swap(value, (1, 2))

    def cross(value):
        return swap(value, (2, 1))

    def far(value, layer):
        return swap(value, (4 * layer, 4 * layer))

    def beside(value):
        return lax.ppermute(value, "fan", [(0, 1), (1, 0)])

    gate, up, down = w_gate[0], w_up[0], w_down[0]
    tokens = hidden.shape[0]
    sync = lax.optimization_barrier
    token = norm_message(hidden, norm_gain, route_ids, route_logits)
    level_2, level_1 = far(token, 2), far(token, 1)
    first_0, cross_0 = near(token), cross(token)
    third_0 = cross(first_0)
    q_mine, own_mine = pack(queries, new_kv, sample_prompt, token)
    q_both = (q_mine, beside(q_mine))
    own_both = (own_mine, beside(own_mine))

    def attend_half(local, half, *after):
        heads = tuple(range(half * KVH // 2, (half + 1) * KVH // 2))
        return attend(local, heads, prompt_lens, q_both, own_both, prompt_kv, *after)

    def expert(pieces, at_row, *after):
        return expert_chunk(pieces, at_row, tokens, gate, up, down, *after)

    def with_fan(pieces):
        return pieces + [beside(piece) for piece in pieces]

    def sum_cores(result, back):
        send = result[1]
        half = send.shape[0]
        return (send.astype(jnp.float32) + back[half:].astype(jnp.float32)).astype(jnp.bfloat16)

    def sum_cross(result, back, turned):
        single = tokens

        def total(at):
            mine = result[0][at].astype(jnp.float32) + back[at].astype(jnp.float32)
            return mine + turned[at].astype(jnp.float32)

        return total(slice(0, single)), total(slice(single, 2 * single)).astype(jnp.bfloat16)

    def widen(value):
        return value.astype(jnp.float32)

    def narrow(value):
        return value.astype(jnp.bfloat16)

    context_0a = attend_half(0, 0)
    own_0 = token
    context_0a, level_2, level_1, own_0, first_0, third_0 = sync(
        (context_0a, level_2, level_1, own_0, first_0, third_0)
    )
    pair = stack(level_2, level_1)
    level_3 = far(level_2, 1)
    pieces_0 = with_fan([own_0, first_0, cross_0, third_0])
    context_0b = attend_half(0, 1, context_0a, pair)
    context_0b, level_3, first_p, cross_p, *pieces_0 = sync(
        (context_0b, level_3, near(pair), cross(pair), *pieces_0)
    )
    third_p = cross(first_p)
    first_3, cross_3 = near(level_3), cross(level_3)
    fans_p = [beside(value) for value in (pair, first_p, cross_p)]
    result_0 = expert(pieces_0, 0, context_0b, first_p)

    third_p, result_0, *fans_p = sync((third_p, result_0, *fans_p))
    back_0 = beside(result_0[2])
    pieces_p = [pair, first_p, cross_p, third_p, *fans_p, beside(third_p)]
    result_2 = expert(pieces_p, 0, result_0[0])

    first_3, cross_3, back_0, result_2, fan_3 = sync(
        (first_3, cross_3, back_0, result_2, beside(level_3))
    )
    back_2 = beside(result_2[2])
    third_3 = cross(first_3)
    fans_3 = [beside(value) for value in (first_3, cross_3)]
    there_0 = sum_cores(result_0, back_0)
    context_1a = attend_half(1, 0, first_3, cross_3, there_0)
    context_1a, third_3, back_2, *fans_3 = sync((context_1a, third_3, back_2, *fans_3))
    pieces_3 = [level_3, first_3, cross_3, third_3, fan_3, *fans_3, beside(third_3)]
    there_2 = sum_cores(result_2, back_2)
    result_3 = expert(pieces_3, 0, there_2)

    turned_0, turned_2, result_3 = sync((cross(there_0), cross(there_2), result_3))
    back_3 = beside(result_3[2])
    held_2, passed_2 = sum_cross(result_2, back_2, turned_2)
    there_3 = sum_cores(result_3, back_3)
    sent = [beside(value) for value in (context_0a, context_0b, context_1a)]
    held_0, passed_0 = sum_cross(result_0, back_0, turned_0)
    result_1 = expert(pieces_p, tokens, there_3, passed_2)

    turned_3, ended_2, result_1, *sent = sync((cross(there_3), near(passed_2), result_1, *sent))
    far_2 = far(narrow(held_2 + widen(ended_2)), 2)
    back_1 = beside(result_1[2])
    held_3, passed_3 = sum_cross(result_3, back_3, turned_3)
    passed_3, back_1 = sync((passed_3, back_1))
    there_1 = sum_cores(result_1, back_1)
    context_1b = attend_half(1, 1, there_1)
    ended_3, turned_1, context_1b = sync((near(passed_3), cross(there_1), context_1b))
    far_3 = far(narrow(held_3 + widen(ended_3)), 3)
    held_1, passed_1 = sum_cross(result_1, back_1, turned_1)
    contexts = [context_0a, context_0b, context_1a, context_1b]
    sent = [*sent, beside(context_1b)]
    ordered = [contexts[0], contexts[2], sent[0], sent[2], contexts[1], contexts[3], sent[1], sent[3]]
    own_late, far_2, far_3 = sync((own_mine, far_2, far_3))
    context = place_context(own_late, ordered, jax.ShapeDtypeStruct(queries.shape, jnp.bfloat16))
    total_1, passed_0 = sync((narrow(held_1 + widen(near(passed_1))), passed_0))
    far_1 = far(total_1, 1)
    context, far_1 = sync((context, far_1))
    total = held_0 + widen(near(passed_0)) + widen(far_1)
    expert_out = narrow(total + widen(far_2) + widen(far_3))
    return (context, expert_out)


def solution(mesh):
    placed = (
        P(("parts", "ep", "fan"), None, None),
        P(("parts", "ep", "fan"), None, None),
        P(("parts", "ep", "fan"), None, None),
        P(("parts", "ep")),
        P(("parts", "ep", "fan")),
        P(("parts", "ep", "fan"), None),
        P(),
        P(("parts", "ep", "fan"), None),
        P(("parts", "ep", "fan"), None),
        P("ep", None, "fan"),
        P("ep", None, "fan"),
        P("ep", "fan", None),
    )
    return jax.shard_map(
        on_device,
        mesh=mesh,
        in_specs=placed,
        out_specs=(P(("parts", "ep", "fan"), None, None), P(("parts", "ep", "fan"), None)),
        check_vma=False,
    )
```
